128 devices in a mesh: replica: 4 (over x), shard: 32 (over z, y, core).
Axes of the slice: x: 4, y: 4, z: 4, core: 2. Of those that a mesh axis runs over, the one named last changes fastest.
Arguments:
- grads: bfloat16 [4, 62914560], P('replica', 'shard'), may hold values from -3 to 3
- slot_table: int32 [32, 3], replicated, may hold values from -1 to 59, as said below
- left_factor: float32 [32, 3, 1024, 1024], P('shard', None, 'replica'), may hold values from -6 to 6
- right_factor: float32 [32, 3, 1024, 1024], P('shard', None, 'replica'), may hold values from -6 to 6
- left_root: bfloat16 [32, 3, 1024, 1024], P('shard', None, 'replica')
- right_root: bfloat16 [32, 3, 1024, 1024], P('shard', None, 'replica')
Outputs:
- new_left: float32 [32, 3, 1024, 1024], P('shard', None, 'replica')
- new_right: float32 [32, 3, 1024, 1024], P('shard', None, 'replica')
- update: bfloat16 [4, 62914560], P('replica', 'shard')
The draws below stay inside these ranges and needn't reach their ends.
Inputs may be any that keep to these rules, and one draw needn't show every extreme that they name: slot_table[h, k] is a block number or -1 (empty slot); every block stands in exactly one slot; slot k of shard index h holds only blocks of block row (h + k) mod 4; some shard index has all 3 slots filled.
All inputs are finite; a program needn't handle non-finite values.
Results may differ from the reference program's by a relative error of at most 0.018.
Values may be sent and summed in bfloat16 or wider, within the bound.
A program may use at most 128 MiB of HBM per device.

```python
import jax
import jax.numpy as jnp
from jax import lax

ROWS = 4096
COLS = 15360
BLK = 1024
NBR = 4
NBC = 15
SLOTS = 3
N_REPLICA = 4
N_SHARD = 32


def rooted(key, rise, spread):
    first, second = jax.random.split(key)
    noise = jax.random.normal(first, (N_SHARD, SLOTS, BLK, BLK), jnp.float32)
    position = jnp.arange(BLK, dtype=jnp.float32) / (BLK - 1)
    wobble = jax.random.uniform(second, (N_SHARD, SLOTS, BLK), jnp.float32, -spread, spread)
    scales = (1.0 + rise * position) * jnp.exp(wobble)
    identity = (jnp.arange(BLK)[:, None] == jnp.arange(BLK)[None, :]).astype(jnp.float32)
    values = scales[..., None] * (2.0 * identity + 1.5 * noise / jnp.sqrt(jnp.float32(BLK)))
    return values.astype(jnp.bfloat16)


def draw_left_root(key, part):
    key = jax.random.fold_in(key, 2)
    return rooted(key, 2.0, 0.3)


def draw_right_root(key, part):
    key = jax.random.fold_in(key, 3)
    return rooted(key, 0.0, 0.3)


def draw_slot_table(key, part):
    key = jax.random.fold_in(key, 1)
    key_first, key_order, key_cols = jax.random.split(key, 3)
    cell_count = N_SHARD * SLOTS
    holder = jnp.broadcast_to(jnp.arange(N_SHARD, dtype=jnp.int32)[:, None], (N_SHARD, SLOTS)).reshape(cell_count)
    slot_ids = jnp.broadcast_to(jnp.arange(SLOTS, dtype=jnp.int32)[None, :], (N_SHARD, SLOTS)).reshape(cell_count)
    block_rows = (holder + slot_ids) % NBR
    favored = jax.random.randint(key_first, (), 0, N_SHARD)
    order = jax.random.permutation(key_order, cell_count).astype(jnp.int32)
    score = jnp.where(holder == favored, slot_ids - SLOTS, order)
    same = block_rows[:, None] == block_rows[None, :]
    below = score[None, :] < score[:, None]
    rank = jnp.sum((same & below).astype(jnp.int32), axis=1)
    live = rank < NBC
    perms = jax.vmap(lambda sub: jax.random.permutation(sub, NBC))(jax.random.split(key_cols, NBR)).astype(jnp.int32)
    column = perms[block_rows, jnp.minimum(rank, NBC - 1)]
    table = jnp.where(live, block_rows * NBC + column, -1)
    return table.reshape(N_SHARD, SLOTS).astype(jnp.int32)


def block_levels(own_key, dims, cuts, least, high):
    factor_of, own = 1.0, jax.random.fold_in(own_key, 6)
    for dim, blocks in cuts:
        heights = jnp.exp(jax.random.uniform(jax.random.fold_in(own, dim), (blocks,), jnp.float32, least / len(cuts), high / len(cuts)))
        factor_of = factor_of * jnp.repeat(heights, dims[dim] // blocks).reshape([-1 if axis == dim else 1 for axis in range(len(dims))])
    return factor_of


def gaussian(own_key, extent, scale, reach, cuts=(), kind=jnp.bfloat16):
    level = block_levels(own_key, extent, cuts, -0.22, 0.18) if cuts else 1.0
    entries = jax.random.normal(own_key, extent, jnp.float32) * scale * level
    return jnp.minimum(jnp.maximum(entries, -reach), reach).astype(kind)


def setup_inputs(seed: int = 0) -> dict:
    arg_keys = jax.random.split(jax.random.key(seed), 7)
    grads = gaussian(arg_keys[0], (N_REPLICA, ROWS * COLS), 0.5, 3.0, ((0, 4), (1, 32)))
    slot_table = draw_slot_table(jax.random.fold_in(arg_keys[6], 71), 0)
    left_factor = gaussian(arg_keys[2], (N_SHARD, SLOTS, BLK, BLK), 1.0, 6.0, ((0, 32), (2, 4)), jnp.float32)
    right_factor = gaussian(arg_keys[3], (N_SHARD, SLOTS, BLK, BLK), 1.0, 6.0, ((0, 32), (2, 4)), jnp.float32)
    left_root = draw_left_root(jax.random.fold_in(arg_keys[6], 71), 0)
    right_root = draw_right_root(jax.random.fold_in(arg_keys[6], 71), 0)
    return dict(grads=grads, slot_table=slot_table, left_factor=left_factor, right_factor=right_factor, left_root=left_root, right_root=right_root)


EPSILON = 1e-06

def reference(grads, slot_table, left_factor, right_factor, left_root, right_root):
    total = lax.optimization_barrier(jnp.sum(grads.astype(jnp.float32), axis=0)).astype(jnp.bfloat16)
    row_count = ROWS // BLK
    col_count = COLS // BLK
    blocks = total.reshape(row_count, BLK, col_count, BLK).transpose(0, 2, 1, 3).reshape(row_count * col_count, BLK, BLK)
    cell_count = N_SHARD * SLOTS

    def one_cell(items):
        block_id, left, right, left_inv, right_inv = items

        def filled(unused):
            index = jnp.maximum(block_id, 0).astype(jnp.int32)
            gradient = lax.dynamic_index_in_dim(blocks, index, 0, keepdims=False)
            upper = left + jnp.dot(gradient, gradient.T, preferred_element_type=jnp.float32) / BLK
            lower = right + jnp.dot(gradient.T, gradient, preferred_element_type=jnp.float32) / BLK
            precond = jnp.dot(gradient, right_inv.T, preferred_element_type=jnp.float32).astype(jnp.bfloat16)
            direction = jnp.dot(left_inv, precond, preferred_element_type=jnp.float32)
            grad_power = jnp.mean(jnp.square(gradient.astype(jnp.float32)))
            direction_power = jnp.mean(jnp.square(direction))
            grafted = (direction * (jnp.sqrt(grad_power) / jnp.sqrt(direction_power + EPSILON))).astype(jnp.bfloat16)
            return (upper, lower, grafted)

        def vacant(unused):
            return (left, right, jnp.zeros((BLK, BLK), jnp.bfloat16))
        return lax.cond(block_id >= 0, filled, vacant, None)
    outs = lax.map(one_cell, (slot_table.reshape(cell_count), left_factor.reshape(cell_count, BLK, BLK), right_factor.reshape(cell_count, BLK, BLK), left_root.reshape(cell_count, BLK, BLK), right_root.reshape(cell_count, BLK, BLK)))
    new_left = outs[0].reshape(N_SHARD, SLOTS, BLK, BLK)
    new_right = outs[1].reshape(N_SHARD, SLOTS, BLK, BLK)
    wanted = jnp.arange(row_count * col_count, dtype=jnp.int32)
    match = slot_table.reshape(cell_count)[None, :] == wanted[:, None]
    cells = lax.optimization_barrier(jnp.sum(jnp.where(match, jnp.arange(cell_count, dtype=jnp.int32)[None, :], 0), axis=1)).astype(jnp.int32)
    placed = outs[2][cells]
    matrix = placed.reshape(row_count, col_count, BLK, BLK).transpose(0, 2, 1, 3).reshape(ROWS * COLS)
    update = jnp.broadcast_to(matrix[None, :], (N_REPLICA, ROWS * COLS))
    return (new_left, new_right, update)
```

```python
import functools

import jax
import jax.numpy as jnp
from jax import lax
from jax.experimental import pallas as pl
from jax.experimental.pallas import tpu as pltpu
from jax.sharding import PartitionSpec as P

ROWS = 4096
COLS = 15360
BLK = 1024
EPSILON = 1e-06

N_X = 4
N_S = 32
SLOTS = 3
NBR = 4
NBC = 15
SUBS = 8
CELLS = 24
QROWS = 32
CUT = 8
GROUPS = 4
MESH = pl.DeviceIdType.MESH
f32 = jnp.float32
bf16 = jnp.bfloat16
VMEM_BYTES = 56 * 1024 * 1024


def unpack(flat_ref, out_ref, mid):
    def step(col, carry):
        for row in range(16):
            at = pl.multiple_of(row * COLS + col * BLK, BLK)
            mid[row] = flat_ref[:, pl.ds(at, BLK)].astype(f32).reshape(8, 128)
        for lane in range(8):
            out_ref[0, col, :, lane * 128 : lane * 128 + 128] = mid[:, lane, :].astype(bf16)
        return carry

    lax.fori_loop(0, NBC, step, 0)


def pack(in_ref, out_ref, mid):
    def step(col, carry):
        for part in range(N_X):
            for half in range(2):
                mid[:, part * 2 + half, :] = in_ref[part, 0, col, :, half * 128 : half * 128 + 128].astype(f32)
        for row in range(16):
            at = pl.multiple_of(row * COLS + col * BLK, BLK)
            out_ref[:, pl.ds(at, BLK)] = mid[row].reshape(1, BLK).astype(bf16)
        return carry

    lax.fori_loop(0, NBC, step, 0)


def greet(me_x, me_s):
    barrier = pltpu.get_barrier_semaphore()

    def hail(step, carry):
        pl.semaphore_signal(
            barrier, inc=1, device_id=(me_x, lax.rem(me_s + step, N_S)), device_id_type=MESH
        )
        return carry

    lax.fori_loop(1, N_S, hail, 0)
    for far in range(1, N_X):
        pl.semaphore_signal(
            barrier, inc=1, device_id=(lax.rem(me_x + far, N_X), me_s), device_id_type=MESH
        )
    pl.semaphore_wait(barrier, N_S - 1 + N_X - 1)


def exchange(
    table, own, left, blocks, roots, fwd_a, fwd_b, part_a, part_b, from_p, from_m,
    sum_own, sum_down, sum_up, sum_over, outbox, send, recv, piece_send, piece_recv, local_sem,
):
    me_x, me_s = lax.axis_index("replica"), lax.axis_index("shard")
    row, sub = me_s // SUBS, lax.rem(me_s, SUBS)
    up, down, over = lax.rem(me_x + 1, N_X), lax.rem(me_x + 3, N_X), lax.rem(me_x + 2, N_X)

    def remote(src, dst, place, x):
        return pltpu.make_async_remote_copy(
            src_ref=src, dst_ref=dst, send_sem=send.at[place], recv_sem=recv.at[place],
            device_id=(x, me_s), device_id_type=MESH,
        )

    low, high = pl.ds(0, CUT), pl.ds(CUT, NBC - CUT)
    copies = [None] * 18
    copies[0] = remote(own.at[over, low], fwd_a, 0, down)
    copies[1] = remote(own.at[over, high], fwd_b, 1, up)
    copies[2] = remote(own.at[down, high], from_p.at[high], 2, down)
    copies[3] = remote(own.at[up, low], from_m.at[low], 3, up)
    copies[4] = remote(part_a, from_p.at[low], 4, down)
    copies[5] = remote(part_b, from_m.at[high], 5, up)
    copies[6] = remote(sum_own.at[low], sum_down.at[low], 6, up)
    copies[7] = remote(sum_own.at[high], sum_up.at[high], 7, down)
    copies[8] = remote(sum_own.at[high], sum_down.at[high], 8, up)
    copies[9] = remote(sum_own.at[low], sum_up.at[low], 9, down)
    copies[10] = remote(sum_down.at[low], sum_over.at[low], 10, up)
    copies[11] = remote(sum_up.at[high], sum_over.at[high], 11, down)
    upper, lower = pl.ds(0, 128), pl.ds(128, 128)
    copies[12] = remote(left.at[:, upper], roots.at[:, me_x, upper], 12, up)
    copies[13] = remote(left.at[:, lower], roots.at[:, me_x, lower], 13, down)
    copies[14] = remote(left.at[:, lower], roots.at[:, me_x, lower], 14, up)
    copies[15] = remote(left.at[:, upper], roots.at[:, me_x, upper], 15, down)
    copies[16] = remote(roots.at[:, down, upper], roots.at[:, down, upper], 16, up)
    copies[17] = remote(roots.at[:, up, lower], roots.at[:, up, lower], 17, down)
    keep = pltpu.make_async_copy(left, roots.at[:, me_x], local_sem)

    def piece(quarter, index):
        place = index % SLOTS
        holder = lax.rem(index // SLOTS + me_s // NBR, SUBS) * NBR + lax.rem(row + NBR - place, NBR)
        src = outbox.at[quarter, index]
        dst = blocks.at[place, sub, quarter]
        away = lambda: pltpu.make_async_remote_copy(
            src_ref=src, dst_ref=dst, send_sem=piece_send.at[quarter, index],
            recv_sem=piece_recv.at[place], device_id=(me_x, holder), device_id_type=MESH,
        )
        home = lambda: pltpu.make_async_copy(src, dst, piece_recv.at[place])
        return place, holder, away, home

    def spread(quarter, total):
        def step(index, carry):
            place, holder, away, home = piece(quarter, index)
            block = table[holder * SLOTS + place]
            outbox[quarter, index] = total[lax.rem(jnp.maximum(block, 0), NBC)]

            @pl.when(holder != me_s)
            def _():
                away().start()

            @pl.when(holder == me_s)
            def _():
                home().start()

            return carry

        lax.fori_loop(0, CELLS, step, 0)

    greet(me_x, me_s)
    for place in range(4):
        copies[place].start()
    keep.start()

    def add_a(col, carry):
        part_a[col] = (fwd_a[col].astype(f32) + own[down, col].astype(f32)).astype(bf16)
        return carry

    def add_b(col, carry):
        part_b[col] = (fwd_b[col].astype(f32) + own[up, CUT + col].astype(f32)).astype(bf16)
        return carry

    def add_all(col, carry):
        sum_own[col] = (
            own[me_x, col].astype(f32) + (from_p[col].astype(f32) + from_m[col].astype(f32))
        ).astype(bf16)
        return carry

    copies[0].wait_recv()
    lax.fori_loop(0, CUT, add_a, 0)
    copies[4].start()
    copies[1].wait_recv()
    lax.fori_loop(0, NBC - CUT, add_b, 0)
    copies[5].start()
    copies[3].wait_recv()
    copies[4].wait_recv()
    lax.fori_loop(0, CUT, add_all, 0)
    copies[6].start()
    copies[9].start()
    copies[2].wait_recv()
    copies[5].wait_recv()
    lax.fori_loop(CUT, NBC, add_all, 0)
    copies[7].start()
    copies[8].start()
    spread(me_x, sum_own)
    copies[6].wait_recv()
    copies[10].start()
    copies[7].wait_recv()
    copies[11].start()
    for place in range(12, 16):
        copies[place].start()
    copies[8].wait_recv()
    spread(down, sum_down)
    copies[9].wait_recv()
    spread(up, sum_up)
    copies[12].wait_recv()
    copies[16].start()
    copies[13].wait_recv()
    copies[17].start()
    copies[10].wait_recv()
    copies[11].wait_recv()
    spread(over, sum_over)
    for place in range(14, 18):
        copies[place].wait_recv()
    for place in range(18):
        copies[place].wait_send()
    keep.wait()

    def sent(index, carry):
        for quarter in range(N_X):
            place, holder, away, home = piece(quarter, index)

            @pl.when(holder != me_s)
            def _():
                away().wait_send()

        return carry

    lax.fori_loop(0, CELLS, sent, 0)
    for place in range(SLOTS):
        pltpu.make_async_copy(blocks.at[place], blocks.at[place], piece_recv.at[place]).wait()


def spread_back(
    table, direction, sums, powers, update, sum_box, scaled, inbox_0, inbox_1, inbox_2, inbox_3, own,
    sum_send, sum_recv, piece_send, piece_recv, send, recv, local_sem,
):
    me_x, me_s = lax.axis_index("replica"), lax.axis_index("shard")
    row, sub = me_s // SUBS, lax.rem(me_s, SUBS)
    up, down, over = lax.rem(me_x + 1, N_X), lax.rem(me_x + 3, N_X), lax.rem(me_x + 2, N_X)
    low, high = pl.ds(0, CUT), pl.ds(CUT, NBC - CUT)

    inbox = (inbox_0, inbox_1, inbox_2, inbox_3)

    greet(me_x, me_s)
    shares = []
    for index, x in enumerate((up, down, over)):
        shares.append(
            pltpu.make_async_remote_copy(
                src_ref=sums, dst_ref=sum_box.at[index], send_sem=sum_send.at[index],
                recv_sem=sum_recv.at[index], device_id=(x, me_s), device_id_type=MESH,
            )
        )
        shares[index].start()

    def piece(group, index):
        place, target_sub = index // SUBS, lax.rem(index + sub, SUBS)
        target = lax.rem(me_s + place, NBR) * SUBS + target_sub
        src = scaled.at[group, place, target_sub]
        dst = inbox[group].at[me_s // NBR * SLOTS + place]
        away = lambda: pltpu.make_async_remote_copy(
            src_ref=src, dst_ref=dst, send_sem=piece_send.at[group, index],
            recv_sem=piece_recv.at[group], device_id=(me_x, target), device_id_type=MESH,
        )
        home = lambda: pltpu.make_async_copy(src, dst, piece_recv.at[group])
        return place, target_sub, target, away, home

    for share in shares:
        share.wait_recv()
    all_sums = sums[...] + (sum_box[0] + sum_box[1] + sum_box[2])
    factor = jnp.sqrt(powers[...] / (BLK * BLK)) / jnp.sqrt(all_sums / (BLK * BLK) + EPSILON)

    for group in range(GROUPS):
        for place in range(SLOTS):
            scale = jnp.concatenate([factor[place : place + 1]] * 2, axis=1)

            def step(count, carry):
                target_sub = lax.rem(count + sub, SUBS)
                at = pl.multiple_of(target_sub * 128 + group * QROWS, QROWS)
                scaled[group, place, target_sub] = (
                    direction[place, pl.ds(at, QROWS)] * scale
                ).astype(bf16)
                _, _, target, away, home = piece(group, place * SUBS + count)

                @pl.when(target != me_s)
                def _():
                    away().start()

                @pl.when(target == me_s)
                def _():
                    home().start()

                return carry

            lax.fori_loop(0, SUBS, step, 0)

    def remote(src, dst, group, place, x):
        return pltpu.make_async_remote_copy(
            src_ref=src, dst_ref=dst, send_sem=send.at[group, place],
            recv_sem=recv.at[group, place], device_id=(x, me_s), device_id_type=MESH,
        )

    def links(group):
        mine = update.at[me_x, group]
        return [
            remote(own.at[group, low], mine.at[low], group, 0, up),
            remote(own.at[group, high], mine.at[high], group, 1, down),
            remote(own.at[group, high], mine.at[high], group, 2, up),
            remote(own.at[group, low], mine.at[low], group, 3, down),
            remote(update.at[down, group, low], update.at[down, group, low], group, 4, up),
            remote(update.at[up, group, high], update.at[up, group, high], group, 5, down),
            pltpu.make_async_copy(own.at[group], mine, local_sem.at[group]),
        ]

    every = [links(group) for group in range(GROUPS)]

    def find(col):
        wanted = row * NBC + col
        index = 0
        for cell in range(CELLS):
            place = cell % SLOTS
            holder = cell // SLOTS * NBR + lax.rem(row + NBR - place, NBR)
            index = jnp.where(table[holder * SLOTS + place] == wanted, cell, index)
        return index

    for group in range(GROUPS):
        pltpu.make_async_copy(inbox[group], inbox[group], piece_recv.at[group]).wait()

        def place_col(col, carry):
            own[group, col] = inbox[group][find(col)]
            return carry

        lax.fori_loop(0, NBC, place_col, 0)
        for place in (0, 1, 2, 3, 6):
            every[group][place].start()
        if group > 0:
            every[group - 1][0].wait_recv()
            every[group - 1][4].start()
            every[group - 1][1].wait_recv()
            every[group - 1][5].start()
    every[GROUPS - 1][0].wait_recv()
    every[GROUPS - 1][4].start()
    every[GROUPS - 1][1].wait_recv()
    every[GROUPS - 1][5].start()
    for group in range(GROUPS):
        for place in range(2, 6):
            every[group][place].wait_recv()
        for place in range(6):
            every[group][place].wait_send()
        every[group][6].wait()
    for share in shares:
        share.wait_send()

    def sent(index, carry):
        for group in range(GROUPS):
            _, _, target, away, home = piece(group, index)

            @pl.when(target != me_s)
            def _():
                away().wait_send()

        return carry

    lax.fori_loop(0, CELLS, sent, 0)


def contract_last(a, b):
    return lax.dot_general(a, b, (((1,), (1,)), ((), ())), preferred_element_type=f32)


def precondition(scalars, grad, left, right, left_fac, right_fac, new_left, new_right, direction, sums, powers):
    slot = pl.program_id(0)
    start = pl.multiple_of(scalars[0] * 256, 256)
    scale = jnp.where(scalars[1 + slot] >= 0, 1.0 / BLK, 0.0).astype(f32)
    whole = grad[0]
    rows = grad[0, pl.ds(start, 256), :]
    new_left[0] = left_fac[0] + contract_last(rows, whole) * scale
    cols = grad[0, :, pl.ds(start, 256)]
    new_right[0] = right_fac[0] + jnp.dot(cols.T, whole, preferred_element_type=f32) * scale
    precond = contract_last(whole, right[0]).astype(bf16)
    result = jnp.dot(left[0], precond, preferred_element_type=f32)
    direction[0] = result
    sums[0] = jnp.full((8, 128), jnp.sum(jnp.square(result)), f32)
    powers[0] = jnp.full((8, 128), jnp.sum(jnp.square(whole.astype(f32))), f32)


def on_device(grads, slot_table, left_factor, right_factor, left_root, right_root):
    me_x, me_s = lax.axis_index("replica"), lax.axis_index("shard")
    table = slot_table.reshape(N_S * SLOTS)
    vmem = pl.BlockSpec(memory_space=pltpu.VMEM)
    smem = pl.BlockSpec(memory_space=pltpu.SMEM)
    hbm = pl.BlockSpec(memory_space=pl.ANY)
    dma = pltpu.SemaphoreType.DMA

    own = pl.pallas_call(
        unpack,
        grid=(N_X, 2),
        in_specs=[pl.BlockSpec((1, 16 * COLS), lambda i, j: (0, i * 2 + j))],
        out_specs=pl.BlockSpec((1, NBC, 16, BLK), lambda i, j: (i, 0, j, 0)),
        out_shape=jax.ShapeDtypeStruct((N_X, NBC, QROWS, BLK), bf16),
        scratch_shapes=[pltpu.VMEM((16, 8, 128), f32)],
        compiler_params=pltpu.CompilerParams(vmem_limit_bytes=VMEM_BYTES),
        name="unpack",
    )(grads)

    blocks, roots = pl.pallas_call(
        exchange,
        in_specs=[smem, vmem, hbm],
        out_specs=[hbm, hbm],
        out_shape=[
            jax.ShapeDtypeStruct((SLOTS, SUBS, N_X, QROWS, BLK), bf16),
            jax.ShapeDtypeStruct((SLOTS, N_X, 256, BLK), bf16),
        ],
        scratch_shapes=[
            pltpu.VMEM((CUT, QROWS, BLK), bf16),
            pltpu.VMEM((NBC - CUT, QROWS, BLK), bf16),
            pltpu.VMEM((CUT, QROWS, BLK), bf16),
            pltpu.VMEM((NBC - CUT, QROWS, BLK), bf16),
            pltpu.VMEM((NBC, QROWS, BLK), bf16),
            pltpu.VMEM((NBC, QROWS, BLK), bf16),
            pltpu.VMEM((NBC, QROWS, BLK), bf16),
            pltpu.VMEM((NBC, QROWS, BLK), bf16),
            pltpu.VMEM((NBC, QROWS, BLK), bf16),
            pltpu.VMEM((NBC, QROWS, BLK), bf16),
            pltpu.VMEM((N_X, CELLS, QROWS, BLK), bf16),
            dma((18,)),
            dma((18,)),
            dma((N_X, CELLS)),
            dma((SLOTS,)),
            dma,
        ],
        compiler_params=pltpu.CompilerParams(
            collective_id=0, has_side_effects=True, vmem_limit_bytes=VMEM_BYTES
        ),
        name="exchange",
    )(table, own, left_root[0])

    mine = lax.dynamic_index_in_dim(slot_table, me_s, 0, keepdims=False)
    scalars = jnp.concatenate([me_x.astype(jnp.int32)[None], mine])

    def block(shape):
        return pl.BlockSpec((1,) + shape, lambda slot: (slot,) + (0,) * len(shape))

    new_left, new_right, direction, sums, powers = pl.pallas_call(
        precondition,
        grid=(SLOTS,),
        in_specs=[smem] + [block((BLK, BLK))] * 2 + [block((256, BLK))] * 3,
        out_specs=[block((256, BLK))] * 2 + [block((BLK, 256))] + [block((8, 128))] * 2,
        out_shape=[
            jax.ShapeDtypeStruct((SLOTS, 256, BLK), f32),
            jax.ShapeDtypeStruct((SLOTS, 256, BLK), f32),
            jax.ShapeDtypeStruct((SLOTS, BLK, 256), f32),
            jax.ShapeDtypeStruct((SLOTS, 8, 128), f32),
            jax.ShapeDtypeStruct((SLOTS, 8, 128), f32),
        ],
        compiler_params=pltpu.CompilerParams(vmem_limit_bytes=VMEM_BYTES),
        name="precondition",
    )(
        scalars,
        blocks.reshape(SLOTS, BLK, BLK),
        roots.reshape(SLOTS, BLK, BLK),
        right_root[0],
        left_factor[0],
        right_factor[0],
    )

    def lines(values):
        return jnp.pad(values[:, 0, :], ((0, 8 - SLOTS), (0, 0)))

    update = pl.pallas_call(
        spread_back,
        in_specs=[smem, vmem, vmem, vmem],
        out_specs=hbm,
        out_shape=jax.ShapeDtypeStruct((N_X, GROUPS, NBC, QROWS, 256), bf16),
        scratch_shapes=[
            pltpu.VMEM((3, 8, 128), f32),
            pltpu.VMEM((GROUPS, SLOTS, SUBS, QROWS, 256), bf16),
            pltpu.VMEM((CELLS, QROWS, 256), bf16),
            pltpu.VMEM((CELLS, QROWS, 256), bf16),
            pltpu.VMEM((CELLS, QROWS, 256), bf16),
            pltpu.VMEM((CELLS, QROWS, 256), bf16),
            pltpu.VMEM((GROUPS, NBC, QROWS, 256), bf16),
            dma((3,)),
            dma((3,)),
            dma((GROUPS, CELLS)),
            dma((GROUPS,)),
            dma((GROUPS, 6)),
            dma((GROUPS, 6)),
            dma((GROUPS,)),
        ],
        compiler_params=pltpu.CompilerParams(
            collective_id=1, has_side_effects=True, vmem_limit_bytes=VMEM_BYTES
        ),
        name="spread_back",
    )(table, direction, lines(sums), lines(powers))

    flat = pl.pallas_call(
        pack,
        grid=(GROUPS, 2),
        in_specs=[pl.BlockSpec((N_X, 1, NBC, 16, 256), lambda i, j: (0, i, 0, j, 0))],
        out_specs=pl.BlockSpec((1, 16 * COLS), lambda i, j: (0, i * 2 + j)),
        out_shape=jax.ShapeDtypeStruct((1, 128 * COLS), bf16),
        scratch_shapes=[pltpu.VMEM((16, 8, 128), f32)],
        compiler_params=pltpu.CompilerParams(vmem_limit_bytes=VMEM_BYTES),
        name="pack",
    )(update)
    return new_left[None], new_right[None], flat


def solution(mesh):
    rows = P("shard", None, "replica", None)
    flat = P("replica", "shard")
    return jax.shard_map(
        on_device,
        mesh=mesh,
        in_specs=(flat, P(), rows, rows, rows, rows),
        out_specs=(rows, rows, flat),
        check_vma=False,
    )
```

```python
import functools

import jax
import jax.numpy as jnp
from jax import lax
from jax.experimental import pallas as pl
from jax.experimental.pallas import tpu as pltpu
from jax.sharding import PartitionSpec as P

ROWS = 4096
COLS = 15360
BLK = 1024
EPSILON = 1e-06

N_X = 4
N_S = 32
SLOTS = 3
NBR = 4
NBC = 15
SUBS = 8
CELLS = 24
QROWS = 32
CUT = 8
GROUPS = 4
MESH = pl.DeviceIdType.MESH
f32 = jnp.float32
bf16 = jnp.bfloat16
VMEM_BYTES = 56 * 1024 * 1024


STEP = 9


def pack(in_ref, out_ref, mid):
    def step(col, carry):
        for part in range(N_X):
            for half in range(2):
                mid[pl.ds(part * 2 + half, 16, STEP), :] = in_ref[part, 0, col, :, half * 128 : half * 128 + 128].astype(f32)
        for row in range(16):
            at = pl.multiple_of(row * COLS + col * BLK, BLK)
            out_ref[:, pl.ds(at, BLK)] = mid[row * STEP : row * STEP + 8, :].reshape(1, BLK).astype(bf16)
        return carry

    lax.fori_loop(0, NBC, step, 0)


def hail(me_x, me_s):
    barrier = pltpu.get_barrier_semaphore()

    def one(step, carry):
        pl.semaphore_signal(
            barrier, inc=1, device_id=(me_x, lax.rem(me_s + step, N_S)), device_id_type=MESH
        )
        return carry

    lax.fori_loop(1, N_S, one, 0)
    for far in range(1, N_X):
        pl.semaphore_signal(
            barrier, inc=1, device_id=(lax.rem(me_x + far, N_X), me_s), device_id_type=MESH
        )


def admitted():
    pl.semaphore_wait(pltpu.get_barrier_semaphore(), N_S - 1 + N_X - 1)


def shampoo(
    table, grads, left, right, blocks_out, update,
    flat, mid, tiles, fwd_a, fwd_b, part_a, part_b, from_p, from_m,
    sum_own, sum_down, sum_up, sum_over, outbox, blocks, roots, right_box, precond, direction,
    sums, sum_box, scaled, inbox_0, inbox_1, inbox_2, inbox_3, own,
    flat_sem, right_sem, keep_sem, out_sem, send, recv, root_send, root_recv,
    piece_send, piece_recv, sum_send, sum_recv, back_send, back_recv, ring_send, ring_recv, local_sem,
):
    me_x, me_s = lax.axis_index("replica"), lax.axis_index("shard")
    row, sub = me_s // SUBS, lax.rem(me_s, SUBS)
    up, down, over = lax.rem(me_x + 1, N_X), lax.rem(me_x + 3, N_X), lax.rem(me_x + 2, N_X)
    low, high = pl.ds(0, CUT), pl.ds(CUT, NBC - CUT)
    inbox = (inbox_0, inbox_1, inbox_2, inbox_3)
    OVER, DOWN, UP, OWN = range(4)

    def cross(src, dst, send_sem, recv_sem, x):
        return pltpu.make_async_remote_copy(
            src_ref=src, dst_ref=dst, send_sem=send_sem, recv_sem=recv_sem,
            device_id=(x, me_s), device_id_type=MESH,
        )

    def remote(src, dst, place, x):
        return cross(src, dst, send.at[place], recv.at[place], x)

    copies = [
        remote(tiles.at[OVER, low], fwd_a, 0, down),
        remote(tiles.at[OVER, high], fwd_b, 1, up),
        remote(tiles.at[DOWN, high], from_p.at[high], 2, down),
        remote(tiles.at[UP, low], from_m.at[low], 3, up),
        remote(part_a, from_p.at[low], 4, down),
        remote(part_b, from_m.at[high], 5, up),
        remote(sum_own.at[low], sum_down.at[low], 6, up),
        remote(sum_own.at[high], sum_up.at[high], 7, down),
        remote(sum_own.at[high], sum_down.at[high], 8, up),
        remote(sum_own.at[low], sum_up.at[low], 9, down),
        remote(sum_down.at[low], sum_over.at[low], 10, up),
        remote(sum_up.at[high], sum_over.at[high], 11, down),
    ]
    upper, lower = pl.ds(0, 128), pl.ds(128, 128)

    def root(slot, place, src, dst, x):
        return cross(src, dst, root_send.at[slot, place], root_recv.at[slot, place], x)

    root_copies = []
    for slot in range(SLOTS):
        mine, there = left.at[slot], roots.at[slot, me_x]
        below, above = roots.at[slot, down, upper], roots.at[slot, up, lower]
        root_copies.append([
            root(slot, 0, mine.at[upper], there.at[upper], up),
            root(slot, 1, mine.at[lower], there.at[lower], down),
            root(slot, 2, mine.at[lower], there.at[lower], up),
            root(slot, 3, mine.at[upper], there.at[upper], down),
            root(slot, 4, below, below, up),
            root(slot, 5, above, above, down),
        ])
    keep = pltpu.make_async_copy(left, roots.at[:, me_x], keep_sem)
    fetch_right = pltpu.make_async_copy(right, right_box, right_sem)
    size = QROWS * COLS
    quarters = (over, down, up, me_x)
    loads = [
        pltpu.make_async_copy(
            grads.at[:, pl.ds(pl.multiple_of(quarters[part] * size, size), size)],
            flat.at[part % 2], flat_sem.at[part % 2],
        )
        for part in range(N_X)
    ]

    def unpack(part, first, last):
        def step(col, carry):
            for half in range(2):
                for line in range(16):
                    at = pl.multiple_of((half * 16 + line) * COLS + col * BLK, BLK)
                    mid[line * STEP : line * STEP + 8, :] = (
                        flat[part % 2, :, pl.ds(at, BLK)].astype(f32).reshape(8, 128)
                    )
                for lane in range(8):
                    tiles[part, col, half * 16 : half * 16 + 16, lane * 128 : lane * 128 + 128] = (
                        mid[pl.ds(lane, 16, STEP), :].astype(bf16)
                    )
            return carry

        lax.fori_loop(first, last, step, 0)

    def piece(quarter, index):
        place = index % SLOTS
        holder = lax.rem(index // SLOTS + me_s // NBR, SUBS) * NBR + lax.rem(row + NBR - place, NBR)
        src = outbox.at[quarter, index]
        dst = blocks.at[place, sub, quarter]
        away = lambda: pltpu.make_async_remote_copy(
            src_ref=src, dst_ref=dst, send_sem=piece_send.at[quarter, index],
            recv_sem=piece_recv.at[place], device_id=(me_x, holder), device_id_type=MESH,
        )
        home = lambda: pltpu.make_async_copy(src, dst, piece_recv.at[place])
        return place, holder, away, home

    def spread(quarter, total):
        def step(index, carry):
            place, holder, away, home = piece(quarter, index)
            block = table[holder * SLOTS + place]
            outbox[quarter, index] = total[lax.rem(jnp.maximum(block, 0), NBC)]

            @pl.when(holder != me_s)
            def _():
                away().start()

            @pl.when(holder == me_s)
            def _():
                home().start()

            return carry

        lax.fori_loop(0, CELLS, step, 0)

    def add_a(col, carry):
        part_a[col] = (fwd_a[col].astype(f32) + tiles[DOWN, col].astype(f32)).astype(bf16)
        return carry

    def add_b(col, carry):
        part_b[col] = (fwd_b[col].astype(f32) + tiles[UP, CUT + col].astype(f32)).astype(bf16)
        return carry

    def add_all(col, carry):
        sum_own[col] = (
            tiles[OWN, col].astype(f32) + (from_p[col].astype(f32) + from_m[col].astype(f32))
        ).astype(bf16)
        return carry

    loads[0].start()
    loads[1].start()
    fetch_right.start()
    hail(me_x, me_s)
    loads[0].wait()
    unpack(OVER, 0, CUT)
    admitted()
    keep.start()
    copies[0].start()
    unpack(OVER, CUT, NBC)
    copies[1].start()
    loads[2].start()
    loads[1].wait()
    unpack(DOWN, 0, NBC)
    copies[2].start()
    loads[3].start()
    loads[2].wait()
    unpack(UP, 0, NBC)
    copies[3].start()
    copies[0].wait_recv()
    lax.fori_loop(0, CUT, add_a, 0)
    copies[4].start()
    copies[1].wait_recv()
    lax.fori_loop(0, NBC - CUT, add_b, 0)
    copies[5].start()
    loads[3].wait()
    unpack(OWN, 0, NBC)
    copies[3].wait_recv()
    copies[4].wait_recv()
    lax.fori_loop(0, CUT, add_all, 0)
    copies[6].start()
    copies[9].start()
    copies[2].wait_recv()
    copies[5].wait_recv()
    lax.fori_loop(CUT, NBC, add_all, 0)
    copies[7].start()
    copies[8].start()
    for place in range(4):
        for slot in range(SLOTS):
            root_copies[slot][place].start()
    spread(me_x, sum_own)
    copies[6].wait_recv()
    copies[10].start()
    copies[7].wait_recv()
    copies[11].start()
    copies[8].wait_recv()
    spread(down, sum_down)
    copies[9].wait_recv()
    spread(up, sum_up)
    copies[10].wait_recv()
    copies[11].wait_recv()
    spread(over, sum_over)
    for slot in range(SLOTS):
        root_copies[slot][0].wait_recv()
        root_copies[slot][4].start()
        root_copies[slot][1].wait_recv()
        root_copies[slot][5].start()

    fetch_right.wait()
    powers = []
    for slot in range(SLOTS):
        pltpu.make_async_copy(blocks.at[slot], blocks.at[slot], piece_recv.at[slot]).wait()
        pltpu.make_async_copy(blocks.at[slot], blocks_out.at[slot], out_sem.at[slot]).start()
        grad = blocks[slot].reshape(BLK, BLK)
        precond[slot] = contract_last(grad, right_box[slot]).astype(bf16)
        powers.append(jnp.sum(jnp.square(grad.astype(f32))) / (BLK * BLK))

    keep.wait()
    shares = []
    for slot in range(SLOTS):
        for place in range(2, 6):
            root_copies[slot][place].wait_recv()
        result = jnp.dot(
            roots[slot].reshape(BLK, BLK), precond[slot], preferred_element_type=f32
        )
        direction[slot] = result
        sums[slot] = jnp.full((8, 128), jnp.sum(jnp.square(result)), f32)
        for index, x in enumerate((up, down, over)):
            share = cross(
                sums.at[slot], sum_box.at[slot, index],
                sum_send.at[slot, index], sum_recv.at[slot, index], x,
            )
            share.start()
            shares.append(share)
    for share in shares:
        share.wait_recv()
    scales = []
    for slot in range(SLOTS):
        total = sums[slot] + (sum_box[slot, 0] + sum_box[slot, 1] + sum_box[slot, 2])
        factor = jnp.sqrt(powers[slot]) / jnp.sqrt(total[0:1] / (BLK * BLK) + EPSILON)
        scales.append(jnp.concatenate([factor, factor], axis=1))

    def back(group, index):
        place, target_sub = index // SUBS, lax.rem(index + sub, SUBS)
        target = lax.rem(me_s + place, NBR) * SUBS + target_sub
        src = scaled.at[group, place, target_sub]
        dst = inbox[group].at[me_s // NBR * SLOTS + place]
        away = lambda: pltpu.make_async_remote_copy(
            src_ref=src, dst_ref=dst, send_sem=back_send.at[group, index],
            recv_sem=back_recv.at[group], device_id=(me_x, target), device_id_type=MESH,
        )
        home = lambda: pltpu.make_async_copy(src, dst, back_recv.at[group])
        return target_sub, target, away, home

    for group in range(GROUPS):
        for place in range(SLOTS):

            def step(count, carry):
                target_sub, target, away, home = back(group, place * SUBS + count)
                at = pl.multiple_of(target_sub * 128 + group * QROWS, QROWS)
                scaled[group, place, target_sub] = (
                    direction[place, pl.ds(at, QROWS)] * scales[place]
                ).astype(bf16)

                @pl.when(target != me_s)
                def _():
                    away().start()

                @pl.when(target == me_s)
                def _():
                    home().start()

                return carry

            lax.fori_loop(0, SUBS, step, 0)

    def ring(src, dst, group, place, x):
        return cross(src, dst, ring_send.at[group, place], ring_recv.at[group, place], x)

    def links(group):
        mine = update.at[me_x, group]
        below, above = update.at[down, group, low], update.at[up, group, high]
        return [
            ring(own.at[group, low], mine.at[low], group, 0, up),
            ring(own.at[group, high], mine.at[high], group, 1, down),
            ring(own.at[group, high], mine.at[high], group, 2, up),
            ring(own.at[group, low], mine.at[low], group, 3, down),
            ring(below, below, group, 4, up),
            ring(above, above, group, 5, down),
            pltpu.make_async_copy(own.at[group], mine, local_sem.at[group]),
        ]

    every = [links(group) for group in range(GROUPS)]

    def find(col):
        wanted = row * NBC + col
        index = 0
        for cell in range(CELLS):
            place = cell % SLOTS
            holder = cell // SLOTS * NBR + lax.rem(row + NBR - place, NBR)
            index = jnp.where(table[holder * SLOTS + place] == wanted, cell, index)
        return index

    def forward(group):
        every[group][0].wait_recv()
        every[group][4].start()
        every[group][1].wait_recv()
        every[group][5].start()

    for group in range(GROUPS):
        pltpu.make_async_copy(inbox[group], inbox[group], back_recv.at[group]).wait()

        def place_col(col, carry):
            own[group, col] = inbox[group][find(col)]
            return carry

        lax.fori_loop(0, NBC, place_col, 0)
        for place in (0, 1, 2, 3, 6):
            every[group][place].start()
        if group > 0:
            forward(group - 1)
    forward(GROUPS - 1)
    for group in range(GROUPS):
        for place in range(2, 6):
            every[group][place].wait_recv()
        for place in range(6):
            every[group][place].wait_send()
        every[group][6].wait()
    for share in shares:
        share.wait_send()
    for copy in copies:
        copy.wait_send()
    for slot in range(SLOTS):
        for copy in root_copies[slot]:
            copy.wait_send()
        pltpu.make_async_copy(blocks.at[slot], blocks_out.at[slot], out_sem.at[slot]).wait()

    def sent(index, carry):
        for quarter in range(N_X):
            place, holder, away, home = piece(quarter, index)

            @pl.when(holder != me_s)
            def _():
                away().wait_send()

        for group in range(GROUPS):
            target_sub, target, back_away, back_home = back(group, index)

            @pl.when(target != me_s)
            def _():
                back_away().wait_send()

        return carry

    lax.fori_loop(0, CELLS, sent, 0)


def contract_last(a, b):
    return lax.dot_general(a, b, (((1,), (1,)), ((), ())), preferred_element_type=f32)


def statistics(scalars, grad, left_fac, right_fac, new_left, new_right):
    slot = pl.program_id(0)
    start = pl.multiple_of(scalars[0] * 256, 256)
    scale = jnp.where(scalars[1 + slot] >= 0, 1.0 / BLK, 0.0).astype(f32)
    whole = grad[0]
    rows = grad[0, pl.ds(start, 256), :]
    new_left[0] = left_fac[0] + contract_last(rows, whole) * scale
    cols = grad[0, :, pl.ds(start, 256)]
    new_right[0] = right_fac[0] + jnp.dot(cols.T, whole, preferred_element_type=f32) * scale


def on_device(grads, slot_table, left_factor, right_factor, left_root, right_root):
    me_x, me_s = lax.axis_index("replica"), lax.axis_index("shard")
    table = slot_table.reshape(N_S * SLOTS)
    smem = pl.BlockSpec(memory_space=pltpu.SMEM)
    hbm = pl.BlockSpec(memory_space=pl.ANY)
    dma = pltpu.SemaphoreType.DMA
    vmem = pltpu.VMEM

    blocks, update = pl.pallas_call(
        shampoo,
        in_specs=[smem, hbm, hbm, hbm],
        out_specs=[hbm, hbm],
        out_shape=[
            jax.ShapeDtypeStruct((SLOTS, SUBS, N_X, QROWS, BLK), bf16),
            jax.ShapeDtypeStruct((N_X, GROUPS, NBC, QROWS, 256), bf16),
        ],
        scratch_shapes=[
            vmem((2, 1, QROWS * COLS), bf16),
            vmem((16 * STEP, 128), f32),
            vmem((N_X, NBC, QROWS, BLK), bf16),
            vmem((CUT, QROWS, BLK), bf16),
            vmem((NBC - CUT, QROWS, BLK), bf16),
            vmem((CUT, QROWS, BLK), bf16),
            vmem((NBC - CUT, QROWS, BLK), bf16),
        ]
        + [vmem((NBC, QROWS, BLK), bf16)] * 6
        + [
            vmem((N_X, CELLS, QROWS, BLK), bf16),
            vmem((SLOTS, SUBS, N_X, QROWS, BLK), bf16),
            vmem((SLOTS, N_X, 256, BLK), bf16),
            vmem((SLOTS, 256, BLK), bf16),
            vmem((SLOTS, BLK, 256), bf16),
            vmem((SLOTS, BLK, 256), f32),
            vmem((SLOTS, 8, 128), f32),
            vmem((SLOTS, 3, 8, 128), f32),
            vmem((GROUPS, SLOTS, SUBS, QROWS, 256), bf16),
        ]
        + [vmem((CELLS, QROWS, 256), bf16)] * GROUPS
        + [
            vmem((GROUPS, NBC, QROWS, 256), bf16),
            dma((2,)),
            dma,
            dma,
            dma((SLOTS,)),
            dma((12,)),
            dma((12,)),
            dma((SLOTS, 6)),
            dma((SLOTS, 6)),
            dma((N_X, CELLS)),
            dma((SLOTS,)),
            dma((SLOTS, 3)),
            dma((SLOTS, 3)),
            dma((GROUPS, CELLS)),
            dma((GROUPS,)),
            dma((GROUPS, 6)),
            dma((GROUPS, 6)),
            dma((GROUPS,)),
        ],
        compiler_params=pltpu.CompilerParams(
            collective_id=0, has_side_effects=True, vmem_limit_bytes=VMEM_BYTES
        ),
        name="shampoo",
    )(table, grads, left_root[0], right_root[0])

    mine = lax.dynamic_index_in_dim(slot_table, me_s, 0, keepdims=False)
    scalars = jnp.concatenate([me_x.astype(jnp.int32)[None], mine])

    def block(shape):
        return pl.BlockSpec((1,) + shape, lambda slot: (slot,) + (0,) * len(shape))

    new_left, new_right = pl.pallas_call(
        statistics,
        grid=(SLOTS,),
        in_specs=[smem, block((BLK, BLK))] + [block((256, BLK))] * 2,
        out_specs=[block((256, BLK))] * 2,
        out_shape=[jax.ShapeDtypeStruct((SLOTS, 256, BLK), f32)] * 2,
        compiler_params=pltpu.CompilerParams(vmem_limit_bytes=VMEM_BYTES),
        name="statistics",
    )(scalars, blocks.reshape(SLOTS, BLK, BLK), left_factor[0], right_factor[0])

    flat = pl.pallas_call(
        pack,
        grid=(GROUPS, 2),
        in_specs=[pl.BlockSpec((N_X, 1, NBC, 16, 256), lambda i, j: (0, i, 0, j, 0))],
        out_specs=pl.BlockSpec((1, 16 * COLS), lambda i, j: (0, i * 2 + j)),
        out_shape=jax.ShapeDtypeStruct((1, 128 * COLS), bf16),
        scratch_shapes=[pltpu.VMEM((16 * STEP, 128), f32)],
        compiler_params=pltpu.CompilerParams(vmem_limit_bytes=VMEM_BYTES),
        name="pack",
    )(update)
    return new_left[None], new_right[None], flat


def solution(mesh):
    rows = P("shard", None, "replica", None)
    flat = P("replica", "shard")
    return jax.shard_map(
        on_device,
        mesh=mesh,
        in_specs=(flat, P(), rows, rows, rows, rows),
        out_specs=(rows, rows, flat),
        check_vma=False,
    )
```

```python
import functools

import jax
import jax.numpy as jnp
from jax import lax
from jax.experimental import pallas as pl
from jax.experimental.pallas import tpu as pltpu
from jax.sharding import PartitionSpec as P

ROWS = 4096
COLS = 15360
BLK = 1024
EPSILON = 1e-06

N_X = 4
N_S = 32
SLOTS = 3
NBR = 4
NBC = 15
SUBS = 8
CELLS = 24
QROWS = 32
CUT = 8
GROUPS = 4
MESH = pl.DeviceIdType.MESH
f32 = jnp.float32
bf16 = jnp.bfloat16
VMEM_BYTES = 58 * 1024 * 1024


STEP = 9


def pack(in_ref, out_ref, mid):
    def step(col, carry):
        for part in range(N_X):
            for half in range(2):
                mid[pl.ds(part * 2 + half, 16, STEP), :] = in_ref[part, 0, col, :, half * 128 : half * 128 + 128].astype(f32)
        for row in range(16):
            at = pl.multiple_of(row * COLS + col * BLK, BLK)
            out_ref[:, pl.ds(at, BLK)] = mid[row * STEP : row * STEP + 8, :].reshape(1, BLK).astype(bf16)
        return carry

    lax.fori_loop(0, NBC, step, 0)


def hail(me_x, me_s):
    barrier = pltpu.get_barrier_semaphore()

    def one(step, carry):
        pl.semaphore_signal(
            barrier, inc=1, device_id=(me_x, lax.rem(me_s + step, N_S)), device_id_type=MESH
        )
        return carry

    lax.fori_loop(1, N_S, one, 0)
    for far in range(1, N_X):
        pl.semaphore_signal(
            barrier, inc=1, device_id=(lax.rem(me_x + far, N_X), me_s), device_id_type=MESH
        )


def admitted():
    pl.semaphore_wait(pltpu.get_barrier_semaphore(), N_S - 1 + N_X - 1)


def shampoo(
    table, grads, left, right, left_fac, right_fac, new_left, new_right, update,
    flat, mid, tiles, fwd_a, fwd_b, part_a, part_b, from_p, from_m,
    sum_own, sum_down, sum_up, sum_over, outbox, blocks, roots, right_box, precond, direction,
    sums, sum_box, scaled, inbox_early, inbox_0, inbox_1, inbox_2, inbox_3, own, left_box, right_fac_box, places,
    flat_sem, right_sem, keep_sem, out_sem, send, recv, root_send, root_recv,
    fac_sem, piece_send, piece_recv, sum_send, sum_recv, back_send, back_recv, early_recv, ring_send, ring_recv, local_sem,
):
    me_x, me_s = lax.axis_index("replica"), lax.axis_index("shard")
    row, sub = me_s // SUBS, lax.rem(me_s, SUBS)
    up, down, over = lax.rem(me_x + 1, N_X), lax.rem(me_x + 3, N_X), lax.rem(me_x + 2, N_X)
    low, high = pl.ds(0, CUT), pl.ds(CUT, NBC - CUT)
    inbox = (inbox_0, inbox_1, inbox_2, inbox_3)
    OVER, DOWN, UP, OWN = range(4)

    def cross(src, dst, send_sem, recv_sem, x):
        return pltpu.make_async_remote_copy(
            src_ref=src, dst_ref=dst, send_sem=send_sem, recv_sem=recv_sem,
            device_id=(x, me_s), device_id_type=MESH,
        )

    def remote(src, dst, place, x):
        return cross(src, dst, send.at[place], recv.at[place], x)

    copies = [
        remote(tiles.at[OVER, low], fwd_a, 0, down),
        remote(tiles.at[OVER, high], fwd_b, 1, up),
        remote(tiles.at[DOWN, high], from_p.at[high], 2, down),
        remote(tiles.at[UP, low], from_m.at[low], 3, up),
        remote(part_a, from_p.at[low], 4, down),
        remote(part_b, from_m.at[high], 5, up),
        remote(sum_own.at[low], sum_down.at[low], 6, up),
        remote(sum_own.at[high], sum_up.at[high], 7, down),
        remote(sum_own.at[high], sum_down.at[high], 8, up),
        remote(sum_own.at[low], sum_up.at[low], 9, down),
        remote(sum_down.at[low], sum_over.at[low], 10, up),
        remote(sum_up.at[high], sum_over.at[high], 11, down),
    ]
    upper, lower = pl.ds(0, 128), pl.ds(128, 128)

    def root(slot, place, src, dst, x):
        return cross(src, dst, root_send.at[slot, place], root_recv.at[slot, place], x)

    root_copies = []
    for slot in range(SLOTS):
        mine, there = left.at[slot], roots.at[slot, me_x]
        below, above = roots.at[slot, down, upper], roots.at[slot, up, lower]
        root_copies.append([
            root(slot, 0, mine.at[upper], there.at[upper], up),
            root(slot, 1, mine.at[lower], there.at[lower], down),
            root(slot, 2, mine.at[lower], there.at[lower], up),
            root(slot, 3, mine.at[upper], there.at[upper], down),
            root(slot, 4, below, below, up),
            root(slot, 5, above, above, down),
        ])
    keep = pltpu.make_async_copy(left, roots.at[:, me_x], keep_sem)
    fetch_right = pltpu.make_async_copy(right, right_box, right_sem)
    fetch_left_fac = pltpu.make_async_copy(left_fac, left_box, fac_sem.at[0])
    fetch_right_fac = pltpu.make_async_copy(right_fac, right_fac_box, fac_sem.at[1])
    size = QROWS * COLS
    quarters = (over, down, up, me_x)
    loads = [
        pltpu.make_async_copy(
            grads.at[:, pl.ds(pl.multiple_of(quarters[part] * size, size), size)],
            flat.at[part % 2], flat_sem.at[part % 2],
        )
        for part in range(N_X)
    ]

    def unpack(part, first, last):
        def step(col, carry):
            for half in range(2):
                for line in range(16):
                    at = pl.multiple_of((half * 16 + line) * COLS + col * BLK, BLK)
                    mid[line * STEP : line * STEP + 8, :] = (
                        flat[part % 2, :, pl.ds(at, BLK)].astype(f32).reshape(8, 128)
                    )
                for lane in range(8):
                    tiles[part, col, half * 16 : half * 16 + 16, lane * 128 : lane * 128 + 128] = (
                        mid[pl.ds(lane, 16, STEP), :].astype(bf16)
                    )
            return carry

        lax.fori_loop(first, last, step, 0)

    def piece(quarter, index):
        place = index % SLOTS
        holder = lax.rem(index // SLOTS + me_s // NBR, SUBS) * NBR + lax.rem(row + NBR - place, NBR)
        src = outbox.at[quarter, index]
        dst = blocks.at[place, sub, quarter]
        away = lambda: pltpu.make_async_remote_copy(
            src_ref=src, dst_ref=dst, send_sem=piece_send.at[quarter, index],
            recv_sem=piece_recv.at[place], device_id=(me_x, holder), device_id_type=MESH,
        )
        home = lambda: pltpu.make_async_copy(src, dst, piece_recv.at[place])
        return place, holder, away, home

    def spread(quarter, total):
        def step(index, carry):
            place, holder, away, home = piece(quarter, index)
            block = table[holder, place]
            outbox[quarter, index] = total[lax.rem(jnp.maximum(block, 0), NBC)]

            @pl.when(holder != me_s)
            def _():
                away().start()

            @pl.when(holder == me_s)
            def _():
                home().start()

            return carry

        lax.fori_loop(0, CELLS, step, 0)

    def locate(col, carry):
        wanted = row * NBC + col
        early, late, is_late = 0, 0, 0
        for cell in range(CELLS):
            block_of, place = cell // SLOTS, cell % SLOTS
            holder = block_of * NBR + lax.rem(row + NBR - place, NBR)
            found = table[holder, place] == wanted
            if place == SLOTS - 1:
                late = jnp.where(found, block_of, late)
                is_late = jnp.where(found, 1, is_late)
            else:
                early = jnp.where(found, block_of * 2 + place, early)
        places[0, col] = early
        places[1, col] = late
        places[2, col] = is_late
        return carry

    def add_a(col, carry):
        part_a[col] = (fwd_a[col].astype(f32) + tiles[DOWN, col].astype(f32)).astype(bf16)
        return carry

    def add_b(col, carry):
        part_b[col] = (fwd_b[col].astype(f32) + tiles[UP, CUT + col].astype(f32)).astype(bf16)
        return carry

    def add_all(col, carry):
        sum_own[col] = (
            tiles[OWN, col].astype(f32) + (from_p[col].astype(f32) + from_m[col].astype(f32))
        ).astype(bf16)
        return carry

    loads[0].start()
    loads[1].start()
    fetch_right.start()
    fetch_left_fac.start()
    fetch_right_fac.start()
    hail(me_x, me_s)
    loads[0].wait()
    unpack(OVER, 0, CUT)
    admitted()
    keep.start()
    copies[0].start()
    unpack(OVER, CUT, NBC)
    copies[1].start()
    loads[2].start()
    loads[1].wait()
    unpack(DOWN, 0, NBC)
    copies[2].start()
    loads[3].start()
    loads[2].wait()
    unpack(UP, 0, NBC)
    copies[3].start()
    copies[0].wait_recv()
    lax.fori_loop(0, CUT, add_a, 0)
    copies[4].start()
    copies[1].wait_recv()
    lax.fori_loop(0, NBC - CUT, add_b, 0)
    copies[5].start()
    loads[3].wait()
    unpack(OWN, 0, NBC)
    copies[3].wait_recv()
    copies[4].wait_recv()
    lax.fori_loop(0, CUT, add_all, 0)
    copies[6].start()
    copies[9].start()
    copies[2].wait_recv()
    copies[5].wait_recv()
    lax.fori_loop(CUT, NBC, add_all, 0)
    copies[7].start()
    copies[8].start()
    for slot in range(SLOTS):
        for place in range(4):
            root_copies[slot][place].start()
    spread(me_x, sum_own)
    lax.fori_loop(0, NBC, locate, 0)
    copies[6].wait_recv()
    copies[10].start()
    copies[7].wait_recv()
    copies[11].start()
    copies[8].wait_recv()
    spread(down, sum_down)
    copies[9].wait_recv()
    spread(up, sum_up)
    copies[10].wait_recv()
    copies[11].wait_recv()
    spread(over, sum_over)
    for slot in range(SLOTS):
        root_copies[slot][0].wait_recv()
        root_copies[slot][4].start()
        root_copies[slot][1].wait_recv()
        root_copies[slot][5].start()

    fetch_right.wait()
    powers = []
    for slot in range(SLOTS):
        pltpu.make_async_copy(blocks.at[slot], blocks.at[slot], piece_recv.at[slot]).wait()
        grad = blocks[slot].reshape(BLK, BLK)
        precond[slot] = contract_last(grad, right_box[slot]).astype(bf16)
        powers.append(jnp.sum(jnp.square(grad.astype(f32))) / (BLK * BLK))

    def back(place, group, count):
        target_sub = lax.rem(count + sub, SUBS)
        target = lax.rem(me_s + place, NBR) * SUBS + target_sub
        if group is None:
            src = scaled.at[place, target_sub]
            dst = inbox_early.at[me_s // NBR * 2 + place]
            send_sem, recv_sem = back_send.at[place, count], early_recv
        else:
            src = scaled.at[place, target_sub, pl.ds(group * QROWS, QROWS)]
            dst = inbox[group].at[me_s // NBR]
            send_sem, recv_sem = back_send.at[place + group, count], back_recv.at[group]
        away = lambda: pltpu.make_async_remote_copy(
            src_ref=src, dst_ref=dst, send_sem=send_sem, recv_sem=recv_sem,
            device_id=(me_x, target), device_id_type=MESH,
        )
        home = lambda: pltpu.make_async_copy(src, dst, recv_sem)
        return target, away, home

    def give_back(place, group):
        def step(count, carry):
            target, away, home = back(place, group, count)

            @pl.when(target != me_s)
            def _():
                away().start()

            @pl.when(target == me_s)
            def _():
                home().start()

            return carry

        lax.fori_loop(0, SUBS, step, 0)

    shares = []

    def direct(slot):
        for place in range(2, 6):
            root_copies[slot][place].wait_recv()
        result = jnp.dot(
            roots[slot].reshape(BLK, BLK), precond[slot], preferred_element_type=f32
        )
        direction[slot] = result
        sums[slot] = jnp.full((8, 128), jnp.sum(jnp.square(result)), f32)
        shares.append([])
        for index, x in enumerate((up, down, over)):
            share = cross(
                sums.at[slot], sum_box.at[slot, index],
                sum_send.at[slot, index], sum_recv.at[slot, index], x,
            )
            share.start()
            shares[slot].append(share)

    def graft(slot):
        for share in shares[slot]:
            share.wait_recv()
        total = sums[slot] + (sum_box[slot, 0] + sum_box[slot, 1] + sum_box[slot, 2])
        factor = jnp.sqrt(powers[slot]) / jnp.sqrt(total[0:1] / (BLK * BLK) + EPSILON)
        scale = jnp.concatenate([factor, factor], axis=1)

        def step(part, carry):
            scaled[slot, part] = (
                direction[slot, pl.ds(pl.multiple_of(part * 128, 128), 128)] * scale
            ).astype(bf16)
            return carry

        lax.fori_loop(0, SUBS, step, 0)

    keep.wait()
    direct(0)
    direct(1)
    graft(0)
    give_back(0, None)
    direct(2)
    graft(1)
    give_back(1, None)
    graft(2)
    give_back(2, 0)
    give_back(2, 1)

    def ring(src, dst, group, place, x):
        return cross(src, dst, ring_send.at[group, place], ring_recv.at[group, place], x)

    def links(group):
        mine = update.at[me_x, group]
        below, above = update.at[down, group, low], update.at[up, group, high]
        return [
            ring(own.at[group, low], mine.at[low], group, 0, up),
            ring(own.at[group, high], mine.at[high], group, 1, down),
            ring(own.at[group, high], mine.at[high], group, 2, up),
            ring(own.at[group, low], mine.at[low], group, 3, down),
            ring(below, below, group, 4, up),
            ring(above, above, group, 5, down),
            pltpu.make_async_copy(own.at[group], mine, local_sem.at[group]),
        ]

    every = [links(group) for group in range(GROUPS)]

    def statistics(slot):
        whole = blocks[slot].reshape(BLK, BLK)
        scale = jnp.where(table[me_s, slot] >= 0, 1.0 / BLK, 0.0).astype(f32)
        rows = blocks[slot, pl.ds(me_x * 2, 2)].reshape(256, BLK)
        left_box[slot] = left_box[slot] + contract_last(rows, whole) * scale
        start = pl.multiple_of(me_x * 256, 256)
        cols = blocks[slot, :, :, :, pl.ds(start, 256)].reshape(BLK, 256)
        right_fac_box[slot] = (
            right_fac_box[slot] + jnp.dot(cols.T, whole, preferred_element_type=f32) * scale
        )
        for copy in leave(slot):
            copy.start()

    def leave(slot):
        return [
            pltpu.make_async_copy(left_box.at[slot], new_left.at[slot], out_sem.at[slot, 0]),
            pltpu.make_async_copy(right_fac_box.at[slot], new_right.at[slot], out_sem.at[slot, 1]),
        ]

    def forward(group):
        every[group][0].wait_recv()
        every[group][4].start()
        every[group][1].wait_recv()
        every[group][5].start()

    fetch_left_fac.wait()
    fetch_right_fac.wait()
    pltpu.make_async_copy(inbox_early, inbox_early, early_recv).wait()
    for group in range(GROUPS):
        pltpu.make_async_copy(inbox[group], inbox[group], back_recv.at[group]).wait()

        def place_col(col, carry):
            early = inbox_early[places[0, col], pl.ds(group * QROWS, QROWS)]
            late = inbox[group][places[1, col]]
            own[group, col] = jnp.where(places[2, col] == 1, late, early)
            return carry

        lax.fori_loop(0, NBC, place_col, 0)
        for place in (0, 1, 2, 3, 6):
            every[group][place].start()
        if group + 2 < GROUPS:
            give_back(2, group + 2)
        if group > 0:
            forward(group - 1)
            statistics(group - 1)
    forward(GROUPS - 1)
    for group in range(GROUPS):
        for place in range(2, 6):
            every[group][place].wait_recv()
        for place in range(6):
            every[group][place].wait_send()
        every[group][6].wait()
    for slot in range(SLOTS):
        for copy in shares[slot] + root_copies[slot]:
            copy.wait_send()
        for copy in leave(slot):
            copy.wait()
    for copy in copies:
        copy.wait_send()

    def sent(index, carry):
        for quarter in range(N_X):
            place, holder, away, home = piece(quarter, index)

            @pl.when(holder != me_s)
            def _():
                away().wait_send()

        return carry

    lax.fori_loop(0, CELLS, sent, 0)

    def sent_back(count, carry):
        for place, group in ((0, None), (1, None), (2, 0), (2, 1), (2, 2), (2, 3)):
            target, back_away, back_home = back(place, group, count)

            @pl.when(target != me_s)
            def _():
                back_away().wait_send()

        return carry

    lax.fori_loop(0, SUBS, sent_back, 0)


def contract_last(a, b):
    return lax.dot_general(a, b, (((1,), (1,)), ((), ())), preferred_element_type=f32)


def on_device(grads, slot_table, left_factor, right_factor, left_root, right_root):
    smem = pl.BlockSpec(memory_space=pltpu.SMEM)
    hbm = pl.BlockSpec(memory_space=pl.ANY)
    dma = pltpu.SemaphoreType.DMA
    vmem = pltpu.VMEM

    new_left, new_right, update = pl.pallas_call(
        shampoo,
        in_specs=[smem] + [hbm] * 5,
        out_specs=[hbm] * 3,
        out_shape=[
            jax.ShapeDtypeStruct((SLOTS, 256, BLK), f32),
            jax.ShapeDtypeStruct((SLOTS, 256, BLK), f32),
            jax.ShapeDtypeStruct((N_X, GROUPS, NBC, QROWS, 256), bf16),
        ],
        scratch_shapes=[
            vmem((2, 1, QROWS * COLS), bf16),
            vmem((16 * STEP, 128), f32),
            vmem((N_X, NBC, QROWS, BLK), bf16),
            vmem((CUT, QROWS, BLK), bf16),
            vmem((NBC - CUT, QROWS, BLK), bf16),
            vmem((CUT, QROWS, BLK), bf16),
            vmem((NBC - CUT, QROWS, BLK), bf16),
        ]
        + [vmem((NBC, QROWS, BLK), bf16)] * 6
        + [
            vmem((N_X, CELLS, QROWS, BLK), bf16),
            vmem((SLOTS, SUBS, N_X, QROWS, BLK), bf16),
            vmem((SLOTS, N_X, 256, BLK), bf16),
            vmem((SLOTS, 256, BLK), bf16),
            vmem((SLOTS, BLK, 256), bf16),
            vmem((SLOTS, BLK, 256), f32),
            vmem((SLOTS, 8, 128), f32),
            vmem((SLOTS, 3, 8, 128), f32),
            vmem((SLOTS, SUBS, 128, 256), bf16),
            vmem((2 * SUBS, 128, 256), bf16),
        ]
        + [vmem((SUBS, QROWS, 256), bf16)] * GROUPS
        + [
            vmem((GROUPS, NBC, QROWS, 256), bf16),
            vmem((SLOTS, 256, BLK), f32),
            vmem((SLOTS, 256, BLK), f32),
            pltpu.SMEM((3, NBC), jnp.int32),
            dma((2,)),
            dma,
            dma,
            dma((SLOTS, 2)),
            dma((12,)),
            dma((12,)),
            dma((SLOTS, 6)),
            dma((SLOTS, 6)),
            dma((2,)),
            dma((N_X, CELLS)),
            dma((SLOTS,)),
            dma((SLOTS, 3)),
            dma((SLOTS, 3)),
            dma((2 + GROUPS, SUBS)),
            dma((GROUPS,)),
            dma,
            dma((GROUPS, 6)),
            dma((GROUPS, 6)),
            dma((GROUPS,)),
        ],
        compiler_params=pltpu.CompilerParams(
            collective_id=0, has_side_effects=True, vmem_limit_bytes=VMEM_BYTES
        ),
        name="shampoo",
    )(slot_table, grads, left_root[0], right_root[0], left_factor[0], right_factor[0])

    flat = pl.pallas_call(
        pack,
        grid=(GROUPS, 2),
        in_specs=[pl.BlockSpec((N_X, 1, NBC, 16, 256), lambda i, j: (0, i, 0, j, 0))],
        out_specs=pl.BlockSpec((1, 16 * COLS), lambda i, j: (0, i * 2 + j)),
        out_shape=jax.ShapeDtypeStruct((1, 128 * COLS), bf16),
        scratch_shapes=[pltpu.VMEM((16 * STEP, 128), f32)],
        compiler_params=pltpu.CompilerParams(vmem_limit_bytes=VMEM_BYTES),
        name="pack",
    )(update)
    return new_left[None], new_right[None], flat


def solution(mesh):
    rows = P("shard", None, "replica", None)
    flat = P("replica", "shard")
    return jax.shard_map(
        on_device,
        mesh=mesh,
        in_specs=(flat, P(), rows, rows, rows, rows),
        out_specs=(rows, rows, flat),
        check_vma=False,
    )
```

```python
import functools

import jax
import jax.numpy as jnp
from jax import lax
from jax.experimental import pallas as pl
from jax.experimental.pallas import tpu as pltpu
from jax.sharding import PartitionSpec as P

ROWS = 4096
COLS = 15360
BLK = 1024
EPSILON = 1e-06

N_X = 4
N_S = 32
SLOTS = 3
NBR = 4
NBC = 15
SUBS = 8
CELLS = 24
QROWS = 32
CUT = 8
GROUPS = 4
MESH = pl.DeviceIdType.MESH
f32 = jnp.float32
bf16 = jnp.bfloat16
VMEM_BYTES = 58 * 1024 * 1024


STEP = 9
WIDE = 3


def pack(in_ref, out_ref, mid):
    def step(count, carry):
        for lane in range(WIDE):
            col, work = count * WIDE + lane, mid.at[lane]
            for part in range(N_X):
                for half in range(2):
                    work[pl.ds(part * 2 + half, 16, STEP), :] = in_ref[
                        part, 0, col, :, half * 128 : half * 128 + 128
                    ].astype(f32)
        for lane in range(WIDE):
            col, work = count * WIDE + lane, mid.at[lane]
            for row in range(16):
                at = pl.multiple_of(row * COLS + col * BLK, BLK)
                out_ref[:, pl.ds(at, BLK)] = (
                    work[row * STEP : row * STEP + 8, :].reshape(1, BLK).astype(bf16)
                )
        return carry

    lax.fori_loop(0, NBC // WIDE, step, 0)


def hail(me_x, me_s):
    barrier = pltpu.get_barrier_semaphore()

    def one(step, carry):
        pl.semaphore_signal(
            barrier, inc=1, device_id=(me_x, lax.rem(me_s + step, N_S)), device_id_type=MESH
        )
        return carry

    lax.fori_loop(1, N_S, one, 0)
    for far in range(1, N_X):
        pl.semaphore_signal(
            barrier, inc=1, device_id=(lax.rem(me_x + far, N_X), me_s), device_id_type=MESH
        )


def admitted():
    pl.semaphore_wait(pltpu.get_barrier_semaphore(), N_S - 1 + N_X - 1)


def shampoo(
    table, grads, left, right, left_fac, right_fac, new_left, new_right, update,
    flat, mid, tiles, fwd_a, fwd_b, part_a, part_b, from_p, from_m,
    sum_own, sum_down, sum_up, sum_over, outbox, blocks, roots, right_box, precond, direction,
    sums, sum_box, scaled, inbox_early, inbox_0, inbox_1, inbox_2, inbox_3, own, left_box, right_fac_box, places,
    flat_sem, right_sem, keep_sem, out_sem, send, recv, root_send, root_recv,
    fac_sem, piece_send, piece_recv, sum_send, sum_recv, back_send, back_recv, early_recv, ring_send, ring_recv, local_sem,
):
    me_x, me_s = lax.axis_index("replica"), lax.axis_index("shard")
    row, sub = me_s // SUBS, lax.rem(me_s, SUBS)
    up, down, over = lax.rem(me_x + 1, N_X), lax.rem(me_x + 3, N_X), lax.rem(me_x + 2, N_X)
    low, high = pl.ds(0, CUT), pl.ds(CUT, NBC - CUT)
    inbox = (inbox_0, inbox_1, inbox_2, inbox_3)
    OVER, DOWN, UP, OWN = range(4)

    def cross(src, dst, send_sem, recv_sem, x):
        return pltpu.make_async_remote_copy(
            src_ref=src, dst_ref=dst, send_sem=send_sem, recv_sem=recv_sem,
            device_id=(x, me_s), device_id_type=MESH,
        )

    def remote(src, dst, place, x):
        return cross(src, dst, send.at[place], recv.at[place], x)

    copies = [
        remote(tiles.at[OVER, low], fwd_a, 0, down),
        remote(tiles.at[OVER, high], fwd_b, 1, up),
        remote(tiles.at[DOWN, high], from_p.at[high], 2, down),
        remote(tiles.at[UP, low], from_m.at[low], 3, up),
        remote(part_a, from_p.at[low], 4, down),
        remote(part_b, from_m.at[high], 5, up),
        remote(sum_own.at[low], sum_down.at[low], 6, up),
        remote(sum_own.at[high], sum_up.at[high], 7, down),
        remote(sum_own.at[high], sum_down.at[high], 8, up),
        remote(sum_own.at[low], sum_up.at[low], 9, down),
        remote(sum_down.at[low], sum_over.at[low], 10, up),
        remote(sum_up.at[high], sum_over.at[high], 11, down),
    ]
    upper, lower = pl.ds(0, 128), pl.ds(128, 128)

    def root(slot, place, src, dst, x):
        return cross(src, dst, root_send.at[slot, place], root_recv.at[slot, place], x)

    root_copies = []
    for slot in range(SLOTS):
        mine, there = left.at[slot], roots.at[slot, me_x]
        below, above = roots.at[slot, down, upper], roots.at[slot, up, lower]
        root_copies.append([
            root(slot, 0, mine.at[upper], there.at[upper], up),
            root(slot, 1, mine.at[lower], there.at[lower], down),
            root(slot, 2, mine.at[lower], there.at[lower], up),
            root(slot, 3, mine.at[upper], there.at[upper], down),
            root(slot, 4, below, below, up),
            root(slot, 5, above, above, down),
        ])
    keep = pltpu.make_async_copy(left, roots.at[:, me_x], keep_sem)
    fetch_right = pltpu.make_async_copy(right, right_box, right_sem)
    fetch_left_fac = pltpu.make_async_copy(left_fac, left_box, fac_sem.at[0])
    fetch_right_fac = pltpu.make_async_copy(right_fac, right_fac_box, fac_sem.at[1])
    size = QROWS * COLS
    quarters = (over, down, up, me_x)
    loads = [
        pltpu.make_async_copy(
            grads.at[:, pl.ds(pl.multiple_of(quarters[part] * size, size), size)],
            flat.at[part % 2], flat_sem.at[part % 2],
        )
        for part in range(N_X)
    ]

    def unpack(part, first, last):
        def step(col, carry):
            for half in range(2):
                for line in range(16):
                    at = pl.multiple_of((half * 16 + line) * COLS + col * BLK, BLK)
                    mid[half, line * STEP : line * STEP + 8, :] = (
                        flat[part % 2, :, pl.ds(at, BLK)].astype(f32).reshape(8, 128)
                    )
            for half in range(2):
                for lane in range(8):
                    tiles[part, col, half * 16 : half * 16 + 16, lane * 128 : lane * 128 + 128] = (
                        mid[half, pl.ds(lane, 16, STEP), :].astype(bf16)
                    )
            return carry

        lax.fori_loop(first, last, step, 0)

    def piece(quarter, index):
        place = index % SLOTS
        holder = lax.rem(index // SLOTS + me_s // NBR, SUBS) * NBR + lax.rem(row + NBR - place, NBR)
        src = outbox.at[quarter, index]
        dst = blocks.at[place, sub, quarter]
        away = lambda: pltpu.make_async_remote_copy(
            src_ref=src, dst_ref=dst, send_sem=piece_send.at[quarter, index],
            recv_sem=piece_recv.at[place], device_id=(me_x, holder), device_id_type=MESH,
        )
        home = lambda: pltpu.make_async_copy(src, dst, piece_recv.at[place])
        return place, holder, away, home

    def spread(quarter, total, between=()):
        def step(index, carry):
            place, holder, away, home = piece(quarter, index)
            block = table[place, holder]
            outbox[quarter, index] = total[lax.rem(jnp.maximum(block, 0), NBC)]

            @pl.when(holder != me_s)
            def _():
                away().start()

            @pl.when(holder == me_s)
            def _():
                home().start()

            return carry

        run = CELLS // max(len(between), 1)
        for part in range(CELLS // run):
            for copy in between[part : part + 1]:
                copy.start()
            lax.fori_loop(part * run, part * run + run, step, 0)

    def locate(col, carry):
        wanted = row * NBC + col
        early, late, is_late = 0, 0, 0
        for cell in range(CELLS):
            block_of, place = cell // SLOTS, cell % SLOTS
            holder = block_of * NBR + lax.rem(row + NBR - place, NBR)
            found = table[place, holder] == wanted
            if place == SLOTS - 1:
                late = jnp.where(found, block_of, late)
                is_late = jnp.where(found, 1, is_late)
            else:
                early = jnp.where(found, block_of * 2 + place, early)
        places[0, col] = early
        places[1, col] = late
        places[2, col] = is_late
        return carry

    def add_a(col, carry):
        part_a[col] = (fwd_a[col].astype(f32) + tiles[DOWN, col].astype(f32)).astype(bf16)
        return carry

    def add_b(col, carry):
        part_b[col] = (fwd_b[col].astype(f32) + tiles[UP, CUT + col].astype(f32)).astype(bf16)
        return carry

    def add_all(col, carry):
        sum_own[col] = (
            tiles[OWN, col].astype(f32) + (from_p[col].astype(f32) + from_m[col].astype(f32))
        ).astype(bf16)
        return carry

    loads[0].start()
    loads[1].start()
    fetch_right.start()
    fetch_left_fac.start()
    fetch_right_fac.start()
    hail(me_x, me_s)
    loads[0].wait()
    unpack(OVER, 0, CUT)
    admitted()
    keep.start()
    copies[0].start()
    unpack(OVER, CUT, NBC)
    copies[1].start()
    loads[2].start()
    loads[1].wait()
    unpack(DOWN, 0, NBC)
    copies[2].start()
    loads[3].start()
    loads[2].wait()
    unpack(UP, 0, NBC)
    copies[3].start()
    copies[0].wait_recv()
    lax.fori_loop(0, CUT, add_a, 0)
    copies[4].start()
    copies[1].wait_recv()
    lax.fori_loop(0, NBC - CUT, add_b, 0)
    copies[5].start()
    loads[3].wait()
    unpack(OWN, 0, NBC)
    copies[3].wait_recv()
    copies[4].wait_recv()
    lax.fori_loop(0, CUT, add_all, 0)
    copies[6].start()
    copies[9].start()
    copies[2].wait_recv()
    copies[5].wait_recv()
    lax.fori_loop(CUT, NBC, add_all, 0)
    spread(me_x, sum_own, copies[7:9])
    lax.fori_loop(0, NBC, locate, 0)
    copies[6].wait_recv()
    copies[10].start()
    copies[7].wait_recv()
    copies[11].start()
    copies[8].wait_recv()
    spread(down, sum_down, root_copies[0][:4])
    copies[9].wait_recv()
    spread(up, sum_up, root_copies[1][:4])
    copies[10].wait_recv()
    copies[11].wait_recv()
    spread(over, sum_over, root_copies[2][:4])
    for slot in range(SLOTS):
        root_copies[slot][0].wait_recv()
        root_copies[slot][4].start()
        root_copies[slot][1].wait_recv()
        root_copies[slot][5].start()

    fetch_right.wait()
    powers = []
    for slot in range(SLOTS):
        pltpu.make_async_copy(blocks.at[slot], blocks.at[slot], piece_recv.at[slot]).wait()
        grad = blocks[slot].reshape(BLK, BLK)
        precond[slot] = contract_last(grad, right_box[slot]).astype(bf16)
        powers.append(jnp.sum(jnp.square(grad.astype(f32))) / (BLK * BLK))

    def back(place, group, count):
        target_sub = lax.rem(count + sub, SUBS)
        target = lax.rem(me_s + place, NBR) * SUBS + target_sub
        if group is None:
            src = scaled.at[place, target_sub]
            dst = inbox_early.at[me_s // NBR * 2 + place]
            send_sem, recv_sem = back_send.at[place, count], early_recv
        else:
            src = scaled.at[place, target_sub, pl.ds(group * QROWS, QROWS)]
            dst = inbox[group].at[me_s // NBR]
            send_sem, recv_sem = back_send.at[place + group, count], back_recv.at[group]
        away = lambda: pltpu.make_async_remote_copy(
            src_ref=src, dst_ref=dst, send_sem=send_sem, recv_sem=recv_sem,
            device_id=(me_x, target), device_id_type=MESH,
        )
        home = lambda: pltpu.make_async_copy(src, dst, recv_sem)
        return target, away, home

    def give_back(place, group):
        def step(count, carry):
            target, away, home = back(place, group, count)

            @pl.when(target != me_s)
            def _():
                away().start()

            @pl.when(target == me_s)
            def _():
                home().start()

            return carry

        lax.fori_loop(0, SUBS, step, 0)

    shares = []

    def direct(slot):
        for place in range(2, 6):
            root_copies[slot][place].wait_recv()
        result = jnp.dot(
            roots[slot].reshape(BLK, BLK), precond[slot], preferred_element_type=f32
        )
        direction[slot] = result
        sums[slot] = jnp.full((8, 128), jnp.sum(jnp.square(result)), f32)
        shares.append([])
        for index, x in enumerate((up, down, over)):
            share = cross(
                sums.at[slot], sum_box.at[slot, index],
                sum_send.at[slot, index], sum_recv.at[slot, index], x,
            )
            share.start()
            shares[slot].append(share)

    def graft(slot):
        for share in shares[slot]:
            share.wait_recv()
        total = sums[slot] + (sum_box[slot, 0] + sum_box[slot, 1] + sum_box[slot, 2])
        factor = jnp.sqrt(powers[slot]) / jnp.sqrt(total[0:1] / (BLK * BLK) + EPSILON)
        scale = jnp.concatenate([factor, factor], axis=1)

        def step(part, carry):
            scaled[slot, part] = (
                direction[slot, pl.ds(pl.multiple_of(part * 128, 128), 128)] * scale
            ).astype(bf16)
            return carry

        lax.fori_loop(0, SUBS, step, 0)

    keep.wait()
    direct(0)
    direct(1)
    graft(0)
    give_back(0, None)
    direct(2)
    graft(1)
    give_back(1, None)
    graft(2)
    give_back(2, 0)
    give_back(2, 1)

    def ring(src, dst, group, place, x):
        return cross(src, dst, ring_send.at[group, place], ring_recv.at[group, place], x)

    def links(group):
        mine = update.at[me_x, group]
        below, above = update.at[down, group, low], update.at[up, group, high]
        return [
            ring(own.at[group, low], mine.at[low], group, 0, up),
            ring(own.at[group, high], mine.at[high], group, 1, down),
            ring(own.at[group, high], mine.at[high], group, 2, up),
            ring(own.at[group, low], mine.at[low], group, 3, down),
            ring(below, below, group, 4, up),
            ring(above, above, group, 5, down),
            pltpu.make_async_copy(own.at[group], mine, local_sem.at[group]),
        ]

    every = [links(group) for group in range(GROUPS)]

    def statistics(slot):
        whole = blocks[slot].reshape(BLK, BLK)
        scale = jnp.where(table[slot, me_s] >= 0, 1.0 / BLK, 0.0).astype(f32)
        rows = blocks[slot, pl.ds(me_x * 2, 2)].reshape(256, BLK)
        left_box[slot] = left_box[slot] + contract_last(rows, whole) * scale
        start = pl.multiple_of(me_x * 256, 256)
        cols = blocks[slot, :, :, :, pl.ds(start, 256)].reshape(BLK, 256)
        right_fac_box[slot] = (
            right_fac_box[slot] + jnp.dot(cols.T, whole, preferred_element_type=f32) * scale
        )
        for copy in leave(slot):
            copy.start()

    def leave(slot):
        return [
            pltpu.make_async_copy(left_box.at[slot], new_left.at[slot], out_sem.at[slot, 0]),
            pltpu.make_async_copy(right_fac_box.at[slot], new_right.at[slot], out_sem.at[slot, 1]),
        ]

    def forward(group):
        every[group][0].wait_recv()
        every[group][4].start()
        every[group][1].wait_recv()
        every[group][5].start()

    fetch_left_fac.wait()
    fetch_right_fac.wait()
    pltpu.make_async_copy(inbox_early, inbox_early, early_recv).wait()
    for group in range(GROUPS):
        pltpu.make_async_copy(inbox[group], inbox[group], back_recv.at[group]).wait()

        def place_col(col, carry):
            early = inbox_early[places[0, col], pl.ds(group * QROWS, QROWS)]
            late = inbox[group][places[1, col]]
            own[group, col] = jnp.where(places[2, col] == 1, late, early)
            return carry

        lax.fori_loop(0, NBC, place_col, 0)
        for place in (0, 1, 2, 3, 6):
            every[group][place].start()
        if group + 2 < GROUPS:
            give_back(2, group + 2)
        if group > 0:
            forward(group - 1)
            statistics(group - 1)
    forward(GROUPS - 1)
    for group in range(GROUPS):
        for place in range(2, 6):
            every[group][place].wait_recv()
        for place in range(6):
            every[group][place].wait_send()
        every[group][6].wait()
    for slot in range(SLOTS):
        for copy in shares[slot] + root_copies[slot]:
            copy.wait_send()
        for copy in leave(slot):
            copy.wait()
    for copy in copies:
        copy.wait_send()

    def sent(index, carry):
        for quarter in range(N_X):
            place, holder, away, home = piece(quarter, index)

            @pl.when(holder != me_s)
            def _():
                away().wait_send()

        return carry

    lax.fori_loop(0, CELLS, sent, 0)

    def sent_back(count, carry):
        for place, group in ((0, None), (1, None), (2, 0), (2, 1), (2, 2), (2, 3)):
            target, back_away, back_home = back(place, group, count)

            @pl.when(target != me_s)
            def _():
                back_away().wait_send()

        return carry

    lax.fori_loop(0, SUBS, sent_back, 0)


def contract_last(a, b):
    return lax.dot_general(a, b, (((1,), (1,)), ((), ())), preferred_element_type=f32)


def on_device(grads, slot_table, left_factor, right_factor, left_root, right_root):
    smem = pl.BlockSpec(memory_space=pltpu.SMEM)
    hbm = pl.BlockSpec(memory_space=pl.ANY)
    dma = pltpu.SemaphoreType.DMA
    vmem = pltpu.VMEM

    new_left, new_right, update = pl.pallas_call(
        shampoo,
        in_specs=[smem] + [hbm] * 5,
        out_specs=[hbm] * 3,
        out_shape=[
            jax.ShapeDtypeStruct((SLOTS, 256, BLK), f32),
            jax.ShapeDtypeStruct((SLOTS, 256, BLK), f32),
            jax.ShapeDtypeStruct((N_X, GROUPS, NBC, QROWS, 256), bf16),
        ],
        scratch_shapes=[
            vmem((2, 1, QROWS * COLS), bf16),
            vmem((2, 16 * STEP, 128), f32),
            vmem((N_X, NBC, QROWS, BLK), bf16),
            vmem((CUT, QROWS, BLK), bf16),
            vmem((NBC - CUT, QROWS, BLK), bf16),
            vmem((CUT, QROWS, BLK), bf16),
            vmem((NBC - CUT, QROWS, BLK), bf16),
        ]
        + [vmem((NBC, QROWS, BLK), bf16)] * 6
        + [
            vmem((N_X, CELLS, QROWS, BLK), bf16),
            vmem((SLOTS, SUBS, N_X, QROWS, BLK), bf16),
            vmem((SLOTS, N_X, 256, BLK), bf16),
            vmem((SLOTS, 256, BLK), bf16),
            vmem((SLOTS, BLK, 256), bf16),
            vmem((SLOTS, BLK, 256), f32),
            vmem((SLOTS, 8, 128), f32),
            vmem((SLOTS, 3, 8, 128), f32),
            vmem((SLOTS, SUBS, 128, 256), bf16),
            vmem((2 * SUBS, 128, 256), bf16),
        ]
        + [vmem((SUBS, QROWS, 256), bf16)] * GROUPS
        + [
            vmem((GROUPS, NBC, QROWS, 256), bf16),
            vmem((SLOTS, 256, BLK), f32),
            vmem((SLOTS, 256, BLK), f32),
            pltpu.SMEM((3, NBC), jnp.int32),
            dma((2,)),
            dma,
            dma,
            dma((SLOTS, 2)),
            dma((12,)),
            dma((12,)),
            dma((SLOTS, 6)),
            dma((SLOTS, 6)),
            dma((2,)),
            dma((N_X, CELLS)),
            dma((SLOTS,)),
            dma((SLOTS, 3)),
            dma((SLOTS, 3)),
            dma((2 + GROUPS, SUBS)),
            dma((GROUPS,)),
            dma,
            dma((GROUPS, 6)),
            dma((GROUPS, 6)),
            dma((GROUPS,)),
        ],
        compiler_params=pltpu.CompilerParams(
            collective_id=0, has_side_effects=True, vmem_limit_bytes=VMEM_BYTES
        ),
        name="shampoo",
    )(slot_table.T, grads, left_root[0], right_root[0], left_factor[0], right_factor[0])

    flat = pl.pallas_call(
        pack,
        grid=(GROUPS, 2),
        in_specs=[pl.BlockSpec((N_X, 1, NBC, 16, 256), lambda i, j: (0, i, 0, j, 0))],
        out_specs=pl.BlockSpec((1, 16 * COLS), lambda i, j: (0, i * 2 + j)),
        out_shape=jax.ShapeDtypeStruct((1, 128 * COLS), bf16),
        scratch_shapes=[pltpu.VMEM((WIDE, 16 * STEP, 128), f32)],
        compiler_params=pltpu.CompilerParams(vmem_limit_bytes=VMEM_BYTES),
        name="pack",
    )(update)
    return new_left[None], new_right[None], flat


def solution(mesh):
    rows = P("shard", None, "replica", None)
    flat = P("replica", "shard")
    return jax.shard_map(
        on_device,
        mesh=mesh,
        in_specs=(flat, P(), rows, rows, rows, rows),
        out_specs=(rows, rows, flat),
        check_vma=False,
    )
```

```python
import functools

import jax
import jax.numpy as jnp
from jax import lax
from jax.experimental import pallas as pl
from jax.experimental.pallas import tpu as pltpu
from jax.sharding import PartitionSpec as P

ROWS = 4096
COLS = 15360
BLK = 1024
EPSILON = 1e-06

N_X = 4
N_S = 32
SLOTS = 3
NBR = 4
NBC = 15
SUBS = 8
CELLS = 24
QROWS = 32
CUT = 8
GROUPS = 4
MESH = pl.DeviceIdType.MESH
f32 = jnp.float32
bf16 = jnp.bfloat16
VMEM_BYTES = 58 * 1024 * 1024


STEP = 9
HALVES = 2
HROWS = 64
LINES = NBC * 8


def finish(flat_ref, left_ref, right_ref, out_ref, left_out, right_out, sems):
    step = pl.program_id(0)
    copies = (
        pltpu.make_async_copy(left_ref, left_out, sems.at[0]),
        pltpu.make_async_copy(right_ref, right_out, sems.at[1]),
    )

    @pl.when(step == 0)
    def _():
        for copy in copies:
            copy.start()

    def part(count, carry):
        at = pl.ds(pl.multiple_of(count * COLS, COLS), COLS)
        out_ref[:, at] = flat_ref[:, at].astype(bf16)
        return carry

    lax.fori_loop(0, 16, part, 0)

    @pl.when(step == pl.num_programs(0) - 1)
    def _():
        for copy in copies:
            copy.wait()


def hail(me_x, me_s):
    barrier = pltpu.get_barrier_semaphore()

    def one(step, carry):
        pl.semaphore_signal(
            barrier, inc=1, device_id=(me_x, lax.rem(me_s + step, N_S)), device_id_type=MESH
        )
        return carry

    lax.fori_loop(1, N_S, one, 0)
    for far in range(1, N_X):
        pl.semaphore_signal(
            barrier, inc=1, device_id=(lax.rem(me_x + far, N_X), me_s), device_id_type=MESH
        )


def admitted():
    pl.semaphore_wait(pltpu.get_barrier_semaphore(), N_S - 1 + N_X - 1)


def shampoo(
    table, grads, left, right, left_fac, right_fac, new_left, new_right, update,
    flat, mid, tiles, fwd_a, fwd_b, part_a, part_b, from_p, from_m,
    sum_own, sum_down, sum_up, sum_over, outbox, blocks, roots, right_box, precond,
    sums, sum_box, factors, factor_box, raw, inbox_0, inbox_1, gathered, lines, left_box, right_fac_box, places,
    flat_sem, right_sem, keep_sem, out_sem, send, recv, root_send, root_recv,
    fac_sem, piece_send, piece_recv, sum_send, sum_recv, factor_send, factor_recv,
    back_send, back_recv, ring_send, ring_recv, line_sem,
):
    me_x, me_s = lax.axis_index("replica"), lax.axis_index("shard")
    row, sub = me_s // SUBS, lax.rem(me_s, SUBS)
    up, down, over = lax.rem(me_x + 1, N_X), lax.rem(me_x + 3, N_X), lax.rem(me_x + 2, N_X)
    low, high = pl.ds(0, CUT), pl.ds(CUT, NBC - CUT)
    inbox = (inbox_0, inbox_1)
    OVER, DOWN, UP, OWN = range(4)

    def cross(src, dst, send_sem, recv_sem, x):
        return pltpu.make_async_remote_copy(
            src_ref=src, dst_ref=dst, send_sem=send_sem, recv_sem=recv_sem,
            device_id=(x, me_s), device_id_type=MESH,
        )

    def remote(src, dst, place, x):
        return cross(src, dst, send.at[place], recv.at[place], x)

    copies = [
        remote(tiles.at[OVER, low], fwd_a, 0, down),
        remote(tiles.at[OVER, high], fwd_b, 1, up),
        remote(tiles.at[DOWN, high], from_p.at[high], 2, down),
        remote(tiles.at[UP, low], from_m.at[low], 3, up),
        remote(part_a, from_p.at[low], 4, down),
        remote(part_b, from_m.at[high], 5, up),
        remote(sum_own.at[low], sum_down.at[low], 6, up),
        remote(sum_own.at[high], sum_up.at[high], 7, down),
        remote(sum_own.at[high], sum_down.at[high], 8, up),
        remote(sum_own.at[low], sum_up.at[low], 9, down),
        remote(sum_down.at[low], sum_over.at[low], 10, up),
        remote(sum_up.at[high], sum_over.at[high], 11, down),
    ]
    def root(slot, half):
        mine, there = left.at[slot], roots.at[slot, me_x]
        below, above = roots.at[slot, down, 0, half], roots.at[slot, up, 1, half]

        def one(place, src, dst, x):
            return cross(
                src, dst, root_send.at[slot, half, place], root_recv.at[slot, half, place], x
            )

        return [
            one(0, mine.at[0, half], there.at[0, half], up),
            one(1, mine.at[1, half], there.at[1, half], down),
            one(2, mine.at[1, half], there.at[1, half], up),
            one(3, mine.at[0, half], there.at[0, half], down),
            one(4, below, below, up),
            one(5, above, above, down),
        ]

    root_copies = [[root(slot, half) for slot in range(SLOTS)] for half in range(HALVES)]

    def pass_root(half, slot):
        for place in range(2):
            root_copies[half][slot][place].wait_recv()
            root_copies[half][slot][place + 4].start()

    keep = pltpu.make_async_copy(left, roots.at[:, me_x], keep_sem)
    fetch_right = pltpu.make_async_copy(right, right_box, right_sem)
    fetch_left_fac = pltpu.make_async_copy(left_fac, left_box, fac_sem.at[0])
    fetch_right_fac = pltpu.make_async_copy(right_fac, right_fac_box, fac_sem.at[1])
    size = QROWS * COLS
    quarters = (over, down, up, me_x)
    loads = [
        pltpu.make_async_copy(
            grads.at[:, pl.ds(pl.multiple_of(quarters[part] * size, size), size)],
            flat.at[part % 2], flat_sem.at[part % 2],
        )
        for part in range(N_X)
    ]

    def unpack(part, first, last):
        def step(col, carry):
            for half in range(2):
                for line in range(16):
                    at = pl.multiple_of((half * 16 + line) * COLS + col * BLK, BLK)
                    mid[half, line * STEP : line * STEP + 8, :] = (
                        flat[part % 2, :, pl.ds(at, BLK)].astype(f32).reshape(8, 128)
                    )
            for half in range(2):
                for lane in range(8):
                    tiles[part, col, half * 16 : half * 16 + 16, lane * 128 : lane * 128 + 128] = (
                        mid[half, pl.ds(lane, 16, STEP), :].astype(bf16)
                    )
            return carry

        lax.fori_loop(first, last, step, 0)

    def piece(quarter, index):
        place = index % SLOTS
        holder = lax.rem(index // SLOTS + me_s // NBR, SUBS) * NBR + lax.rem(row + NBR - place, NBR)
        src = outbox.at[quarter, index]
        dst = blocks.at[place, sub, quarter]
        away = lambda: pltpu.make_async_remote_copy(
            src_ref=src, dst_ref=dst, send_sem=piece_send.at[quarter, index],
            recv_sem=piece_recv.at[place], device_id=(me_x, holder), device_id_type=MESH,
        )
        home = lambda: pltpu.make_async_copy(src, dst, piece_recv.at[place])
        return place, holder, away, home

    def spread(quarter, total, between=()):
        def step(index, carry):
            place, holder, away, home = piece(quarter, index)
            block = table[place, holder]
            outbox[quarter, index] = total[lax.rem(jnp.maximum(block, 0), NBC)]

            @pl.when(holder != me_s)
            def _():
                away().start()

            @pl.when(holder == me_s)
            def _():
                home().start()

            return carry

        run = CELLS // max(len(between), 1)
        for part in range(CELLS // run):
            for copy in between[part : part + 1]:
                copy.start()
            lax.fori_loop(part * run, part * run + run, step, 0)

    def locate(col, carry):
        wanted = row * NBC + col
        index = 0
        for cell in range(CELLS):
            place = cell % SLOTS
            holder = cell // SLOTS * NBR + lax.rem(row + NBR - place, NBR)
            index = jnp.where(table[place, holder] == wanted, cell, index)
        places[col] = index
        return carry

    def add_a(col, carry):
        part_a[col] = (fwd_a[col].astype(f32) + tiles[DOWN, col].astype(f32)).astype(bf16)
        return carry

    def add_b(col, carry):
        part_b[col] = (fwd_b[col].astype(f32) + tiles[UP, CUT + col].astype(f32)).astype(bf16)
        return carry

    def add_all(col, carry):
        sum_own[col] = (
            tiles[OWN, col].astype(f32) + (from_p[col].astype(f32) + from_m[col].astype(f32))
        ).astype(bf16)
        return carry

    loads[0].start()
    loads[1].start()
    fetch_right.start()
    fetch_left_fac.start()
    fetch_right_fac.start()
    hail(me_x, me_s)
    loads[0].wait()
    unpack(OVER, 0, CUT)
    admitted()
    keep.start()
    copies[0].start()
    for copy in root_copies[0][0][:4]:
        copy.start()
    unpack(OVER, CUT, NBC)
    copies[1].start()
    loads[2].start()
    loads[1].wait()
    unpack(DOWN, 0, NBC)
    copies[2].start()
    loads[3].start()
    loads[2].wait()
    unpack(UP, 0, NBC)
    copies[3].start()
    copies[0].wait_recv()
    lax.fori_loop(0, CUT, add_a, 0)
    copies[4].start()
    copies[1].wait_recv()
    lax.fori_loop(0, NBC - CUT, add_b, 0)
    copies[5].start()
    for copy in root_copies[0][1][:4]:
        copy.start()
    loads[3].wait()
    unpack(OWN, 0, NBC)
    copies[3].wait_recv()
    copies[4].wait_recv()
    lax.fori_loop(0, CUT, add_all, 0)
    copies[6].start()
    copies[9].start()
    copies[2].wait_recv()
    copies[5].wait_recv()
    lax.fori_loop(CUT, NBC, add_all, 0)
    spread(me_x, sum_own, copies[7:9])
    lax.fori_loop(0, NBC, locate, 0)
    copies[6].wait_recv()
    copies[10].start()
    copies[7].wait_recv()
    copies[11].start()
    pass_root(0, 0)
    pass_root(0, 1)
    copies[8].wait_recv()
    spread(down, sum_down, root_copies[0][2][:4])
    copies[9].wait_recv()
    spread(up, sum_up, root_copies[1][0][:4])
    copies[10].wait_recv()
    copies[11].wait_recv()
    spread(over, sum_over, root_copies[1][1][:4] + root_copies[1][2][:4])
    pass_root(0, 2)
    for slot in range(SLOTS):
        pass_root(1, slot)

    fetch_right.wait()
    powers = []
    for slot in range(SLOTS):
        pltpu.make_async_copy(blocks.at[slot], blocks.at[slot], piece_recv.at[slot]).wait()
        grad = blocks[slot].reshape(BLK, BLK)
        precond[slot] = contract_last(grad, right_box[slot]).astype(bf16)
        powers.append(jnp.sum(jnp.square(grad.astype(f32))) / (BLK * BLK))

    def target_of(place, count):
        target_sub = lax.rem(count + sub, SUBS)
        return target_sub, lax.rem(me_s + place, NBR) * SUBS + target_sub

    def sender(src, dst, send_sem, recv_sem, target):
        away = lambda: pltpu.make_async_remote_copy(
            src_ref=src, dst_ref=dst, send_sem=send_sem, recv_sem=recv_sem,
            device_id=(me_x, target), device_id_type=MESH,
        )
        home = lambda: pltpu.make_async_copy(src, dst, recv_sem)
        return target, away, home

    def back(place, half, count):
        target_sub, target = target_of(place, count)
        return sender(
            raw.at[half, place, target_sub], inbox[half].at[me_s // NBR * SLOTS + place],
            back_send.at[half, place, count], back_recv.at[half], target,
        )

    def tell(place, count):
        target_sub, target = target_of(place, count)
        return sender(
            factors.at[place], factor_box.at[me_s // NBR * SLOTS + place],
            factor_send.at[place, count], factor_recv, target,
        )

    def start_all(describe):
        def step(count, carry):
            target, away, home = describe(count)

            @pl.when(target != me_s)
            def _():
                away().start()

            @pl.when(target == me_s)
            def _():
                home().start()

            return carry

        lax.fori_loop(0, SUBS, step, 0)

    def finish_all(describe):
        def step(count, carry):
            target, away, home = describe(count)

            @pl.when(target != me_s)
            def _():
                away().wait_send()

            return carry

        lax.fori_loop(0, SUBS, step, 0)

    squares = [[] for slot in range(SLOTS)]

    def direct(half, slot):
        for copy in root_copies[half][slot][2:]:
            copy.wait_recv()
        result = jnp.dot(
            roots[slot, :, :, half].reshape(BLK // HALVES, BLK), precond[slot],
            preferred_element_type=f32,
        )
        raw[half, slot] = result.astype(bf16).reshape(SUBS, HROWS, 256)
        start_all(functools.partial(back, slot, half))
        squares[slot].append(jnp.sum(jnp.square(result)))

    shares = []

    def share(slot):
        sums[slot] = jnp.full((8, 128), squares[slot][0] + squares[slot][1], f32)
        for index, x in enumerate((up, down, over)):
            copy = cross(
                sums.at[slot], sum_box.at[slot, index],
                sum_send.at[slot, index], sum_recv.at[slot, index], x,
            )
            copy.start()
            shares.append(copy)

    def graft(slot):
        total = sums[slot] + (sum_box[slot, 0] + sum_box[slot, 1] + sum_box[slot, 2])
        factors[slot] = jnp.sqrt(powers[slot]) / jnp.sqrt(total / (BLK * BLK) + EPSILON)
        start_all(functools.partial(tell, slot))

    def ring(src, dst, group, place, x):
        return cross(src, dst, ring_send.at[group, place], ring_recv.at[group, place], x)

    def links(group):
        mine = gathered.at[me_x, group]
        below, above = gathered.at[down, group, low], gathered.at[up, group, high]
        return [
            ring(mine.at[low], mine.at[low], group, 0, up),
            ring(mine.at[high], mine.at[high], group, 1, down),
            ring(mine.at[high], mine.at[high], group, 2, up),
            ring(mine.at[low], mine.at[low], group, 3, down),
            ring(below, below, group, 4, up),
            ring(above, above, group, 5, down),
        ]

    every = [links(group) for group in range(GROUPS)]

    def statistics(slot):
        whole = blocks[slot].reshape(BLK, BLK)
        scale = jnp.where(table[slot, me_s] >= 0, 1.0 / BLK, 0.0).astype(f32)
        rows = blocks[slot, pl.ds(me_x * 2, 2)].reshape(256, BLK)
        left_box[slot] = left_box[slot] + contract_last(rows, whole) * scale
        start = pl.multiple_of(me_x * 256, 256)
        cols = blocks[slot, :, :, :, pl.ds(start, 256)].reshape(BLK, 256)
        right_fac_box[slot] = (
            right_fac_box[slot] + jnp.dot(cols.T, whole, preferred_element_type=f32) * scale
        )
        for copy in leave(slot):
            copy.start()

    def leave(slot):
        return [
            pltpu.make_async_copy(left_box.at[slot], new_left.at[slot], out_sem.at[slot, 0]),
            pltpu.make_async_copy(right_fac_box.at[slot], new_right.at[slot], out_sem.at[slot, 1]),
        ]

    def forward(group):
        every[group][0].wait_recv()
        every[group][4].start()
        every[group][1].wait_recv()
        every[group][5].start()

    def place_group(group):
        half, first = group // 2, group % 2 * QROWS

        def step(col, carry):
            gathered[me_x, group, col] = inbox[half][places[col], pl.ds(first, QROWS)]
            return carry

        lax.fori_loop(0, NBC, step, 0)

    def ring_group(group):
        for copy in every[group][:4]:
            copy.start()

    def line_copy(group):
        count = QROWS * LINES
        return pltpu.make_async_copy(
            lines.at[group % 2], update.at[pl.ds(group * count, count)], line_sem.at[group % 2]
        )

    def flatten(group):
        for copy in every[group][2:]:
            copy.wait_recv()
        if group >= 2:
            line_copy(group - 2).wait()

        def step(col, carry):
            factor = factor_box[places[col]][0:1, :]
            for part in range(N_X):
                for rows in range(2):
                    for lane in range(2):
                        value = gathered[
                            part, group, col, rows * 16 : rows * 16 + 16, lane * 128 : lane * 128 + 128
                        ].astype(f32)
                        at = rows * 16 * LINES + col * 8 + part * 2 + lane
                        lines[group % 2, pl.ds(at, 16, LINES), :] = value * factor
            return carry

        lax.fori_loop(0, NBC, step, 0)
        line_copy(group).start()

    keep.wait()
    for slot in range(SLOTS):
        direct(0, slot)
    pltpu.make_async_copy(inbox_0, inbox_0, back_recv.at[0]).wait()
    place_group(0)
    ring_group(0)
    place_group(1)
    for slot in range(SLOTS):
        direct(1, slot)
    ring_group(1)
    for slot in range(SLOTS):
        share(slot)
    forward(0)
    pltpu.make_async_copy(inbox_1, inbox_1, back_recv.at[1]).wait()
    place_group(2)
    ring_group(2)
    place_group(3)
    ring_group(3)
    for copy in shares:
        copy.wait_recv()
    for slot in range(SLOTS):
        graft(slot)
    forward(1)
    fetch_left_fac.wait()
    fetch_right_fac.wait()
    statistics(0)
    forward(2)
    statistics(1)
    pltpu.make_async_copy(factor_box, factor_box, factor_recv).wait()
    flatten(0)
    flatten(1)
    forward(3)
    statistics(2)
    flatten(2)
    flatten(3)
    line_copy(2).wait()
    line_copy(3).wait()
    for group in range(GROUPS):
        for copy in every[group]:
            copy.wait_send()
    for copy in shares + copies:
        copy.wait_send()
    for slot in range(SLOTS):
        for half in range(HALVES):
            for copy in root_copies[half][slot]:
                copy.wait_send()
            finish_all(functools.partial(back, slot, half))
        finish_all(functools.partial(tell, slot))
        for copy in leave(slot):
            copy.wait()

    def sent(index, carry):
        for quarter in range(N_X):
            place, holder, away, home = piece(quarter, index)

            @pl.when(holder != me_s)
            def _():
                away().wait_send()

        return carry

    lax.fori_loop(0, CELLS, sent, 0)


def contract_last(a, b):
    return lax.dot_general(a, b, (((1,), (1,)), ((), ())), preferred_element_type=f32)


def on_device(grads, slot_table, left_factor, right_factor, left_root, right_root):
    smem = pl.BlockSpec(memory_space=pltpu.SMEM)
    hbm = pl.BlockSpec(memory_space=pl.ANY)
    dma = pltpu.SemaphoreType.DMA
    vmem = pltpu.VMEM

    new_left, new_right, update = pl.pallas_call(
        shampoo,
        in_specs=[smem] + [hbm] * 5,
        out_specs=[hbm] * 3,
        out_shape=[
            jax.ShapeDtypeStruct((SLOTS, 256, BLK), f32),
            jax.ShapeDtypeStruct((SLOTS, 256, BLK), f32),
            jax.ShapeDtypeStruct((128 * LINES, 128), f32),
        ],
        scratch_shapes=[
            vmem((2, 1, QROWS * COLS), bf16),
            vmem((2, 16 * STEP, 128), f32),
            vmem((N_X, NBC, QROWS, BLK), bf16),
            vmem((CUT, QROWS, BLK), bf16),
            vmem((NBC - CUT, QROWS, BLK), bf16),
            vmem((CUT, QROWS, BLK), bf16),
            vmem((NBC - CUT, QROWS, BLK), bf16),
        ]
        + [vmem((NBC, QROWS, BLK), bf16)] * 6
        + [
            vmem((N_X, CELLS, QROWS, BLK), bf16),
            vmem((SLOTS, SUBS, N_X, QROWS, BLK), bf16),
            vmem((SLOTS, N_X, 2, HALVES, HROWS, BLK), bf16),
            vmem((SLOTS, 256, BLK), bf16),
            vmem((SLOTS, BLK, 256), bf16),
            vmem((SLOTS, 8, 128), f32),
            vmem((SLOTS, 3, 8, 128), f32),
            vmem((SLOTS, 8, 128), f32),
            vmem((CELLS, 8, 128), f32),
            vmem((HALVES, SLOTS, SUBS, HROWS, 256), bf16),
            vmem((CELLS, HROWS, 256), bf16),
            vmem((CELLS, HROWS, 256), bf16),
            vmem((N_X, GROUPS, NBC, QROWS, 256), bf16),
            vmem((2, QROWS * LINES, 128), f32),
            vmem((SLOTS, 256, BLK), f32),
            vmem((SLOTS, 256, BLK), f32),
            pltpu.SMEM((NBC,), jnp.int32),
            dma((2,)),
            dma,
            dma,
            dma((SLOTS, 2)),
            dma((12,)),
            dma((12,)),
            dma((SLOTS, HALVES, 6)),
            dma((SLOTS, HALVES, 6)),
            dma((2,)),
            dma((N_X, CELLS)),
            dma((SLOTS,)),
            dma((SLOTS, 3)),
            dma((SLOTS, 3)),
            dma((SLOTS, SUBS)),
            dma,
            dma((HALVES, SLOTS, SUBS)),
            dma((HALVES,)),
            dma((GROUPS, 6)),
            dma((GROUPS, 6)),
            dma((2,)),
        ],
        compiler_params=pltpu.CompilerParams(
            collective_id=0, has_side_effects=True, vmem_limit_bytes=VMEM_BYTES
        ),
        name="shampoo",
    )(slot_table.T, grads, left_root.reshape(SLOTS, 2, HALVES, HROWS, BLK), right_root[0], left_factor[0], right_factor[0])

    piece = 16 * COLS
    flat, new_left, new_right = pl.pallas_call(
        finish,
        grid=(8,),
        in_specs=[pl.BlockSpec((1, piece), lambda i: (0, i)), hbm, hbm],
        out_specs=[pl.BlockSpec((1, piece), lambda i: (0, i)), hbm, hbm],
        out_shape=[
            jax.ShapeDtypeStruct((1, 128 * COLS), bf16),
            jax.ShapeDtypeStruct((SLOTS, 256, BLK), f32),
            jax.ShapeDtypeStruct((SLOTS, 256, BLK), f32),
        ],
        scratch_shapes=[dma((2,))],
        compiler_params=pltpu.CompilerParams(vmem_limit_bytes=VMEM_BYTES),
        name="finish",
    )(update.reshape(1, 128 * COLS), new_left, new_right)
    return new_left[None], new_right[None], flat


def solution(mesh):
    rows = P("shard", None, "replica", None)
    flat = P("replica", "shard")
    return jax.shard_map(
        on_device,
        mesh=mesh,
        in_specs=(flat, P(), rows, rows, rows, rows),
        out_specs=(rows, rows, flat),
        check_vma=False,
    )
```

```python
import functools

import jax
import jax.numpy as jnp
from jax import lax
from jax.experimental import pallas as pl
from jax.experimental.pallas import tpu as pltpu
from jax.sharding import PartitionSpec as P

ROWS = 4096
COLS = 15360
BLK = 1024
EPSILON = 1e-06

N_X = 4
N_S = 32
SLOTS = 3
NBR = 4
NBC = 15
SUBS = 8
CELLS = 24
QROWS = 32
CUT = 8
GROUPS = 4
MESH = pl.DeviceIdType.MESH
f32 = jnp.float32
bf16 = jnp.bfloat16
VMEM_BYTES = 58 * 1024 * 1024


STEP = 9
HALVES = 2
HROWS = 64
LINES = NBC * 8


def finish(lines_ref, left_ref, right_ref, out_ref, left_out, right_out):
    left_out[...] = left_ref[...]
    right_out[...] = right_ref[...]

    def part(count, carry):
        for line in range(NBC):
            at = count * NBC + line
            rows = lines_ref[pl.ds(pl.multiple_of(at * 8, 8), 8), :]
            out_ref[:, pl.ds(pl.multiple_of(at * BLK, BLK), BLK)] = rows.reshape(1, BLK).astype(bf16)
        return carry

    lax.fori_loop(0, 16, part, 0)


def hail(me_x, me_s):
    barrier = pltpu.get_barrier_semaphore()

    def one(step, carry):
        pl.semaphore_signal(
            barrier, inc=1, device_id=(me_x, lax.rem(me_s + step, N_S)), device_id_type=MESH
        )
        return carry

    lax.fori_loop(1, N_S, one, 0)
    for far in range(1, N_X):
        pl.semaphore_signal(
            barrier, inc=1, device_id=(lax.rem(me_x + far, N_X), me_s), device_id_type=MESH
        )


def admitted():
    pl.semaphore_wait(pltpu.get_barrier_semaphore(), N_S - 1 + N_X - 1)


def shampoo(
    table, grads, left, right, left_fac, right_fac, new_left, new_right, update,
    flat, mid, tiles, fwd_a, fwd_b, part_a, part_b, from_p, from_m,
    sum_own, outbox, blocks, roots, right_box, precond,
    sums, sum_box, factors, factor_box, raw, inbox_0, inbox_1, gathered, lines, left_box, right_fac_box, places,
    flat_sem, right_sem, keep_sem, out_sem, send, recv, root_send, root_recv,
    fac_sem, piece_send, piece_recv, block_send, block_recv, sum_send, sum_recv, factor_send, factor_recv,
    back_send, back_recv, ring_send, ring_recv, line_sem,
):
    me_x, me_s = lax.axis_index("replica"), lax.axis_index("shard")
    row, sub = me_s // SUBS, lax.rem(me_s, SUBS)
    up, down, over = lax.rem(me_x + 1, N_X), lax.rem(me_x + 3, N_X), lax.rem(me_x + 2, N_X)
    low, high = pl.ds(0, CUT), pl.ds(CUT, NBC - CUT)
    inbox = (inbox_0, inbox_1)
    OVER, DOWN, UP, OWN = range(4)

    def cross(src, dst, send_sem, recv_sem, x):
        return pltpu.make_async_remote_copy(
            src_ref=src, dst_ref=dst, send_sem=send_sem, recv_sem=recv_sem,
            device_id=(x, me_s), device_id_type=MESH,
        )

    def remote(src, dst, place, x):
        return cross(src, dst, send.at[place], recv.at[place], x)

    copies = [
        remote(tiles.at[OVER, low], fwd_a, 0, down),
        remote(tiles.at[OVER, high], fwd_b, 1, up),
        remote(tiles.at[DOWN, high], from_p.at[high], 2, down),
        remote(tiles.at[UP, low], from_m.at[low], 3, up),
        remote(part_a, from_p.at[low], 4, down),
        remote(part_b, from_m.at[high], 5, up),
    ]
    def root(slot, half):
        mine, there = left.at[slot], roots.at[slot, me_x]
        below, above = roots.at[slot, down, 0, half], roots.at[slot, up, 1, half]

        def one(place, src, dst, x):
            return cross(
                src, dst, root_send.at[slot, half, place], root_recv.at[slot, half, place], x
            )

        return [
            one(0, mine.at[0, half], there.at[0, half], up),
            one(1, mine.at[1, half], there.at[1, half], down),
            one(2, mine.at[1, half], there.at[1, half], up),
            one(3, mine.at[0, half], there.at[0, half], down),
            one(4, below, below, up),
            one(5, above, above, down),
        ]

    root_copies = [[root(slot, half) for slot in range(SLOTS)] for half in range(HALVES)]

    def pass_root(half, slot):
        for place in range(2):
            root_copies[half][slot][place].wait_recv()
            root_copies[half][slot][place + 4].start()

    keep = pltpu.make_async_copy(left, roots.at[:, me_x], keep_sem)
    fetch_right = pltpu.make_async_copy(right, right_box, right_sem)
    fetch_left_fac = pltpu.make_async_copy(left_fac, left_box, fac_sem.at[0])
    fetch_right_fac = pltpu.make_async_copy(right_fac, right_fac_box, fac_sem.at[1])
    size = QROWS * COLS
    quarters = (over, down, up, me_x)
    loads = [
        pltpu.make_async_copy(
            grads.at[:, pl.ds(pl.multiple_of(quarters[part] * size, size), size)],
            flat.at[part % 2], flat_sem.at[part % 2],
        )
        for part in range(N_X)
    ]

    def unpack(part, first, last):
        def step(col, carry):
            for half in range(2):
                for line in range(16):
                    at = pl.multiple_of((half * 16 + line) * COLS + col * BLK, BLK)
                    mid[half, line * STEP : line * STEP + 8, :] = (
                        flat[part % 2, :, pl.ds(at, BLK)].astype(f32).reshape(8, 128)
                    )
            for half in range(2):
                for lane in range(8):
                    tiles[part, col, half * 16 : half * 16 + 16, lane * 128 : lane * 128 + 128] = (
                        mid[half, pl.ds(lane, 16, STEP), :].astype(bf16)
                    )
            return carry

        lax.fori_loop(first, last, step, 0)

    def sender(src, dst, send_sem, recv_sem, target):
        away = lambda: pltpu.make_async_remote_copy(
            src_ref=src, dst_ref=dst, send_sem=send_sem, recv_sem=recv_sem,
            device_id=(me_x, target), device_id_type=MESH,
        )
        home = lambda: pltpu.make_async_copy(src, dst, recv_sem)
        return target, away, home

    def piece(place, count):
        holder = lax.rem(count + me_s // NBR, SUBS) * NBR + lax.rem(row + NBR - place, NBR)
        src, dst = outbox.at[place, count], blocks.at[place, sub, me_x]
        target, away, home = sender(
            src, dst, piece_send.at[place, count], piece_recv.at[place], holder
        )
        return target, away, home

    def spread(place):
        def step(count, carry):
            holder, away, home = piece(place, count)
            block = table[place, holder]
            outbox[place, count] = sum_own[lax.rem(jnp.maximum(block, 0), NBC)]

            @pl.when(holder != me_s)
            def _():
                away().start()

            @pl.when(holder == me_s)
            def _():
                home().start()

            return carry

        lax.fori_loop(0, SUBS, step, 0)

    def gather_block(slot):
        first, second = pl.ds(0, 4), pl.ds(4, 4)

        def one(place, subs, x_from, x):
            ref = blocks.at[slot, subs, x_from]
            return cross(ref, ref, block_send.at[slot, place], block_recv.at[slot, place], x)

        return [
            one(0, first, me_x, up),
            one(1, second, me_x, down),
            one(2, second, me_x, up),
            one(3, first, me_x, down),
            one(4, first, down, up),
            one(5, second, up, down),
        ]

    block_copies = [gather_block(slot) for slot in range(SLOTS)]

    def pass_block(slot):
        for place in range(2):
            block_copies[slot][place].wait_recv()
            block_copies[slot][place + 4].start()

    def locate(col, carry):
        wanted = row * NBC + col
        index = 0
        for cell in range(CELLS):
            place = cell % SLOTS
            holder = cell // SLOTS * NBR + lax.rem(row + NBR - place, NBR)
            index = jnp.where(table[place, holder] == wanted, cell, index)
        places[col] = index
        return carry

    def add_a(col, carry):
        part_a[col] = (fwd_a[col].astype(f32) + tiles[DOWN, col].astype(f32)).astype(bf16)
        return carry

    def add_b(col, carry):
        part_b[col] = (fwd_b[col].astype(f32) + tiles[UP, CUT + col].astype(f32)).astype(bf16)
        return carry

    def add_all(col, carry):
        sum_own[col] = (
            tiles[OWN, col].astype(f32) + (from_p[col].astype(f32) + from_m[col].astype(f32))
        ).astype(bf16)
        return carry

    loads[0].start()
    loads[1].start()
    fetch_right.start()
    fetch_left_fac.start()
    fetch_right_fac.start()
    hail(me_x, me_s)
    loads[0].wait()
    unpack(OVER, 0, CUT)
    admitted()
    keep.start()
    copies[0].start()
    for copy in root_copies[0][0][:4]:
        copy.start()
    unpack(OVER, CUT, NBC)
    copies[1].start()
    loads[2].start()
    loads[1].wait()
    unpack(DOWN, 0, NBC)
    copies[2].start()
    loads[3].start()
    loads[2].wait()
    unpack(UP, 0, NBC)
    copies[3].start()
    copies[0].wait_recv()
    lax.fori_loop(0, CUT, add_a, 0)
    copies[4].start()
    copies[1].wait_recv()
    lax.fori_loop(0, NBC - CUT, add_b, 0)
    copies[5].start()
    loads[3].wait()
    unpack(OWN, 0, NBC)
    copies[3].wait_recv()
    copies[4].wait_recv()
    lax.fori_loop(0, CUT, add_all, 0)
    copies[2].wait_recv()
    copies[5].wait_recv()
    lax.fori_loop(CUT, NBC, add_all, 0)
    for slot in range(SLOTS):
        spread(slot)
    for half, slot in ((0, 1), (0, 2), (1, 0)):
        for copy in root_copies[half][slot][:4]:
            copy.start()
    lax.fori_loop(0, NBC, locate, 0)
    pass_root(0, 0)
    for slot in range(SLOTS):
        arrived = blocks.at[slot, :, me_x]
        pltpu.make_async_copy(arrived, arrived, piece_recv.at[slot]).wait()
        for copy in block_copies[slot][:4]:
            copy.start()
    pass_root(0, 1)
    pass_root(0, 2)
    pass_root(1, 0)
    for slot in range(1, SLOTS):
        for copy in root_copies[1][slot][:4]:
            copy.start()
    for slot in range(SLOTS):
        pass_block(slot)

    fetch_right.wait()
    powers = []
    for slot in range(SLOTS):
        for copy in block_copies[slot][2:]:
            copy.wait_recv()
        grad = blocks[slot].reshape(BLK, BLK)
        precond[slot] = contract_last(grad, right_box[slot]).astype(bf16)
        powers.append(jnp.sum(jnp.square(grad.astype(f32))) / (BLK * BLK))

    def target_of(place, count):
        target_sub = lax.rem(count + sub, SUBS)
        return target_sub, lax.rem(me_s + place, NBR) * SUBS + target_sub

    def back(place, half, count):
        target_sub, target = target_of(place, count)
        return sender(
            raw.at[half, place, target_sub], inbox[half].at[me_s // NBR * SLOTS + place],
            back_send.at[half, place, count], back_recv.at[half], target,
        )

    def tell(place, count):
        target_sub, target = target_of(place, count)
        return sender(
            factors.at[place], factor_box.at[me_s // NBR * SLOTS + place],
            factor_send.at[place, count], factor_recv, target,
        )

    def start_all(describe):
        def step(count, carry):
            target, away, home = describe(count)

            @pl.when(target != me_s)
            def _():
                away().start()

            @pl.when(target == me_s)
            def _():
                home().start()

            return carry

        lax.fori_loop(0, SUBS, step, 0)

    def finish_all(describe):
        def step(count, carry):
            target, away, home = describe(count)

            @pl.when(target != me_s)
            def _():
                away().wait_send()

            return carry

        lax.fori_loop(0, SUBS, step, 0)

    squares = [[] for slot in range(SLOTS)]

    def direct(half, slot):
        for copy in root_copies[half][slot][2:]:
            copy.wait_recv()
        result = jnp.dot(
            roots[slot, :, :, half].reshape(BLK // HALVES, BLK), precond[slot],
            preferred_element_type=f32,
        )
        raw[half, slot] = result.astype(bf16).reshape(SUBS, HROWS, 256)
        start_all(functools.partial(back, slot, half))
        squares[slot].append(jnp.sum(jnp.square(result)))

    shares = []

    def share(slot):
        sums[slot] = jnp.full((8, 128), squares[slot][0] + squares[slot][1], f32)
        for index, x in enumerate((up, down, over)):
            copy = cross(
                sums.at[slot], sum_box.at[slot, index],
                sum_send.at[slot, index], sum_recv.at[slot, index], x,
            )
            copy.start()
            shares.append(copy)

    def graft(slot):
        total = sums[slot] + (sum_box[slot, 0] + sum_box[slot, 1] + sum_box[slot, 2])
        factors[slot] = jnp.sqrt(powers[slot]) / jnp.sqrt(total / (BLK * BLK) + EPSILON)
        start_all(functools.partial(tell, slot))

    def ring(src, dst, group, place, x):
        return cross(src, dst, ring_send.at[group, place], ring_recv.at[group, place], x)

    def links(group):
        mine = gathered.at[me_x, group]
        below, above = gathered.at[down, group, low], gathered.at[up, group, high]
        return [
            ring(mine.at[low], mine.at[low], group, 0, up),
            ring(mine.at[high], mine.at[high], group, 1, down),
            ring(mine.at[high], mine.at[high], group, 2, up),
            ring(mine.at[low], mine.at[low], group, 3, down),
            ring(below, below, group, 4, up),
            ring(above, above, group, 5, down),
        ]

    every = [links(group) for group in range(GROUPS)]

    def statistics(slot):
        whole = blocks[slot].reshape(BLK, BLK)
        scale = jnp.where(table[slot, me_s] >= 0, 1.0 / BLK, 0.0).astype(f32)
        rows = blocks[slot, pl.ds(me_x * 2, 2)].reshape(256, BLK)
        left_box[slot] = left_box[slot] + contract_last(rows, whole) * scale
        start = pl.multiple_of(me_x * 256, 256)
        cols = blocks[slot, :, :, :, pl.ds(start, 256)].reshape(BLK, 256)
        right_fac_box[slot] = (
            right_fac_box[slot] + jnp.dot(cols.T, whole, preferred_element_type=f32) * scale
        )
        for copy in leave(slot):
            copy.start()

    def leave(slot):
        return [
            pltpu.make_async_copy(left_box.at[slot], new_left.at[slot], out_sem.at[slot, 0]),
            pltpu.make_async_copy(right_fac_box.at[slot], new_right.at[slot], out_sem.at[slot, 1]),
        ]

    def forward(group):
        every[group][0].wait_recv()
        every[group][4].start()
        every[group][1].wait_recv()
        every[group][5].start()

    def place_group(group):
        half, first = group // 2, group % 2 * QROWS

        def step(col, carry):
            gathered[me_x, group, col] = inbox[half][places[col], pl.ds(first, QROWS)]
            return carry

        lax.fori_loop(0, NBC, step, 0)

    def ring_group(group):
        for copy in every[group][:4]:
            copy.start()

    def line_copy(group):
        count = QROWS * LINES
        return pltpu.make_async_copy(
            lines.at[group % 2], update.at[pl.ds(group * count, count)], line_sem.at[group % 2]
        )

    def flatten(group):
        for copy in every[group][2:]:
            copy.wait_recv()
        if group >= 2:
            line_copy(group - 2).wait()

        def step(col, carry):
            factor = factor_box[places[col]][0:1, :]
            for part in range(N_X):
                for rows in range(2):
                    for lane in range(2):
                        value = gathered[
                            part, group, col, rows * 16 : rows * 16 + 16, lane * 128 : lane * 128 + 128
                        ].astype(f32)
                        at = rows * 16 * LINES + col * 8 + part * 2 + lane
                        lines[group % 2, pl.ds(at, 16, LINES), :] = value * factor
            return carry

        lax.fori_loop(0, NBC, step, 0)
        line_copy(group).start()

    keep.wait()
    for slot in range(SLOTS):
        direct(0, slot)
    for slot in range(1, SLOTS):
        pass_root(1, slot)
    pltpu.make_async_copy(inbox_0, inbox_0, back_recv.at[0]).wait()
    place_group(0)
    ring_group(0)
    place_group(1)
    for slot in range(SLOTS):
        direct(1, slot)
    ring_group(1)
    for slot in range(SLOTS):
        share(slot)
    forward(0)
    pltpu.make_async_copy(inbox_1, inbox_1, back_recv.at[1]).wait()
    place_group(2)
    ring_group(2)
    place_group(3)
    ring_group(3)
    for copy in shares:
        copy.wait_recv()
    for slot in range(SLOTS):
        graft(slot)
    forward(1)
    fetch_left_fac.wait()
    fetch_right_fac.wait()
    statistics(0)
    forward(2)
    statistics(1)
    pltpu.make_async_copy(factor_box, factor_box, factor_recv).wait()
    flatten(0)
    flatten(1)
    forward(3)
    statistics(2)
    flatten(2)
    flatten(3)
    line_copy(2).wait()
    line_copy(3).wait()
    for group in range(GROUPS):
        for copy in every[group]:
            copy.wait_send()
    for copy in shares + copies:
        copy.wait_send()
    for slot in range(SLOTS):
        for half in range(HALVES):
            for copy in root_copies[half][slot]:
                copy.wait_send()
            finish_all(functools.partial(back, slot, half))
        finish_all(functools.partial(tell, slot))
        finish_all(functools.partial(piece, slot))
        for copy in block_copies[slot]:
            copy.wait_send()
        for copy in leave(slot):
            copy.wait()


def contract_last(a, b):
    return lax.dot_general(a, b, (((1,), (1,)), ((), ())), preferred_element_type=f32)


def on_device(grads, slot_table, left_factor, right_factor, left_root, right_root):
    smem = pl.BlockSpec(memory_space=pltpu.SMEM)
    hbm = pl.BlockSpec(memory_space=pl.ANY)
    dma = pltpu.SemaphoreType.DMA
    vmem = pltpu.VMEM

    new_left, new_right, update = pl.pallas_call(
        shampoo,
        in_specs=[smem] + [hbm] * 5,
        out_specs=[hbm] * 3,
        out_shape=[
            jax.ShapeDtypeStruct((SLOTS, 256, BLK), f32),
            jax.ShapeDtypeStruct((SLOTS, 256, BLK), f32),
            jax.ShapeDtypeStruct((128 * LINES, 128), f32),
        ],
        scratch_shapes=[
            vmem((2, 1, QROWS * COLS), bf16),
            vmem((2, 16 * STEP, 128), f32),
            vmem((N_X, NBC, QROWS, BLK), bf16),
            vmem((CUT, QROWS, BLK), bf16),
            vmem((NBC - CUT, QROWS, BLK), bf16),
            vmem((CUT, QROWS, BLK), bf16),
            vmem((NBC - CUT, QROWS, BLK), bf16),
        ]
        + [vmem((NBC, QROWS, BLK), bf16)] * 3
        + [
            vmem((SLOTS, SUBS, QROWS, BLK), bf16),
            vmem((SLOTS, SUBS, N_X, QROWS, BLK), bf16),
            vmem((SLOTS, N_X, 2, HALVES, HROWS, BLK), bf16),
            vmem((SLOTS, 256, BLK), bf16),
            vmem((SLOTS, BLK, 256), bf16),
            vmem((SLOTS, 8, 128), f32),
            vmem((SLOTS, 3, 8, 128), f32),
            vmem((SLOTS, 8, 128), f32),
            vmem((CELLS, 8, 128), f32),
            vmem((HALVES, SLOTS, SUBS, HROWS, 256), bf16),
            vmem((CELLS, HROWS, 256), bf16),
            vmem((CELLS, HROWS, 256), bf16),
            vmem((N_X, GROUPS, NBC, QROWS, 256), bf16),
            vmem((2, QROWS * LINES, 128), f32),
            vmem((SLOTS, 256, BLK), f32),
            vmem((SLOTS, 256, BLK), f32),
            pltpu.SMEM((NBC,), jnp.int32),
            dma((2,)),
            dma,
            dma,
            dma((SLOTS, 2)),
            dma((6,)),
            dma((6,)),
            dma((SLOTS, HALVES, 6)),
            dma((SLOTS, HALVES, 6)),
            dma((2,)),
            dma((SLOTS, SUBS)),
            dma((SLOTS,)),
            dma((SLOTS, 6)),
            dma((SLOTS, 6)),
            dma((SLOTS, 3)),
            dma((SLOTS, 3)),
            dma((SLOTS, SUBS)),
            dma,
            dma((HALVES, SLOTS, SUBS)),
            dma((HALVES,)),
            dma((GROUPS, 6)),
            dma((GROUPS, 6)),
            dma((2,)),
        ],
        compiler_params=pltpu.CompilerParams(
            collective_id=0, has_side_effects=True, vmem_limit_bytes=VMEM_BYTES
        ),
        name="shampoo",
    )(slot_table.T, grads, left_root.reshape(SLOTS, 2, HALVES, HROWS, BLK), right_root[0], left_factor[0], right_factor[0])

    piece = 16 * COLS
    lines_in = pl.BlockSpec((16 * LINES, 128), lambda i: (i, 0))
    flat_out = pl.BlockSpec((1, piece), lambda i: (0, i))
    table_block = pl.BlockSpec((SLOTS, 32, BLK), lambda i: (0, i, 0))
    flat, new_left, new_right = pl.pallas_call(
        finish,
        grid=(8,),
        in_specs=[lines_in, table_block, table_block],
        out_specs=[flat_out, table_block, table_block],
        out_shape=[
            jax.ShapeDtypeStruct((1, 128 * COLS), bf16),
            jax.ShapeDtypeStruct((SLOTS, 256, BLK), f32),
            jax.ShapeDtypeStruct((SLOTS, 256, BLK), f32),
        ],
        compiler_params=pltpu.CompilerParams(vmem_limit_bytes=VMEM_BYTES),
        name="finish",
    )(update, new_left, new_right)
    return new_left[None], new_right[None], flat


def solution(mesh):
    rows = P("shard", None, "replica", None)
    flat = P("replica", "shard")
    return jax.shard_map(
        on_device,
        mesh=mesh,
        in_specs=(flat, P(), rows, rows, rows, rows),
        out_specs=(rows, rows, flat),
        check_vma=False,
    )
```

```python
import functools

import jax
import jax.numpy as jnp
from jax import lax
from jax.experimental import pallas as pl
from jax.experimental.pallas import tpu as pltpu
from jax.sharding import PartitionSpec as P

ROWS = 4096
COLS = 15360
BLK = 1024
EPSILON = 1e-06

N_X = 4
N_S = 32
SLOTS = 3
NBR = 4
NBC = 15
SUBS = 8
CELLS = 24
QROWS = 32
CUT = 8
GROUPS = 4
MESH = pl.DeviceIdType.MESH
f32 = jnp.float32
bf16 = jnp.bfloat16
VMEM_BYTES = 58 * 1024 * 1024


STEP = 9
HALVES = 2
HROWS = 64


def hail(me_x, me_s):
    barrier = pltpu.get_barrier_semaphore()

    def one(step, carry):
        pl.semaphore_signal(
            barrier, inc=1, device_id=(me_x, lax.rem(me_s + step, N_S)), device_id_type=MESH
        )
        return carry

    lax.fori_loop(1, N_S, one, 0)
    for far in range(1, N_X):
        pl.semaphore_signal(
            barrier, inc=1, device_id=(lax.rem(me_x + far, N_X), me_s), device_id_type=MESH
        )


def admitted():
    pl.semaphore_wait(pltpu.get_barrier_semaphore(), N_S - 1 + N_X - 1)


def shampoo(
    table, grads, left, right, left_fac, right_fac, new_left, new_right, update,
    flat, mid, tiles, fwd_a, fwd_b, part_a, part_b, from_p, from_m,
    sum_own, sum_down, sum_up, sum_over, outbox, blocks, roots, right_box, precond,
    sums, sum_box, factors, factor_box, raw, inbox_0, inbox_1, gathered, left_box, right_fac_box, places,
    flat_sem, right_sem, keep_sem, out_sem, send, recv, root_send, root_recv,
    fac_sem, piece_send, piece_recv, sum_send, sum_recv, factor_send, factor_recv,
    back_send, back_recv, ring_send, ring_recv,
):
    me_x, me_s = lax.axis_index("replica"), lax.axis_index("shard")
    row, sub = me_s // SUBS, lax.rem(me_s, SUBS)
    up, down, over = lax.rem(me_x + 1, N_X), lax.rem(me_x + 3, N_X), lax.rem(me_x + 2, N_X)
    low, high = pl.ds(0, CUT), pl.ds(CUT, NBC - CUT)
    inbox = (inbox_0, inbox_1)
    OVER, DOWN, UP, OWN = range(4)

    def cross(src, dst, send_sem, recv_sem, x):
        return pltpu.make_async_remote_copy(
            src_ref=src, dst_ref=dst, send_sem=send_sem, recv_sem=recv_sem,
            device_id=(x, me_s), device_id_type=MESH,
        )

    def remote(src, dst, place, x):
        return cross(src, dst, send.at[place], recv.at[place], x)

    copies = [
        remote(tiles.at[OVER, low], fwd_a, 0, down),
        remote(tiles.at[OVER, high], fwd_b, 1, up),
        remote(tiles.at[DOWN, high], from_p.at[high], 2, down),
        remote(tiles.at[UP, low], from_m.at[low], 3, up),
        remote(part_a, from_p.at[low], 4, down),
        remote(part_b, from_m.at[high], 5, up),
        remote(sum_own.at[low], sum_down.at[low], 6, up),
        remote(sum_own.at[high], sum_up.at[high], 7, down),
        remote(sum_own.at[high], sum_down.at[high], 8, up),
        remote(sum_own.at[low], sum_up.at[low], 9, down),
        remote(sum_down.at[low], sum_over.at[low], 10, up),
        remote(sum_up.at[high], sum_over.at[high], 11, down),
    ]
    def root(slot, half):
        mine, there = left.at[slot], roots.at[slot, me_x]
        below, above = roots.at[slot, down, 0, half], roots.at[slot, up, 1, half]

        def one(place, src, dst, x):
            return cross(
                src, dst, root_send.at[slot, half, place], root_recv.at[slot, half, place], x
            )

        return [
            one(0, mine.at[0, half], there.at[0, half], up),
            one(1, mine.at[1, half], there.at[1, half], down),
            one(2, mine.at[1, half], there.at[1, half], up),
            one(3, mine.at[0, half], there.at[0, half], down),
            one(4, below, below, up),
            one(5, above, above, down),
        ]

    root_copies = [[root(slot, half) for slot in range(SLOTS)] for half in range(HALVES)]

    def pass_root(half, slot):
        for place in range(2):
            root_copies[half][slot][place].wait_recv()
            root_copies[half][slot][place + 4].start()

    keep = pltpu.make_async_copy(left, roots.at[:, me_x], keep_sem)
    fetch_right = pltpu.make_async_copy(right, right_box, right_sem)
    fetch_left_fac = pltpu.make_async_copy(left_fac, left_box, fac_sem.at[0])
    fetch_right_fac = pltpu.make_async_copy(right_fac, right_fac_box, fac_sem.at[1])
    size = QROWS * COLS
    quarters = (over, down, up, me_x)
    loads = [
        pltpu.make_async_copy(
            grads.at[:, pl.ds(pl.multiple_of(quarters[part] * size, size), size)],
            flat.at[part % 2], flat_sem.at[part % 2],
        )
        for part in range(N_X)
    ]

    def unpack(part, first, last):
        def step(col, carry):
            for half in range(2):
                for line in range(16):
                    at = pl.multiple_of((half * 16 + line) * COLS + col * BLK, BLK)
                    mid[half, line * STEP : line * STEP + 8, :] = (
                        flat[part % 2, :, pl.ds(at, BLK)].astype(f32).reshape(8, 128)
                    )
            for half in range(2):
                for lane in range(8):
                    tiles[part, col, half * 16 : half * 16 + 16, lane * 128 : lane * 128 + 128] = (
                        mid[half, pl.ds(lane, 16, STEP), :].astype(bf16)
                    )
            return carry

        lax.fori_loop(first, last, step, 0)

    def piece(quarter, index):
        place = index % SLOTS
        holder = lax.rem(index // SLOTS + me_s // NBR, SUBS) * NBR + lax.rem(row + NBR - place, NBR)
        src = outbox.at[quarter, index]
        dst = blocks.at[place, sub, quarter]
        away = lambda: pltpu.make_async_remote_copy(
            src_ref=src, dst_ref=dst, send_sem=piece_send.at[quarter, index],
            recv_sem=piece_recv.at[place], device_id=(me_x, holder), device_id_type=MESH,
        )
        home = lambda: pltpu.make_async_copy(src, dst, piece_recv.at[place])
        return place, holder, away, home

    def spread(quarter, total, between=()):
        def step(count, carry):
            index = lax.rem(count * 7 + me_s * 5, CELLS)
            place, holder, away, home = piece(quarter, index)
            block = table[place, holder]
            outbox[quarter, index] = total[lax.rem(jnp.maximum(block, 0), NBC)]

            @pl.when(holder != me_s)
            def _():
                away().start()

            @pl.when(holder == me_s)
            def _():
                home().start()

            return carry

        run = CELLS // max(len(between), 1)
        for part in range(CELLS // run):
            for copy in between[part : part + 1]:
                copy.start()
            lax.fori_loop(part * run, part * run + run, step, 0)

    def locate(col, carry):
        wanted = row * NBC + col
        index = 0
        for cell in range(CELLS):
            place = cell % SLOTS
            holder = cell // SLOTS * NBR + lax.rem(row + NBR - place, NBR)
            index = jnp.where(table[place, holder] == wanted, cell, index)
        places[col] = index
        return carry

    def add_a(col, carry):
        part_a[col] = (fwd_a[col].astype(f32) + tiles[DOWN, col].astype(f32)).astype(bf16)
        return carry

    def add_b(col, carry):
        part_b[col] = (fwd_b[col].astype(f32) + tiles[UP, CUT + col].astype(f32)).astype(bf16)
        return carry

    def add_all(col, carry):
        sum_own[col] = (
            tiles[OWN, col].astype(f32) + (from_p[col].astype(f32) + from_m[col].astype(f32))
        ).astype(bf16)
        return carry

    loads[0].start()
    loads[1].start()
    fetch_right.start()
    fetch_left_fac.start()
    fetch_right_fac.start()
    hail(me_x, me_s)
    loads[0].wait()
    unpack(OVER, 0, CUT)
    admitted()
    keep.start()
    copies[0].start()
    for copy in root_copies[0][0][:4]:
        copy.start()
    unpack(OVER, CUT, NBC)
    copies[1].start()
    loads[2].start()
    loads[1].wait()
    unpack(DOWN, 0, NBC)
    copies[2].start()
    loads[3].start()
    loads[2].wait()
    unpack(UP, 0, NBC)
    copies[3].start()
    copies[0].wait_recv()
    lax.fori_loop(0, CUT, add_a, 0)
    copies[4].start()
    copies[1].wait_recv()
    lax.fori_loop(0, NBC - CUT, add_b, 0)
    copies[5].start()
    for copy in root_copies[0][1][:4]:
        copy.start()
    loads[3].wait()
    unpack(OWN, 0, NBC)
    copies[3].wait_recv()
    copies[4].wait_recv()
    lax.fori_loop(0, CUT, add_all, 0)
    copies[6].start()
    copies[9].start()
    copies[2].wait_recv()
    copies[5].wait_recv()
    lax.fori_loop(CUT, NBC, add_all, 0)
    spread(me_x, sum_own, copies[7:9])
    lax.fori_loop(0, NBC, locate, 0)
    copies[6].wait_recv()
    copies[10].start()
    copies[7].wait_recv()
    copies[11].start()
    pass_root(0, 0)
    pass_root(0, 1)
    copies[8].wait_recv()
    spread(down, sum_down, root_copies[0][2][:4])
    copies[9].wait_recv()
    spread(up, sum_up, root_copies[1][0][:4])
    copies[10].wait_recv()
    copies[11].wait_recv()
    spread(over, sum_over, root_copies[1][1][:4] + root_copies[1][2][:4])
    pass_root(0, 2)
    for slot in range(SLOTS):
        pass_root(1, slot)

    fetch_right.wait()
    powers = []
    for slot in range(SLOTS):
        pltpu.make_async_copy(blocks.at[slot], blocks.at[slot], piece_recv.at[slot]).wait()
        grad = blocks[slot].reshape(BLK, BLK)
        precond[slot] = contract_last(grad, right_box[slot]).astype(bf16)
        powers.append(jnp.sum(jnp.square(grad.astype(f32))) / (BLK * BLK))

    def target_of(place, count):
        target_sub = lax.rem(3 * count + 3 * sub + 2 * row, SUBS)
        return target_sub, lax.rem(me_s + place, NBR) * SUBS + target_sub

    def sender(src, dst, send_sem, recv_sem, target):
        away = lambda: pltpu.make_async_remote_copy(
            src_ref=src, dst_ref=dst, send_sem=send_sem, recv_sem=recv_sem,
            device_id=(me_x, target), device_id_type=MESH,
        )
        home = lambda: pltpu.make_async_copy(src, dst, recv_sem)
        return target, away, home

    def back(place, half, count):
        target_sub, target = target_of(place, count)
        return sender(
            raw.at[half, place, target_sub], inbox[half].at[me_s // NBR * SLOTS + place],
            back_send.at[half, place, count], back_recv.at[half], target,
        )

    def tell(place, count):
        target_sub, target = target_of(place, count)
        return sender(
            factors.at[place], factor_box.at[me_s // NBR * SLOTS + place],
            factor_send.at[place, count], factor_recv, target,
        )

    def start_all(describe):
        def step(count, carry):
            target, away, home = describe(count)

            @pl.when(target != me_s)
            def _():
                away().start()

            @pl.when(target == me_s)
            def _():
                home().start()

            return carry

        lax.fori_loop(0, SUBS, step, 0)

    def finish_all(describe):
        def step(count, carry):
            target, away, home = describe(count)

            @pl.when(target != me_s)
            def _():
                away().wait_send()

            return carry

        lax.fori_loop(0, SUBS, step, 0)

    squares = [[] for slot in range(SLOTS)]

    def direct(half, slot):
        for copy in root_copies[half][slot][2:]:
            copy.wait_recv()
        result = jnp.dot(
            roots[slot, :, :, half].reshape(BLK // HALVES, BLK), precond[slot],
            preferred_element_type=f32,
        )
        raw[half, slot] = result.astype(bf16).reshape(SUBS, HROWS, 256)
        start_all(functools.partial(back, slot, half))
        squares[slot].append(jnp.sum(jnp.square(result)))

    shares = []

    def share(slot):
        sums[slot] = jnp.full((8, 128), squares[slot][0] + squares[slot][1], f32)
        for index, x in enumerate((up, down, over)):
            copy = cross(
                sums.at[slot], sum_box.at[slot, index],
                sum_send.at[slot, index], sum_recv.at[slot, index], x,
            )
            copy.start()
            shares.append(copy)

    def graft(slot):
        total = sums[slot] + (sum_box[slot, 0] + sum_box[slot, 1] + sum_box[slot, 2])
        factors[slot] = jnp.sqrt(powers[slot]) / jnp.sqrt(total / (BLK * BLK) + EPSILON)
        start_all(functools.partial(tell, slot))

    def ring(src, dst, group, place, x):
        return cross(src, dst, ring_send.at[group, place], ring_recv.at[group, place], x)

    def links(group):
        mine = gathered.at[me_x, group]
        below, above = gathered.at[down, group, low], gathered.at[up, group, high]
        return [
            ring(mine.at[low], mine.at[low], group, 0, up),
            ring(mine.at[high], mine.at[high], group, 1, down),
            ring(mine.at[high], mine.at[high], group, 2, up),
            ring(mine.at[low], mine.at[low], group, 3, down),
            ring(below, below, group, 4, up),
            ring(above, above, group, 5, down),
        ]

    every = [links(group) for group in range(GROUPS)]

    def statistics(slot):
        whole = blocks[slot].reshape(BLK, BLK)
        scale = jnp.where(table[slot, me_s] >= 0, 1.0 / BLK, 0.0).astype(f32)
        rows = blocks[slot, pl.ds(me_x * 2, 2)].reshape(256, BLK)
        left_box[slot] = left_box[slot] + contract_last(rows, whole) * scale
        start = pl.multiple_of(me_x * 256, 256)
        cols = blocks[slot, :, :, :, pl.ds(start, 256)].reshape(BLK, 256)
        right_fac_box[slot] = (
            right_fac_box[slot] + jnp.dot(cols.T, whole, preferred_element_type=f32) * scale
        )
        for copy in leave(slot):
            copy.start()

    def leave(slot):
        return [
            pltpu.make_async_copy(left_box.at[slot], new_left.at[slot], out_sem.at[slot, 0]),
            pltpu.make_async_copy(right_fac_box.at[slot], new_right.at[slot], out_sem.at[slot, 1]),
        ]

    def forward(group):
        every[group][0].wait_recv()
        every[group][4].start()
        every[group][1].wait_recv()
        every[group][5].start()

    def place_group(group):
        half, first = group // 2, group % 2 * QROWS

        def step(col, carry):
            gathered[me_x, group, col] = inbox[half][places[col], pl.ds(first, QROWS)]
            return carry

        lax.fori_loop(0, NBC, step, 0)

    def ring_group(group):
        for copy in every[group][:4]:
            copy.start()

    def flat_copy(group):
        at = pl.ds(group * size, size)
        return pltpu.make_async_copy(flat.at[group % 2], update.at[:, at], flat_sem.at[group % 2])

    def flatten(group):
        for copy in every[group][2:]:
            copy.wait_recv()
        if group >= 2:
            flat_copy(group - 2).wait()

        def step(col, carry):
            factor = factor_box[places[col]][0:1, :]
            for rows in range(2):
                for part in range(N_X):
                    for lane in range(2):
                        value = gathered[
                            part, group, col, rows * 16 : rows * 16 + 16, lane * 128 : lane * 128 + 128
                        ].astype(f32)
                        mid[rows, pl.ds(part * 2 + lane, 16, STEP), :] = value * factor
            for rows in range(2):
                for line in range(16):
                    at = pl.multiple_of((rows * 16 + line) * COLS + col * BLK, BLK)
                    flat[group % 2, :, pl.ds(at, BLK)] = (
                        mid[rows, line * STEP : line * STEP + 8, :].reshape(1, BLK).astype(bf16)
                    )
            return carry

        lax.fori_loop(0, NBC, step, 0)
        flat_copy(group).start()

    keep.wait()
    for slot in range(SLOTS):
        direct(0, slot)
    pltpu.make_async_copy(inbox_0, inbox_0, back_recv.at[0]).wait()
    place_group(0)
    ring_group(0)
    place_group(1)
    for slot in range(SLOTS):
        direct(1, slot)
    ring_group(1)
    for slot in range(SLOTS):
        share(slot)
    forward(0)
    pltpu.make_async_copy(inbox_1, inbox_1, back_recv.at[1]).wait()
    place_group(2)
    ring_group(2)
    place_group(3)
    ring_group(3)
    for copy in shares:
        copy.wait_recv()
    for slot in range(SLOTS):
        graft(slot)
    forward(1)
    fetch_left_fac.wait()
    fetch_right_fac.wait()
    statistics(0)
    forward(2)
    statistics(1)
    pltpu.make_async_copy(factor_box, factor_box, factor_recv).wait()
    flatten(0)
    flatten(1)
    forward(3)
    statistics(2)
    flatten(2)
    flatten(3)
    flat_copy(2).wait()
    flat_copy(3).wait()
    for group in range(GROUPS):
        for copy in every[group]:
            copy.wait_send()
    for copy in shares + copies:
        copy.wait_send()
    for slot in range(SLOTS):
        for half in range(HALVES):
            for copy in root_copies[half][slot]:
                copy.wait_send()
            finish_all(functools.partial(back, slot, half))
        finish_all(functools.partial(tell, slot))
        for copy in leave(slot):
            copy.wait()

    def sent(index, carry):
        for quarter in range(N_X):
            place, holder, away, home = piece(quarter, index)

            @pl.when(holder != me_s)
            def _():
                away().wait_send()

        return carry

    lax.fori_loop(0, CELLS, sent, 0)


def contract_last(a, b):
    return lax.dot_general(a, b, (((1,), (1,)), ((), ())), preferred_element_type=f32)


def on_device(grads, slot_table, left_factor, right_factor, left_root, right_root):
    smem = pl.BlockSpec(memory_space=pltpu.SMEM)
    hbm = pl.BlockSpec(memory_space=pl.ANY)
    dma = pltpu.SemaphoreType.DMA
    vmem = pltpu.VMEM

    new_left, new_right, update = pl.pallas_call(
        shampoo,
        in_specs=[smem] + [hbm] * 5,
        out_specs=[hbm] * 3,
        out_shape=[
            jax.ShapeDtypeStruct((SLOTS, 256, BLK), f32),
            jax.ShapeDtypeStruct((SLOTS, 256, BLK), f32),
            jax.ShapeDtypeStruct((1, 128 * COLS), bf16),
        ],
        scratch_shapes=[
            vmem((2, 1, QROWS * COLS), bf16),
            vmem((2, 16 * STEP, 128), f32),
            vmem((N_X, NBC, QROWS, BLK), bf16),
            vmem((CUT, QROWS, BLK), bf16),
            vmem((NBC - CUT, QROWS, BLK), bf16),
            vmem((CUT, QROWS, BLK), bf16),
            vmem((NBC - CUT, QROWS, BLK), bf16),
        ]
        + [vmem((NBC, QROWS, BLK), bf16)] * 6
        + [
            vmem((N_X, CELLS, QROWS, BLK), bf16),
            vmem((SLOTS, SUBS, N_X, QROWS, BLK), bf16),
            vmem((SLOTS, N_X, 2, HALVES, HROWS, BLK), bf16),
            vmem((SLOTS, 256, BLK), bf16),
            vmem((SLOTS, BLK, 256), bf16),
            vmem((SLOTS, 8, 128), f32),
            vmem((SLOTS, 3, 8, 128), f32),
            vmem((SLOTS, 8, 128), f32),
            vmem((CELLS, 8, 128), f32),
            vmem((HALVES, SLOTS, SUBS, HROWS, 256), bf16),
            vmem((CELLS, HROWS, 256), bf16),
            vmem((CELLS, HROWS, 256), bf16),
            vmem((N_X, GROUPS, NBC, QROWS, 256), bf16),
            vmem((SLOTS, 256, BLK), f32),
            vmem((SLOTS, 256, BLK), f32),
            pltpu.SMEM((NBC,), jnp.int32),
            dma((2,)),
            dma,
            dma,
            dma((SLOTS, 2)),
            dma((12,)),
            dma((12,)),
            dma((SLOTS, HALVES, 6)),
            dma((SLOTS, HALVES, 6)),
            dma((2,)),
            dma((N_X, CELLS)),
            dma((SLOTS,)),
            dma((SLOTS, 3)),
            dma((SLOTS, 3)),
            dma((SLOTS, SUBS)),
            dma,
            dma((HALVES, SLOTS, SUBS)),
            dma((HALVES,)),
            dma((GROUPS, 6)),
            dma((GROUPS, 6)),
        ],
        compiler_params=pltpu.CompilerParams(
            collective_id=0, has_side_effects=True, vmem_limit_bytes=VMEM_BYTES
        ),
        name="shampoo",
    )(slot_table.T, grads, left_root.reshape(SLOTS, 2, HALVES, HROWS, BLK), right_root[0], left_factor[0], right_factor[0])

    return new_left[None], new_right[None], update


def solution(mesh):
    rows = P("shard", None, "replica", None)
    flat = P("replica", "shard")
    return jax.shard_map(
        on_device,
        mesh=mesh,
        in_specs=(flat, P(), rows, rows, rows, rows),
        out_specs=(rows, rows, flat),
        check_vma=False,
    )
```

```python
import functools

import jax
import jax.numpy as jnp
from jax import lax
from jax.experimental import pallas as pl
from jax.experimental.pallas import tpu as pltpu
from jax.sharding import PartitionSpec as P

ROWS = 4096
COLS = 15360
BLK = 1024
EPSILON = 1e-06

N_X = 4
N_S = 32
SLOTS = 3
NBR = 4
NBC = 15
SUBS = 8
CELLS = 24
QROWS = 32
CUT = 8
GROUPS = 4
MESH = pl.DeviceIdType.MESH
f32 = jnp.float32
bf16 = jnp.bfloat16
VMEM_BYTES = 58 * 1024 * 1024


STEP = 9
HALVES = 2
HROWS = 64
PARTS = 4


def deliver(*refs):
    sources, targets, boxes = refs[:3], refs[3:6], refs[6:9]
    read_sem, write_sem = refs[9:]
    reads, writes = [], []
    for index in range(3):
        for part in range(PARTS):
            if index == 0:
                count = 128 * COLS // PARTS
                at = (slice(None), pl.ds(part * count, count))
            else:
                count = SLOTS * 256 // PARTS
                at = (pl.ds(part * count, count),)
            box = boxes[index].at[at]
            reads.append(pltpu.make_async_copy(sources[index].at[at], box, read_sem.at[index, part]))
            writes.append(pltpu.make_async_copy(box, targets[index].at[at], write_sem.at[index, part]))
    for read in reads:
        read.start()
    for read, write in zip(reads, writes):
        read.wait()
        write.start()
    for write in writes:
        write.wait()


def hail(me_x, me_s):
    barrier = pltpu.get_barrier_semaphore()

    def one(step, carry):
        pl.semaphore_signal(
            barrier, inc=1, device_id=(me_x, lax.rem(me_s + step, N_S)), device_id_type=MESH
        )
        return carry

    lax.fori_loop(1, N_S, one, 0)
    for far in range(1, N_X):
        pl.semaphore_signal(
            barrier, inc=1, device_id=(lax.rem(me_x + far, N_X), me_s), device_id_type=MESH
        )


def admitted():
    pl.semaphore_wait(pltpu.get_barrier_semaphore(), N_S - 1 + N_X - 1)


def shampoo(
    table, grads, left, right, left_fac, right_fac, new_left, new_right, update,
    flat, mid, tiles, fwd_a, fwd_b, part_a, part_b, from_p, from_m,
    sum_own, outbox, blocks, roots, right_box, precond,
    sums, sum_box, factors, factor_box, raw, inbox_0, inbox_1, gathered, left_box, right_fac_box, places,
    flat_sem, right_sem, keep_sem, out_sem, send, recv, root_send, root_recv,
    fac_sem, piece_send, piece_recv, block_send, block_recv, sum_send, sum_recv, factor_send, factor_recv,
    back_send, back_recv, ring_send, ring_recv,
):
    me_x, me_s = lax.axis_index("replica"), lax.axis_index("shard")
    row, sub = me_s // SUBS, lax.rem(me_s, SUBS)
    up, down, over = lax.rem(me_x + 1, N_X), lax.rem(me_x + 3, N_X), lax.rem(me_x + 2, N_X)
    low, high = pl.ds(0, CUT), pl.ds(CUT, NBC - CUT)
    inbox = (inbox_0, inbox_1)
    OVER, DOWN, UP, OWN = range(4)

    def cross(src, dst, send_sem, recv_sem, x):
        return pltpu.make_async_remote_copy(
            src_ref=src, dst_ref=dst, send_sem=send_sem, recv_sem=recv_sem,
            device_id=(x, me_s), device_id_type=MESH,
        )

    def remote(src, dst, place, x):
        return cross(src, dst, send.at[place], recv.at[place], x)

    copies = [
        remote(tiles.at[OVER, low], fwd_a, 0, down),
        remote(tiles.at[OVER, high], fwd_b, 1, up),
        remote(tiles.at[DOWN, high], from_p.at[high], 2, down),
        remote(tiles.at[UP, low], from_m.at[low], 3, up),
        remote(part_a, from_p.at[low], 4, down),
        remote(part_b, from_m.at[high], 5, up),
    ]
    def root(slot, half):
        mine, there = left.at[slot], roots.at[slot, me_x]
        below, above = roots.at[slot, down, 0, half], roots.at[slot, up, 1, half]

        def one(place, src, dst, x):
            return cross(
                src, dst, root_send.at[slot, half, place], root_recv.at[slot, half, place], x
            )

        return [
            one(0, mine.at[0, half], there.at[0, half], up),
            one(1, mine.at[1, half], there.at[1, half], down),
            one(2, mine.at[1, half], there.at[1, half], up),
            one(3, mine.at[0, half], there.at[0, half], down),
            one(4, below, below, up),
            one(5, above, above, down),
        ]

    root_copies = [[root(slot, half) for slot in range(SLOTS)] for half in range(HALVES)]

    def pass_root(half, slot):
        for place in range(2):
            root_copies[half][slot][place].wait_recv()
            root_copies[half][slot][place + 4].start()

    keep = pltpu.make_async_copy(left, roots.at[:, me_x], keep_sem)
    fetch_right = pltpu.make_async_copy(right, right_box, right_sem)
    fetch_left_fac = pltpu.make_async_copy(left_fac, left_box, fac_sem.at[0])
    fetch_right_fac = pltpu.make_async_copy(right_fac, right_fac_box, fac_sem.at[1])
    size = QROWS * COLS
    quarters = (over, down, up, me_x)
    loads = [
        pltpu.make_async_copy(
            grads.at[:, pl.ds(pl.multiple_of(quarters[part] * size, size), size)],
            flat.at[part % 2], flat_sem.at[part % 2],
        )
        for part in range(N_X)
    ]

    def unpack(part, first, last):
        def step(col, carry):
            for half in range(2):
                for line in range(16):
                    at = pl.multiple_of((half * 16 + line) * COLS + col * BLK, BLK)
                    mid[half, line * STEP : line * STEP + 8, :] = (
                        flat[part % 2, :, pl.ds(at, BLK)].astype(f32).reshape(8, 128)
                    )
            for half in range(2):
                for lane in range(8):
                    tiles[part, col, half * 16 : half * 16 + 16, lane * 128 : lane * 128 + 128] = (
                        mid[half, pl.ds(lane, 16, STEP), :].astype(bf16)
                    )
            return carry

        lax.fori_loop(first, last, step, 0)

    def sender(src, dst, send_sem, recv_sem, target):
        away = lambda: pltpu.make_async_remote_copy(
            src_ref=src, dst_ref=dst, send_sem=send_sem, recv_sem=recv_sem,
            device_id=(me_x, target), device_id_type=MESH,
        )
        home = lambda: pltpu.make_async_copy(src, dst, recv_sem)
        return target, away, home

    def piece(place, count):
        holder = lax.rem(count + me_s // NBR, SUBS) * NBR + lax.rem(row + NBR - place, NBR)
        src, dst = outbox.at[place, count], blocks.at[place, sub, me_x]
        target, away, home = sender(
            src, dst, piece_send.at[place, count], piece_recv.at[place], holder
        )
        return target, away, home

    def spread(place):
        def step(count, carry):
            holder, away, home = piece(place, count)
            block = table[place, holder]
            outbox[place, count] = sum_own[lax.rem(jnp.maximum(block, 0), NBC)]

            @pl.when(holder != me_s)
            def _():
                away().start()

            @pl.when(holder == me_s)
            def _():
                home().start()

            return carry

        lax.fori_loop(0, SUBS, step, 0)

    def gather_block(slot):
        first, second = pl.ds(0, 4), pl.ds(4, 4)

        def one(place, subs, x_from, x):
            ref = blocks.at[slot, subs, x_from]
            return cross(ref, ref, block_send.at[slot, place], block_recv.at[slot, place], x)

        return [
            one(0, first, me_x, up),
            one(1, second, me_x, down),
            one(2, second, me_x, up),
            one(3, first, me_x, down),
            one(4, first, down, up),
            one(5, second, up, down),
        ]

    block_copies = [gather_block(slot) for slot in range(SLOTS)]

    def pass_block(slot):
        for place in range(2):
            block_copies[slot][place].wait_recv()
            block_copies[slot][place + 4].start()

    def locate(col, carry):
        wanted = row * NBC + col
        index = 0
        for cell in range(CELLS):
            place = cell % SLOTS
            holder = cell // SLOTS * NBR + lax.rem(row + NBR - place, NBR)
            index = jnp.where(table[place, holder] == wanted, cell, index)
        places[col] = index
        return carry

    def add_a(col, carry):
        part_a[col] = (fwd_a[col].astype(f32) + tiles[DOWN, col].astype(f32)).astype(bf16)
        return carry

    def add_b(col, carry):
        part_b[col] = (fwd_b[col].astype(f32) + tiles[UP, CUT + col].astype(f32)).astype(bf16)
        return carry

    def add_all(col, carry):
        sum_own[col] = (
            tiles[OWN, col].astype(f32) + (from_p[col].astype(f32) + from_m[col].astype(f32))
        ).astype(bf16)
        return carry

    loads[0].start()
    loads[1].start()
    fetch_right.start()
    fetch_left_fac.start()
    fetch_right_fac.start()
    hail(me_x, me_s)
    loads[0].wait()
    unpack(OVER, 0, CUT)
    admitted()
    keep.start()
    copies[0].start()
    for copy in root_copies[0][0][:4]:
        copy.start()
    unpack(OVER, CUT, NBC)
    copies[1].start()
    loads[2].start()
    loads[1].wait()
    unpack(DOWN, 0, NBC)
    copies[2].start()
    loads[3].start()
    loads[2].wait()
    unpack(UP, 0, NBC)
    copies[3].start()
    copies[0].wait_recv()
    lax.fori_loop(0, CUT, add_a, 0)
    copies[4].start()
    copies[1].wait_recv()
    lax.fori_loop(0, NBC - CUT, add_b, 0)
    copies[5].start()
    loads[3].wait()
    unpack(OWN, 0, NBC)
    copies[3].wait_recv()
    copies[4].wait_recv()
    lax.fori_loop(0, CUT, add_all, 0)
    copies[2].wait_recv()
    copies[5].wait_recv()
    lax.fori_loop(CUT, NBC, add_all, 0)
    for slot in range(SLOTS):
        spread(slot)
    for half, slot in ((0, 1), (0, 2), (1, 0), (1, 1)):
        for copy in root_copies[half][slot][:4]:
            copy.start()
    lax.fori_loop(0, NBC, locate, 0)
    pass_root(0, 0)
    for slot in range(SLOTS):
        arrived = blocks.at[slot, :, me_x]
        pltpu.make_async_copy(arrived, arrived, piece_recv.at[slot]).wait()
        for copy in block_copies[slot][:4]:
            copy.start()
    for copy in root_copies[1][2][:4]:
        copy.start()
    pass_root(0, 1)
    pass_root(0, 2)
    for slot in range(SLOTS):
        pass_block(slot)
    for slot in range(SLOTS):
        pass_root(1, slot)

    def target_of(place, count):
        target_sub = lax.rem(3 * count + 3 * sub + 2 * row, SUBS)
        return target_sub, lax.rem(me_s + place, NBR) * SUBS + target_sub

    def back(place, half, count):
        target_sub, target = target_of(place, count)
        return sender(
            raw.at[half, place, target_sub], inbox[half].at[me_s // NBR * SLOTS + place],
            back_send.at[half, place, count], back_recv.at[half], target,
        )

    def tell(place, count):
        target_sub, target = target_of(place, count)
        return sender(
            factors.at[place], factor_box.at[me_s // NBR * SLOTS + place],
            factor_send.at[place, count], factor_recv, target,
        )

    def start_all(describe):
        def step(count, carry):
            target, away, home = describe(count)

            @pl.when(target != me_s)
            def _():
                away().start()

            @pl.when(target == me_s)
            def _():
                home().start()

            return carry

        lax.fori_loop(0, SUBS, step, 0)

    def finish_all(describe):
        def step(count, carry):
            target, away, home = describe(count)

            @pl.when(target != me_s)
            def _():
                away().wait_send()

            return carry

        lax.fori_loop(0, SUBS, step, 0)

    squares = [[] for slot in range(SLOTS)]

    def direct(half, slot):
        for copy in root_copies[half][slot][2:]:
            copy.wait_recv()
        result = jnp.dot(
            roots[slot, :, :, half].reshape(BLK // HALVES, BLK), precond[slot],
            preferred_element_type=f32,
        )
        raw[half, slot] = result.astype(bf16).reshape(SUBS, HROWS, 256)
        start_all(functools.partial(back, slot, half))
        squares[slot].append(jnp.sum(jnp.square(result)))

    shares = []

    def share(slot):
        sums[slot] = jnp.full((8, 128), squares[slot][0] + squares[slot][1], f32)
        for index, x in enumerate((up, down, over)):
            copy = cross(
                sums.at[slot], sum_box.at[slot, index],
                sum_send.at[slot, index], sum_recv.at[slot, index], x,
            )
            copy.start()
            shares.append(copy)

    def graft(slot):
        total = sums[slot] + (sum_box[slot, 0] + sum_box[slot, 1] + sum_box[slot, 2])
        factors[slot] = jnp.sqrt(powers[slot]) / jnp.sqrt(total / (BLK * BLK) + EPSILON)
        start_all(functools.partial(tell, slot))

    def ring(src, dst, group, place, x):
        return cross(src, dst, ring_send.at[group, place], ring_recv.at[group, place], x)

    def links(group):
        mine = gathered.at[me_x, group]
        below, above = gathered.at[down, group, low], gathered.at[up, group, high]
        return [
            ring(mine.at[low], mine.at[low], group, 0, up),
            ring(mine.at[high], mine.at[high], group, 1, down),
            ring(mine.at[high], mine.at[high], group, 2, up),
            ring(mine.at[low], mine.at[low], group, 3, down),
            ring(below, below, group, 4, up),
            ring(above, above, group, 5, down),
        ]

    every = [links(group) for group in range(GROUPS)]

    def statistics(slot):
        whole = blocks[slot].reshape(BLK, BLK)
        scale = jnp.where(table[slot, me_s] >= 0, 1.0 / BLK, 0.0).astype(f32)
        rows = blocks[slot, pl.ds(me_x * 2, 2)].reshape(256, BLK)
        left_box[slot] = left_box[slot] + contract_last(rows, whole) * scale
        start = pl.multiple_of(me_x * 256, 256)
        cols = blocks[slot, :, :, :, pl.ds(start, 256)].reshape(BLK, 256)
        right_fac_box[slot] = (
            right_fac_box[slot] + jnp.dot(cols.T, whole, preferred_element_type=f32) * scale
        )
        for copy in leave(slot):
            copy.start()

    def leave(slot):
        return [
            pltpu.make_async_copy(left_box.at[slot], new_left.at[slot], out_sem.at[slot, 0]),
            pltpu.make_async_copy(right_fac_box.at[slot], new_right.at[slot], out_sem.at[slot, 1]),
        ]

    def forward(group):
        every[group][0].wait_recv()
        every[group][4].start()
        every[group][1].wait_recv()
        every[group][5].start()

    def place_group(group):
        half, first = group // 2, group % 2 * QROWS

        def step(col, carry):
            gathered[me_x, group, col] = inbox[half][places[col], pl.ds(first, QROWS)]
            return carry

        lax.fori_loop(0, NBC, step, 0)

    def ring_group(group):
        for copy in every[group][:4]:
            copy.start()

    def flat_copy(group):
        at = pl.ds(group * size, size)
        return pltpu.make_async_copy(flat.at[group % 2], update.at[:, at], flat_sem.at[group % 2])

    def flatten(group):
        for copy in every[group][2:]:
            copy.wait_recv()
        if group >= 2:
            flat_copy(group - 2).wait()

        def step(col, carry):
            factor = factor_box[places[col]][0:1, :]
            for rows in range(2):
                for part in range(N_X):
                    for lane in range(2):
                        value = gathered[
                            part, group, col, rows * 16 : rows * 16 + 16, lane * 128 : lane * 128 + 128
                        ].astype(f32)
                        mid[rows, pl.ds(part * 2 + lane, 16, STEP), :] = value * factor
            for rows in range(2):
                for line in range(16):
                    at = pl.multiple_of((rows * 16 + line) * COLS + col * BLK, BLK)
                    flat[group % 2, :, pl.ds(at, BLK)] = (
                        mid[rows, line * STEP : line * STEP + 8, :].reshape(1, BLK).astype(bf16)
                    )
            return carry

        lax.fori_loop(0, NBC, step, 0)
        flat_copy(group).start()

    keep.wait()
    fetch_right.wait()
    powers = []
    for slot in range(SLOTS):
        for copy in block_copies[slot][2:]:
            copy.wait_recv()
        grad = blocks[slot].reshape(BLK, BLK)
        precond[slot] = contract_last(grad, right_box[slot]).astype(bf16)
        direct(0, slot)
    pltpu.make_async_copy(inbox_0, inbox_0, back_recv.at[0]).wait()
    place_group(0)
    ring_group(0)
    place_group(1)
    for slot in range(SLOTS):
        direct(1, slot)
    ring_group(1)
    for slot in range(SLOTS):
        share(slot)
    forward(0)
    pltpu.make_async_copy(inbox_1, inbox_1, back_recv.at[1]).wait()
    place_group(2)
    ring_group(2)
    place_group(3)
    ring_group(3)
    for slot in range(SLOTS):
        grad = blocks[slot].reshape(BLK, BLK)
        powers.append(jnp.sum(jnp.square(grad.astype(f32))) / (BLK * BLK))
    for copy in shares:
        copy.wait_recv()
    for slot in range(SLOTS):
        graft(slot)
    forward(1)
    fetch_left_fac.wait()
    fetch_right_fac.wait()
    statistics(0)
    forward(2)
    statistics(1)
    pltpu.make_async_copy(factor_box, factor_box, factor_recv).wait()
    flatten(0)
    flatten(1)
    forward(3)
    statistics(2)
    flatten(2)
    flatten(3)
    flat_copy(2).wait()
    flat_copy(3).wait()
    for group in range(GROUPS):
        for copy in every[group]:
            copy.wait_send()
    for copy in shares + copies:
        copy.wait_send()
    for slot in range(SLOTS):
        for half in range(HALVES):
            for copy in root_copies[half][slot]:
                copy.wait_send()
            finish_all(functools.partial(back, slot, half))
        finish_all(functools.partial(tell, slot))
        finish_all(functools.partial(piece, slot))
        for copy in block_copies[slot]:
            copy.wait_send()
        for copy in leave(slot):
            copy.wait()


def contract_last(a, b):
    return lax.dot_general(a, b, (((1,), (1,)), ((), ())), preferred_element_type=f32)


def on_device(grads, slot_table, left_factor, right_factor, left_root, right_root):
    smem = pl.BlockSpec(memory_space=pltpu.SMEM)
    hbm = pl.BlockSpec(memory_space=pl.ANY)
    dma = pltpu.SemaphoreType.DMA
    vmem = pltpu.VMEM

    new_left, new_right, update = pl.pallas_call(
        shampoo,
        in_specs=[smem] + [hbm] * 5,
        out_specs=[hbm] * 3,
        out_shape=[
            jax.ShapeDtypeStruct((SLOTS, 256, BLK), f32),
            jax.ShapeDtypeStruct((SLOTS, 256, BLK), f32),
            jax.ShapeDtypeStruct((1, 128 * COLS), bf16),
        ],
        scratch_shapes=[
            vmem((2, 1, QROWS * COLS), bf16),
            vmem((2, 16 * STEP, 128), f32),
            vmem((N_X, NBC, QROWS, BLK), bf16),
            vmem((CUT, QROWS, BLK), bf16),
            vmem((NBC - CUT, QROWS, BLK), bf16),
            vmem((CUT, QROWS, BLK), bf16),
            vmem((NBC - CUT, QROWS, BLK), bf16),
        ]
        + [vmem((NBC, QROWS, BLK), bf16)] * 3
        + [
            vmem((SLOTS, SUBS, QROWS, BLK), bf16),
            vmem((SLOTS, SUBS, N_X, QROWS, BLK), bf16),
            vmem((SLOTS, N_X, 2, HALVES, HROWS, BLK), bf16),
            vmem((SLOTS, 256, BLK), bf16),
            vmem((SLOTS, BLK, 256), bf16),
            vmem((SLOTS, 8, 128), f32),
            vmem((SLOTS, 3, 8, 128), f32),
            vmem((SLOTS, 8, 128), f32),
            vmem((CELLS, 8, 128), f32),
            vmem((HALVES, SLOTS, SUBS, HROWS, 256), bf16),
            vmem((CELLS, HROWS, 256), bf16),
            vmem((CELLS, HROWS, 256), bf16),
            vmem((N_X, GROUPS, NBC, QROWS, 256), bf16),
            vmem((SLOTS, 256, BLK), f32),
            vmem((SLOTS, 256, BLK), f32),
            pltpu.SMEM((NBC,), jnp.int32),
            dma((2,)),
            dma,
            dma,
            dma((SLOTS, 2)),
            dma((6,)),
            dma((6,)),
            dma((SLOTS, HALVES, 6)),
            dma((SLOTS, HALVES, 6)),
            dma((2,)),
            dma((SLOTS, SUBS)),
            dma((SLOTS,)),
            dma((SLOTS, 6)),
            dma((SLOTS, 6)),
            dma((SLOTS, 3)),
            dma((SLOTS, 3)),
            dma((SLOTS, SUBS)),
            dma,
            dma((HALVES, SLOTS, SUBS)),
            dma((HALVES,)),
            dma((GROUPS, 6)),
            dma((GROUPS, 6)),
        ],
        compiler_params=pltpu.CompilerParams(
            collective_id=0, has_side_effects=True, vmem_limit_bytes=VMEM_BYTES
        ),
        name="shampoo",
    )(slot_table.T, grads, left_root.reshape(SLOTS, 2, HALVES, HROWS, BLK), right_root[0], left_factor[0], right_factor[0])

    shapes = [
        jax.ShapeDtypeStruct((1, 128 * COLS), bf16),
        jax.ShapeDtypeStruct((SLOTS * 256, BLK), f32),
        jax.ShapeDtypeStruct((SLOTS * 256, BLK), f32),
    ]
    flat, new_left, new_right = pl.pallas_call(
        deliver,
        in_specs=[hbm] * 3,
        out_specs=[hbm] * 3,
        out_shape=shapes,
        scratch_shapes=[vmem(shape.shape, shape.dtype) for shape in shapes] + [dma((3, PARTS))] * 2,
        compiler_params=pltpu.CompilerParams(vmem_limit_bytes=VMEM_BYTES),
        name="deliver",
    )(update, new_left.reshape(SLOTS * 256, BLK), new_right.reshape(SLOTS * 256, BLK))
    rows = (1, SLOTS, 256, BLK)
    return new_left.reshape(rows), new_right.reshape(rows), flat


def solution(mesh):
    rows = P("shard", None, "replica", None)
    flat = P("replica", "shard")
    return jax.shard_map(
        on_device,
        mesh=mesh,
        in_specs=(flat, P(), rows, rows, rows, rows),
        out_specs=(rows, rows, flat),
        check_vma=False,
    )
```

```python
import functools

import jax
import jax.numpy as jnp
from jax import lax
from jax.experimental import pallas as pl
from jax.experimental.pallas import tpu as pltpu
from jax.sharding import PartitionSpec as P

ROWS = 4096
COLS = 15360
BLK = 1024
EPSILON = 1e-06

N_X = 4
N_S = 32
SLOTS = 3
NBR = 4
NBC = 15
SUBS = 8
CELLS = 24
QROWS = 32
CUT = 8
GROUPS = 4
MESH = pl.DeviceIdType.MESH
f32 = jnp.float32
bf16 = jnp.bfloat16
VMEM_BYTES = 58 * 1024 * 1024


STEP = 9
HALVES = 2
HROWS = 64
PARTS = 4


def deliver(*refs):
    sources, targets, boxes = refs[:3], refs[3:6], refs[6:9]
    read_sem, write_sem = refs[9:]
    reads, writes = [], []
    for index in range(3):
        for part in range(PARTS):
            if index == 0:
                count = 128 * COLS // PARTS
                at = (slice(None), pl.ds(part * count, count))
            else:
                count = SLOTS * 256 // PARTS
                at = (pl.ds(part * count, count),)
            box = boxes[index].at[at]
            reads.append(pltpu.make_async_copy(sources[index].at[at], box, read_sem.at[index, part]))
            writes.append(pltpu.make_async_copy(box, targets[index].at[at], write_sem.at[index, part]))
    for read in reads:
        read.start()
    for read, write in zip(reads, writes):
        read.wait()
        write.start()
    for write in writes:
        write.wait()


def hail(me_x, me_s):
    barrier = pltpu.get_barrier_semaphore()

    def one(step, carry):
        pl.semaphore_signal(
            barrier, inc=1, device_id=(me_x, lax.rem(me_s + step, N_S)), device_id_type=MESH
        )
        return carry

    lax.fori_loop(1, N_S, one, 0)
    for far in range(1, N_X):
        pl.semaphore_signal(
            barrier, inc=1, device_id=(lax.rem(me_x + far, N_X), me_s), device_id_type=MESH
        )


def admitted():
    pl.semaphore_wait(pltpu.get_barrier_semaphore(), N_S - 1 + N_X - 1)


def shampoo(
    table, grads, left, right, left_fac, right_fac, new_left, new_right, update,
    flat, mid, tiles, fwd_a, fwd_b, part_a, part_b, from_p, from_m,
    sum_own, sum_down, sum_up, outbox, blocks, roots, right_box, precond,
    sums, sum_box, factors, factor_box, raw, inbox_0, inbox_1, gathered, left_box, right_fac_box, places,
    flat_sem, right_sem, keep_sem, out_sem, send, recv, root_send, root_recv,
    fac_sem, piece_send, piece_recv, block_send, block_recv, sum_send, sum_recv, factor_send, factor_recv,
    back_send, back_recv, ring_send, ring_recv,
):
    me_x, me_s = lax.axis_index("replica"), lax.axis_index("shard")
    row, sub = me_s // SUBS, lax.rem(me_s, SUBS)
    up, down, over = lax.rem(me_x + 1, N_X), lax.rem(me_x + 3, N_X), lax.rem(me_x + 2, N_X)
    low, high = pl.ds(0, CUT), pl.ds(CUT, NBC - CUT)
    inbox = (inbox_0, inbox_1)
    OVER, DOWN, UP, OWN = range(4)

    def cross(src, dst, send_sem, recv_sem, x):
        return pltpu.make_async_remote_copy(
            src_ref=src, dst_ref=dst, send_sem=send_sem, recv_sem=recv_sem,
            device_id=(x, me_s), device_id_type=MESH,
        )

    def remote(src, dst, place, x):
        return cross(src, dst, send.at[place], recv.at[place], x)

    copies = [
        remote(tiles.at[OVER, low], fwd_a, 0, down),
        remote(tiles.at[OVER, high], fwd_b, 1, up),
        remote(tiles.at[DOWN, high], from_p.at[high], 2, down),
        remote(tiles.at[UP, low], from_m.at[low], 3, up),
        remote(part_a, from_p.at[low], 4, down),
        remote(part_b, from_m.at[high], 5, up),
        remote(sum_own.at[low], sum_down.at[low], 6, up),
        remote(sum_own.at[high], sum_up.at[high], 7, down),
        remote(sum_own.at[high], sum_down.at[high], 8, up),
        remote(sum_own.at[low], sum_up.at[low], 9, down),
    ]
    def root(slot, half):
        mine, there = left.at[slot], roots.at[slot, me_x]
        below, above = roots.at[slot, down, 0, half], roots.at[slot, up, 1, half]

        def one(place, src, dst, x):
            return cross(
                src, dst, root_send.at[slot, half, place], root_recv.at[slot, half, place], x
            )

        return [
            one(0, mine.at[0, half], there.at[0, half], up),
            one(1, mine.at[1, half], there.at[1, half], down),
            one(2, mine.at[1, half], there.at[1, half], up),
            one(3, mine.at[0, half], there.at[0, half], down),
            one(4, below, below, up),
            one(5, above, above, down),
        ]

    root_copies = [[root(slot, half) for slot in range(SLOTS)] for half in range(HALVES)]

    def start_root(half, slot):
        for copy in root_copies[half][slot][:4]:
            copy.start()

    def pass_root(half, slot):
        for place in range(2):
            root_copies[half][slot][place].wait_recv()
            root_copies[half][slot][place + 4].start()

    keep = pltpu.make_async_copy(left, roots.at[:, me_x], keep_sem)
    fetch_right = pltpu.make_async_copy(right, right_box, right_sem)
    fetch_left_fac = pltpu.make_async_copy(left_fac, left_box, fac_sem.at[0])
    fetch_right_fac = pltpu.make_async_copy(right_fac, right_fac_box, fac_sem.at[1])
    size = QROWS * COLS
    quarters = (over, down, up, me_x)
    loads = [
        pltpu.make_async_copy(
            grads.at[:, pl.ds(pl.multiple_of(quarters[part] * size, size), size)],
            flat.at[part % 2], flat_sem.at[part % 2],
        )
        for part in range(N_X)
    ]

    def unpack(part, first, last):
        def step(col, carry):
            for half in range(2):
                for line in range(16):
                    at = pl.multiple_of((half * 16 + line) * COLS + col * BLK, BLK)
                    mid[half, line * STEP : line * STEP + 8, :] = (
                        flat[part % 2, :, pl.ds(at, BLK)].astype(f32).reshape(8, 128)
                    )
            for half in range(2):
                for lane in range(8):
                    tiles[part, col, half * 16 : half * 16 + 16, lane * 128 : lane * 128 + 128] = (
                        mid[half, pl.ds(lane, 16, STEP), :].astype(bf16)
                    )
            return carry

        lax.fori_loop(first, last, step, 0)

    def sender(src, dst, send_sem, recv_sem, target):
        away = lambda: pltpu.make_async_remote_copy(
            src_ref=src, dst_ref=dst, send_sem=send_sem, recv_sem=recv_sem,
            device_id=(me_x, target), device_id_type=MESH,
        )
        home = lambda: pltpu.make_async_copy(src, dst, recv_sem)
        return target, away, home

    sums_of = (sum_own, sum_down, sum_up)
    from_of = (me_x, down, up)

    def piece(origin, place, count):
        holder = lax.rem(count + me_s // NBR, SUBS) * NBR + lax.rem(row + NBR - place, NBR)
        src, dst = outbox.at[origin, place, count], blocks.at[place, sub, from_of[origin]]
        return sender(
            src, dst, piece_send.at[origin, place, count], piece_recv.at[origin, place], holder
        )

    def spread(origin):
        for place in range(SLOTS):

            def step(count, carry):
                holder, away, home = piece(origin, place, count)
                block = table[place, holder]
                outbox[origin, place, count] = sums_of[origin][lax.rem(jnp.maximum(block, 0), NBC)]

                @pl.when(holder != me_s)
                def _():
                    away().start()

                @pl.when(holder == me_s)
                def _():
                    home().start()

                return carry

            lax.fori_loop(0, SUBS, step, 0)

    def gather_block(slot):
        def one(place, subs, x_from, x):
            ref = blocks.at[slot, subs, x_from]
            return cross(ref, ref, block_send.at[slot, place], block_recv.at[slot, place], x)

        return [one(0, pl.ds(0, 4), down, up), one(1, pl.ds(4, 4), up, down)]

    block_copies = [gather_block(slot) for slot in range(SLOTS)]

    def arrive(origin, slot):
        pieces = blocks.at[slot, :, from_of[origin]]
        pltpu.make_async_copy(pieces, pieces, piece_recv.at[origin, slot]).wait()

    def locate(col, carry):
        wanted = row * NBC + col
        index = 0
        for cell in range(CELLS):
            place = cell % SLOTS
            holder = cell // SLOTS * NBR + lax.rem(row + NBR - place, NBR)
            index = jnp.where(table[place, holder] == wanted, cell, index)
        places[col] = index
        return carry

    def add_a(col, carry):
        part_a[col] = (fwd_a[col].astype(f32) + tiles[DOWN, col].astype(f32)).astype(bf16)
        return carry

    def add_b(col, carry):
        part_b[col] = (fwd_b[col].astype(f32) + tiles[UP, CUT + col].astype(f32)).astype(bf16)
        return carry

    def add_all(col, carry):
        sum_own[col] = (
            tiles[OWN, col].astype(f32) + (from_p[col].astype(f32) + from_m[col].astype(f32))
        ).astype(bf16)
        return carry

    loads[0].start()
    loads[1].start()
    fetch_right.start()
    fetch_left_fac.start()
    fetch_right_fac.start()
    hail(me_x, me_s)
    loads[0].wait()
    unpack(OVER, 0, CUT)
    admitted()
    keep.start()
    copies[0].start()
    start_root(0, 0)
    unpack(OVER, CUT, NBC)
    copies[1].start()
    loads[2].start()
    loads[1].wait()
    unpack(DOWN, 0, NBC)
    copies[2].start()
    loads[3].start()
    loads[2].wait()
    unpack(UP, 0, NBC)
    copies[3].start()
    copies[0].wait_recv()
    lax.fori_loop(0, CUT, add_a, 0)
    copies[4].start()
    copies[1].wait_recv()
    lax.fori_loop(0, NBC - CUT, add_b, 0)
    copies[5].start()
    loads[3].wait()
    unpack(OWN, 0, NBC)
    copies[3].wait_recv()
    copies[4].wait_recv()
    lax.fori_loop(0, CUT, add_all, 0)
    copies[6].start()
    copies[9].start()
    copies[2].wait_recv()
    copies[5].wait_recv()
    lax.fori_loop(CUT, NBC, add_all, 0)
    copies[7].start()
    copies[8].start()
    spread(0)
    start_root(0, 1)
    start_root(0, 2)
    lax.fori_loop(0, NBC, locate, 0)
    pass_root(0, 0)
    copies[6].wait_recv()
    copies[8].wait_recv()
    spread(1)
    start_root(1, 0)
    copies[7].wait_recv()
    copies[9].wait_recv()
    spread(2)
    start_root(1, 1)
    pass_root(0, 1)
    pass_root(0, 2)
    start_root(1, 2)
    for slot in range(SLOTS):
        arrive(1, slot)
        block_copies[slot][0].start()
        arrive(2, slot)
        block_copies[slot][1].start()
    for slot in range(SLOTS):
        pass_root(1, slot)

    def target_of(place, count):
        target_sub = lax.rem(3 * count + 3 * sub + 2 * row, SUBS)
        return target_sub, lax.rem(me_s + place, NBR) * SUBS + target_sub

    def back(place, half, count):
        target_sub, target = target_of(place, count)
        return sender(
            raw.at[half, place, target_sub], inbox[half].at[me_s // NBR * SLOTS + place],
            back_send.at[half, place, count], back_recv.at[half], target,
        )

    def tell(place, count):
        target_sub, target = target_of(place, count)
        return sender(
            factors.at[place], factor_box.at[me_s // NBR * SLOTS + place],
            factor_send.at[place, count], factor_recv, target,
        )

    def start_all(describe):
        def step(count, carry):
            target, away, home = describe(count)

            @pl.when(target != me_s)
            def _():
                away().start()

            @pl.when(target == me_s)
            def _():
                home().start()

            return carry

        lax.fori_loop(0, SUBS, step, 0)

    def finish_all(describe):
        def step(count, carry):
            target, away, home = describe(count)

            @pl.when(target != me_s)
            def _():
                away().wait_send()

            return carry

        lax.fori_loop(0, SUBS, step, 0)

    squares = [[] for slot in range(SLOTS)]

    def direct(half, slot):
        for copy in root_copies[half][slot][2:]:
            copy.wait_recv()
        result = jnp.dot(
            roots[slot, :, :, half].reshape(BLK // HALVES, BLK), precond[slot],
            preferred_element_type=f32,
        )
        raw[half, slot] = result.astype(bf16).reshape(SUBS, HROWS, 256)
        start_all(functools.partial(back, slot, half))
        squares[slot].append(jnp.sum(jnp.square(result)))

    shares = []

    def share(slot):
        sums[slot] = jnp.full((8, 128), squares[slot][0] + squares[slot][1], f32)
        for index, x in enumerate((up, down, over)):
            copy = cross(
                sums.at[slot], sum_box.at[slot, index],
                sum_send.at[slot, index], sum_recv.at[slot, index], x,
            )
            copy.start()
            shares.append(copy)

    def graft(slot):
        total = sums[slot] + (sum_box[slot, 0] + sum_box[slot, 1] + sum_box[slot, 2])
        factors[slot] = jnp.sqrt(powers[slot]) / jnp.sqrt(total / (BLK * BLK) + EPSILON)
        start_all(functools.partial(tell, slot))

    def ring(src, dst, group, place, x):
        return cross(src, dst, ring_send.at[group, place], ring_recv.at[group, place], x)

    def links(group):
        mine = gathered.at[me_x, group]
        below, above = gathered.at[down, group, low], gathered.at[up, group, high]
        return [
            ring(mine.at[low], mine.at[low], group, 0, up),
            ring(mine.at[high], mine.at[high], group, 1, down),
            ring(mine.at[high], mine.at[high], group, 2, up),
            ring(mine.at[low], mine.at[low], group, 3, down),
            ring(below, below, group, 4, up),
            ring(above, above, group, 5, down),
        ]

    every = [links(group) for group in range(GROUPS)]

    def statistics(slot):
        whole = blocks[slot].reshape(BLK, BLK)
        scale = jnp.where(table[slot, me_s] >= 0, 1.0 / BLK, 0.0).astype(f32)
        rows = blocks[slot, pl.ds(me_x * 2, 2)].reshape(256, BLK)
        left_box[slot] = left_box[slot] + contract_last(rows, whole) * scale
        start = pl.multiple_of(me_x * 256, 256)
        cols = blocks[slot, :, :, :, pl.ds(start, 256)].reshape(BLK, 256)
        right_fac_box[slot] = (
            right_fac_box[slot] + jnp.dot(cols.T, whole, preferred_element_type=f32) * scale
        )
        for copy in leave(slot):
            copy.start()

    def leave(slot):
        return [
            pltpu.make_async_copy(left_box.at[slot], new_left.at[slot], out_sem.at[slot, 0]),
            pltpu.make_async_copy(right_fac_box.at[slot], new_right.at[slot], out_sem.at[slot, 1]),
        ]

    def forward(group):
        every[group][0].wait_recv()
        every[group][4].start()
        every[group][1].wait_recv()
        every[group][5].start()

    def place_group(group):
        half, first = group // 2, group % 2 * QROWS

        def step(col, carry):
            gathered[me_x, group, col] = inbox[half][places[col], pl.ds(first, QROWS)]
            return carry

        lax.fori_loop(0, NBC, step, 0)

    def ring_group(group):
        for copy in every[group][:4]:
            copy.start()

    def flat_copy(group):
        at = pl.ds(group * size, size)
        return pltpu.make_async_copy(flat.at[group % 2], update.at[:, at], flat_sem.at[group % 2])

    def flatten(group):
        for copy in every[group][2:]:
            copy.wait_recv()
        if group >= 2:
            flat_copy(group - 2).wait()

        def step(col, carry):
            factor = factor_box[places[col]][0:1, :]
            for rows in range(2):
                for part in range(N_X):
                    for lane in range(2):
                        value = gathered[
                            part, group, col, rows * 16 : rows * 16 + 16, lane * 128 : lane * 128 + 128
                        ].astype(f32)
                        mid[rows, pl.ds(part * 2 + lane, 16, STEP), :] = value * factor
            for rows in range(2):
                for line in range(16):
                    at = pl.multiple_of((rows * 16 + line) * COLS + col * BLK, BLK)
                    flat[group % 2, :, pl.ds(at, BLK)] = (
                        mid[rows, line * STEP : line * STEP + 8, :].reshape(1, BLK).astype(bf16)
                    )
            return carry

        lax.fori_loop(0, NBC, step, 0)
        flat_copy(group).start()

    keep.wait()
    fetch_right.wait()
    powers = []
    for slot in range(SLOTS):
        arrive(0, slot)
        for copy in block_copies[slot]:
            copy.wait_recv()
        grad = blocks[slot].reshape(BLK, BLK)
        precond[slot] = contract_last(grad, right_box[slot]).astype(bf16)
        direct(0, slot)
    pltpu.make_async_copy(inbox_0, inbox_0, back_recv.at[0]).wait()
    place_group(0)
    ring_group(0)
    place_group(1)
    for slot in range(SLOTS):
        direct(1, slot)
    ring_group(1)
    for slot in range(SLOTS):
        share(slot)
    forward(0)
    pltpu.make_async_copy(inbox_1, inbox_1, back_recv.at[1]).wait()
    place_group(2)
    ring_group(2)
    place_group(3)
    ring_group(3)
    for slot in range(SLOTS):
        grad = blocks[slot].reshape(BLK, BLK)
        powers.append(jnp.sum(jnp.square(grad.astype(f32))) / (BLK * BLK))
    for copy in shares:
        copy.wait_recv()
    for slot in range(SLOTS):
        graft(slot)
    forward(1)
    fetch_left_fac.wait()
    fetch_right_fac.wait()
    statistics(0)
    forward(2)
    statistics(1)
    pltpu.make_async_copy(factor_box, factor_box, factor_recv).wait()
    flatten(0)
    flatten(1)
    forward(3)
    statistics(2)
    flatten(2)
    flatten(3)
    flat_copy(2).wait()
    flat_copy(3).wait()
    for group in range(GROUPS):
        for copy in every[group]:
            copy.wait_send()
    for copy in shares + copies:
        copy.wait_send()
    for slot in range(SLOTS):
        for half in range(HALVES):
            for copy in root_copies[half][slot]:
                copy.wait_send()
            finish_all(functools.partial(back, slot, half))
        finish_all(functools.partial(tell, slot))
        for origin in range(3):
            finish_all(functools.partial(piece, origin, slot))
        for copy in block_copies[slot]:
            copy.wait_send()
        for copy in leave(slot):
            copy.wait()


def contract_last(a, b):
    return lax.dot_general(a, b, (((1,), (1,)), ((), ())), preferred_element_type=f32)


def on_device(grads, slot_table, left_factor, right_factor, left_root, right_root):
    smem = pl.BlockSpec(memory_space=pltpu.SMEM)
    hbm = pl.BlockSpec(memory_space=pl.ANY)
    dma = pltpu.SemaphoreType.DMA
    vmem = pltpu.VMEM

    new_left, new_right, update = pl.pallas_call(
        shampoo,
        in_specs=[smem] + [hbm] * 5,
        out_specs=[hbm] * 3,
        out_shape=[
            jax.ShapeDtypeStruct((SLOTS, 256, BLK), f32),
            jax.ShapeDtypeStruct((SLOTS, 256, BLK), f32),
            jax.ShapeDtypeStruct((1, 128 * COLS), bf16),
        ],
        scratch_shapes=[
            vmem((2, 1, QROWS * COLS), bf16),
            vmem((2, 16 * STEP, 128), f32),
            vmem((N_X, NBC, QROWS, BLK), bf16),
            vmem((CUT, QROWS, BLK), bf16),
            vmem((NBC - CUT, QROWS, BLK), bf16),
            vmem((CUT, QROWS, BLK), bf16),
            vmem((NBC - CUT, QROWS, BLK), bf16),
        ]
        + [vmem((NBC, QROWS, BLK), bf16)] * 5
        + [
            vmem((3, SLOTS, SUBS, QROWS, BLK), bf16),
            vmem((SLOTS, SUBS, N_X, QROWS, BLK), bf16),
            vmem((SLOTS, N_X, 2, HALVES, HROWS, BLK), bf16),
            vmem((SLOTS, 256, BLK), bf16),
            vmem((SLOTS, BLK, 256), bf16),
            vmem((SLOTS, 8, 128), f32),
            vmem((SLOTS, 3, 8, 128), f32),
            vmem((SLOTS, 8, 128), f32),
            vmem((CELLS, 8, 128), f32),
            vmem((HALVES, SLOTS, SUBS, HROWS, 256), bf16),
            vmem((CELLS, HROWS, 256), bf16),
            vmem((CELLS, HROWS, 256), bf16),
            vmem((N_X, GROUPS, NBC, QROWS, 256), bf16),
            vmem((SLOTS, 256, BLK), f32),
            vmem((SLOTS, 256, BLK), f32),
            pltpu.SMEM((NBC,), jnp.int32),
            dma((2,)),
            dma,
            dma,
            dma((SLOTS, 2)),
            dma((10,)),
            dma((10,)),
            dma((SLOTS, HALVES, 6)),
            dma((SLOTS, HALVES, 6)),
            dma((2,)),
            dma((3, SLOTS, SUBS)),
            dma((3, SLOTS)),
            dma((SLOTS, 2)),
            dma((SLOTS, 2)),
            dma((SLOTS, 3)),
            dma((SLOTS, 3)),
            dma((SLOTS, SUBS)),
            dma,
            dma((HALVES, SLOTS, SUBS)),
            dma((HALVES,)),
            dma((GROUPS, 6)),
            dma((GROUPS, 6)),
        ],
        compiler_params=pltpu.CompilerParams(
            collective_id=0, has_side_effects=True, vmem_limit_bytes=VMEM_BYTES
        ),
        name="shampoo",
    )(slot_table.T, grads, left_root.reshape(SLOTS, 2, HALVES, HROWS, BLK), right_root[0], left_factor[0], right_factor[0])

    shapes = [
        jax.ShapeDtypeStruct((1, 128 * COLS), bf16),
        jax.ShapeDtypeStruct((SLOTS * 256, BLK), f32),
        jax.ShapeDtypeStruct((SLOTS * 256, BLK), f32),
    ]
    flat, new_left, new_right = pl.pallas_call(
        deliver,
        in_specs=[hbm] * 3,
        out_specs=[hbm] * 3,
        out_shape=shapes,
        scratch_shapes=[vmem(shape.shape, shape.dtype) for shape in shapes] + [dma((3, PARTS))] * 2,
        compiler_params=pltpu.CompilerParams(vmem_limit_bytes=VMEM_BYTES),
        name="deliver",
    )(update, new_left.reshape(SLOTS * 256, BLK), new_right.reshape(SLOTS * 256, BLK))
    rows = (1, SLOTS, 256, BLK)
    return new_left.reshape(rows), new_right.reshape(rows), flat


def solution(mesh):
    rows = P("shard", None, "replica", None)
    flat = P("replica", "shard")
    return jax.shard_map(
        on_device,
        mesh=mesh,
        in_specs=(flat, P(), rows, rows, rows, rows),
        out_specs=(rows, rows, flat),
        check_vma=False,
    )
```

```python
import functools

import jax
import jax.numpy as jnp
from jax import lax
from jax.experimental import pallas as pl
from jax.experimental.pallas import tpu as pltpu
from jax.sharding import PartitionSpec as P

ROWS = 4096
COLS = 15360
BLK = 1024
EPSILON = 1e-06

N_X = 4
N_S = 32
SLOTS = 3
NBR = 4
NBC = 15
SUBS = 8
CELLS = 24
QROWS = 32
CUT = 8
GROUPS = 4
MESH = pl.DeviceIdType.MESH
f32 = jnp.float32
bf16 = jnp.bfloat16
VMEM_BYTES = 58 * 1024 * 1024


STEP = 9
HALVES = 2
HROWS = 64
PARTS = 4


def deliver(*refs):
    sources, targets, boxes = refs[:3], refs[3:6], refs[6:9]
    read_sem, write_sem = refs[9:]
    reads, writes = [], []
    for index in range(3):
        for part in range(PARTS):
            if index == 0:
                count = 128 * COLS // PARTS
                at = (slice(None), pl.ds(part * count, count))
            else:
                count = SLOTS * 256 // PARTS
                at = (pl.ds(part * count, count),)
            box = boxes[index].at[at]
            reads.append(pltpu.make_async_copy(sources[index].at[at], box, read_sem.at[index, part]))
            writes.append(pltpu.make_async_copy(box, targets[index].at[at], write_sem.at[index, part]))
    for read in reads:
        read.start()
    for read, write in zip(reads, writes):
        read.wait()
        write.start()
    for write in writes:
        write.wait()


def hail(me_x, me_s):
    barrier = pltpu.get_barrier_semaphore()

    def one(step, carry):
        pl.semaphore_signal(
            barrier, inc=1, device_id=(me_x, lax.rem(me_s + step, N_S)), device_id_type=MESH
        )
        return carry

    lax.fori_loop(1, N_S, one, 0)
    for far in range(1, N_X):
        pl.semaphore_signal(
            barrier, inc=1, device_id=(lax.rem(me_x + far, N_X), me_s), device_id_type=MESH
        )


def admitted():
    pl.semaphore_wait(pltpu.get_barrier_semaphore(), N_S - 1 + N_X - 1)


def shampoo(
    table, grads, left, right, left_fac, right_fac, new_left, new_right, update,
    flat, mid, tiles, fwd_a, fwd_b, part_a, part_b, from_p, from_m,
    sum_own, sum_down, sum_up, outbox, blocks, roots, right_box, precond,
    sums, sum_box, factors, factor_box, raw, inbox_0, inbox_1, gathered, left_box, right_fac_box, places,
    flat_sem, right_sem, keep_sem, out_sem, send, recv, root_send, root_recv,
    fac_sem, piece_send, piece_recv, block_send, block_recv, sum_send, sum_recv, factor_send, factor_recv,
    back_send, back_recv, ring_send, ring_recv,
):
    me_x, me_s = lax.axis_index("replica"), lax.axis_index("shard")
    row, sub = me_s // SUBS, lax.rem(me_s, SUBS)
    up, down, over = lax.rem(me_x + 1, N_X), lax.rem(me_x + 3, N_X), lax.rem(me_x + 2, N_X)
    low, high = pl.ds(0, CUT), pl.ds(CUT, NBC - CUT)
    inbox = (inbox_0, inbox_1)
    OVER, DOWN, UP, OWN = range(4)

    def cross(src, dst, send_sem, recv_sem, x):
        return pltpu.make_async_remote_copy(
            src_ref=src, dst_ref=dst, send_sem=send_sem, recv_sem=recv_sem,
            device_id=(x, me_s), device_id_type=MESH,
        )

    def remote(src, dst, place, x):
        return cross(src, dst, send.at[place], recv.at[place], x)

    copies = [
        remote(tiles.at[OVER, low], fwd_a, 0, down),
        remote(tiles.at[OVER, high], fwd_b, 1, up),
        remote(tiles.at[DOWN, high], from_p.at[high], 2, down),
        remote(tiles.at[UP, low], from_m.at[low], 3, up),
        remote(part_a, from_p.at[low], 4, down),
        remote(part_b, from_m.at[high], 5, up),
        remote(sum_own.at[low], sum_down.at[low], 6, up),
        remote(sum_own.at[high], sum_up.at[high], 7, down),
        remote(sum_own.at[high], sum_down.at[high], 8, up),
        remote(sum_own.at[low], sum_up.at[low], 9, down),
    ]
    def root(slot, half):
        mine, there = left.at[slot], roots.at[slot, me_x]
        below, above = roots.at[slot, down, 0, half], roots.at[slot, up, 1, half]

        def one(place, src, dst, x):
            return cross(
                src, dst, root_send.at[slot, half, place], root_recv.at[slot, half, place], x
            )

        return [
            one(0, mine.at[0, half], there.at[0, half], up),
            one(1, mine.at[1, half], there.at[1, half], down),
            one(2, mine.at[1, half], there.at[1, half], up),
            one(3, mine.at[0, half], there.at[0, half], down),
            one(4, below, below, up),
            one(5, above, above, down),
        ]

    root_copies = [[root(slot, half) for slot in range(SLOTS)] for half in range(HALVES)]

    def start_root(half, slot):
        for copy in root_copies[half][slot][:4]:
            copy.start()

    def pass_root(half, slot):
        for place in range(2):
            root_copies[half][slot][place].wait_recv()
            root_copies[half][slot][place + 4].start()

    keep = pltpu.make_async_copy(left, roots.at[:, me_x], keep_sem)
    fetch_right = pltpu.make_async_copy(right, right_box, right_sem)
    fetch_left_fac = pltpu.make_async_copy(left_fac, left_box, fac_sem.at[0])
    fetch_right_fac = pltpu.make_async_copy(right_fac, right_fac_box, fac_sem.at[1])
    size = QROWS * COLS
    quarters = (over, down, up, me_x)
    loads = [
        pltpu.make_async_copy(
            grads.at[:, pl.ds(pl.multiple_of(quarters[part] * size, size), size)],
            flat.at[part % 2], flat_sem.at[part % 2],
        )
        for part in range(N_X)
    ]

    def unpack(part, first, last):
        def step(col, carry):
            for half in range(2):
                for line in range(16):
                    at = pl.multiple_of((half * 16 + line) * COLS + col * BLK, BLK)
                    mid[half, line * STEP : line * STEP + 8, :] = (
                        flat[part % 2, :, pl.ds(at, BLK)].astype(f32).reshape(8, 128)
                    )
            for half in range(2):
                for lane in range(8):
                    tiles[part, col, half * 16 : half * 16 + 16, lane * 128 : lane * 128 + 128] = (
                        mid[half, pl.ds(lane, 16, STEP), :].astype(bf16)
                    )
            return carry

        lax.fori_loop(first, last, step, 0)

    def sender(src, dst, send_sem, recv_sem, target):
        away = lambda: pltpu.make_async_remote_copy(
            src_ref=src, dst_ref=dst, send_sem=send_sem, recv_sem=recv_sem,
            device_id=(me_x, target), device_id_type=MESH,
        )
        home = lambda: pltpu.make_async_copy(src, dst, recv_sem)
        return target, away, home

    sums_of = (sum_own, sum_down, sum_up)
    from_of = (me_x, down, up)

    def piece(origin, place, count):
        holder = lax.rem(count + me_s // NBR, SUBS) * NBR + lax.rem(row + NBR - place, NBR)
        src, dst = outbox.at[origin, place, count], blocks.at[place, sub, from_of[origin]]
        return sender(
            src, dst, piece_send.at[origin, place, count], piece_recv.at[origin, place], holder
        )

    def spread(origin):
        for place in range(SLOTS):

            def step(count, carry):
                holder, away, home = piece(origin, place, count)
                block = table[place, holder]
                outbox[origin, place, count] = sums_of[origin][lax.rem(jnp.maximum(block, 0), NBC)]

                @pl.when(holder != me_s)
                def _():
                    away().start()

                @pl.when(holder == me_s)
                def _():
                    home().start()

                return carry

            lax.fori_loop(0, SUBS, step, 0)

    def gather_block(slot):
        def one(place, subs, x_from, x):
            ref = blocks.at[slot, subs, x_from]
            return cross(ref, ref, block_send.at[slot, place], block_recv.at[slot, place], x)

        return [one(0, pl.ds(0, 4), down, up), one(1, pl.ds(4, 4), up, down)]

    block_copies = [gather_block(slot) for slot in range(SLOTS)]

    def arrive(origin, slot):
        pieces = blocks.at[slot, :, from_of[origin]]
        pltpu.make_async_copy(pieces, pieces, piece_recv.at[origin, slot]).wait()

    def locate(col, carry):
        wanted = row * NBC + col
        index = 0
        for cell in range(CELLS):
            place = cell % SLOTS
            holder = cell // SLOTS * NBR + lax.rem(row + NBR - place, NBR)
            index = jnp.where(table[place, holder] == wanted, cell, index)
        places[col] = index
        return carry

    def add_a(col, carry):
        part_a[col] = (fwd_a[col].astype(f32) + tiles[DOWN, col].astype(f32)).astype(bf16)
        return carry

    def add_b(col, carry):
        part_b[col] = (fwd_b[col].astype(f32) + tiles[UP, CUT + col].astype(f32)).astype(bf16)
        return carry

    def add_all(col, carry):
        sum_own[col] = (
            tiles[OWN, col].astype(f32) + (from_p[col].astype(f32) + from_m[col].astype(f32))
        ).astype(bf16)
        return carry

    loads[0].start()
    loads[1].start()
    fetch_right.start()
    fetch_left_fac.start()
    fetch_right_fac.start()
    hail(me_x, me_s)
    loads[0].wait()
    unpack(OVER, 0, CUT)
    admitted()
    keep.start()
    copies[0].start()
    unpack(OVER, CUT, NBC)
    copies[1].start()
    loads[2].start()
    loads[1].wait()
    unpack(DOWN, 0, NBC)
    copies[2].start()
    loads[3].start()
    loads[2].wait()
    unpack(UP, 0, NBC)
    copies[3].start()
    copies[0].wait_recv()
    lax.fori_loop(0, CUT, add_a, 0)
    copies[4].start()
    copies[1].wait_recv()
    lax.fori_loop(0, NBC - CUT, add_b, 0)
    copies[5].start()
    loads[3].wait()
    unpack(OWN, 0, NBC)
    copies[3].wait_recv()
    copies[4].wait_recv()
    lax.fori_loop(0, CUT, add_all, 0)
    copies[6].start()
    copies[9].start()
    copies[2].wait_recv()
    copies[5].wait_recv()
    lax.fori_loop(CUT, NBC, add_all, 0)
    copies[7].start()
    copies[8].start()
    spread(0)
    lax.fori_loop(0, NBC, locate, 0)
    copies[6].wait_recv()
    copies[8].wait_recv()
    start_root(0, 0)
    spread(1)
    copies[7].wait_recv()
    copies[9].wait_recv()
    start_root(0, 1)
    spread(2)
    start_root(0, 2)
    for slot in range(SLOTS):
        pass_root(0, slot)
    for slot in range(SLOTS):
        start_root(1, slot)
        arrive(1, slot)
        block_copies[slot][0].start()
        arrive(2, slot)
        block_copies[slot][1].start()
    pass_root(1, 0)
    pass_root(1, 1)

    def target_of(place, count):
        target_sub = lax.rem(3 * count + 3 * sub + 2 * row, SUBS)
        return target_sub, lax.rem(me_s + place, NBR) * SUBS + target_sub

    def back(place, half, count):
        target_sub, target = target_of(place, count)
        return sender(
            raw.at[half, place, target_sub], inbox[half].at[me_s // NBR * SLOTS + place],
            back_send.at[half, place, count], back_recv.at[half], target,
        )

    def tell(place, count):
        target_sub, target = target_of(place, count)
        return sender(
            factors.at[place], factor_box.at[me_s // NBR * SLOTS + place],
            factor_send.at[place, count], factor_recv, target,
        )

    def start_all(describe):
        def step(count, carry):
            target, away, home = describe(count)

            @pl.when(target != me_s)
            def _():
                away().start()

            @pl.when(target == me_s)
            def _():
                home().start()

            return carry

        lax.fori_loop(0, SUBS, step, 0)

    def finish_all(describe):
        def step(count, carry):
            target, away, home = describe(count)

            @pl.when(target != me_s)
            def _():
                away().wait_send()

            return carry

        lax.fori_loop(0, SUBS, step, 0)

    squares = [[] for slot in range(SLOTS)]

    def direct(half, slot):
        for copy in root_copies[half][slot][2:]:
            copy.wait_recv()
        result = jnp.dot(
            roots[slot, :, :, half].reshape(BLK // HALVES, BLK), precond[slot],
            preferred_element_type=f32,
        )
        raw[half, slot] = result.astype(bf16).reshape(SUBS, HROWS, 256)
        start_all(functools.partial(back, slot, half))
        squares[slot].append(jnp.sum(jnp.square(result)))

    shares = []

    def share(slot):
        sums[slot] = jnp.full((8, 128), squares[slot][0] + squares[slot][1], f32)
        for index, x in enumerate((up, down, over)):
            copy = cross(
                sums.at[slot], sum_box.at[slot, index],
                sum_send.at[slot, index], sum_recv.at[slot, index], x,
            )
            copy.start()
            shares.append(copy)

    def graft(slot):
        total = sums[slot] + (sum_box[slot, 0] + sum_box[slot, 1] + sum_box[slot, 2])
        factors[slot] = jnp.sqrt(powers[slot]) / jnp.sqrt(total / (BLK * BLK) + EPSILON)
        start_all(functools.partial(tell, slot))

    def ring(src, dst, group, place, x):
        return cross(src, dst, ring_send.at[group, place], ring_recv.at[group, place], x)

    def links(group):
        mine = gathered.at[me_x, group]
        below, above = gathered.at[down, group, low], gathered.at[up, group, high]
        return [
            ring(mine.at[low], mine.at[low], group, 0, up),
            ring(mine.at[high], mine.at[high], group, 1, down),
            ring(mine.at[high], mine.at[high], group, 2, up),
            ring(mine.at[low], mine.at[low], group, 3, down),
            ring(below, below, group, 4, up),
            ring(above, above, group, 5, down),
        ]

    every = [links(group) for group in range(GROUPS)]

    def statistics(slot):
        whole = blocks[slot].reshape(BLK, BLK)
        scale = jnp.where(table[slot, me_s] >= 0, 1.0 / BLK, 0.0).astype(f32)
        rows = blocks[slot, pl.ds(me_x * 2, 2)].reshape(256, BLK)
        left_box[slot] = left_box[slot] + contract_last(rows, whole) * scale
        start = pl.multiple_of(me_x * 256, 256)
        cols = blocks[slot, :, :, :, pl.ds(start, 256)].reshape(BLK, 256)
        right_fac_box[slot] = (
            right_fac_box[slot] + jnp.dot(cols.T, whole, preferred_element_type=f32) * scale
        )
        for copy in leave(slot):
            copy.start()

    def leave(slot):
        return [
            pltpu.make_async_copy(left_box.at[slot], new_left.at[slot], out_sem.at[slot, 0]),
            pltpu.make_async_copy(right_fac_box.at[slot], new_right.at[slot], out_sem.at[slot, 1]),
        ]

    def forward(group):
        every[group][0].wait_recv()
        every[group][4].start()
        every[group][1].wait_recv()
        every[group][5].start()

    def place_group(group):
        half, first = group // 2, group % 2 * QROWS

        def step(col, carry):
            gathered[me_x, group, col] = inbox[half][places[col], pl.ds(first, QROWS)]
            return carry

        lax.fori_loop(0, NBC, step, 0)

    def ring_group(group):
        for copy in every[group][:4]:
            copy.start()

    def flat_copy(group):
        at = pl.ds(group * size, size)
        return pltpu.make_async_copy(flat.at[group % 2], update.at[:, at], flat_sem.at[group % 2])

    def flatten(group):
        for copy in every[group][2:]:
            copy.wait_recv()
        if group >= 2:
            flat_copy(group - 2).wait()

        def step(col, carry):
            factor = factor_box[places[col]][0:1, :]
            for rows in range(2):
                for part in range(N_X):
                    for lane in range(2):
                        value = gathered[
                            part, group, col, rows * 16 : rows * 16 + 16, lane * 128 : lane * 128 + 128
                        ].astype(f32)
                        mid[rows, pl.ds(part * 2 + lane, 16, STEP), :] = value * factor
            for rows in range(2):
                for line in range(16):
                    at = pl.multiple_of((rows * 16 + line) * COLS + col * BLK, BLK)
                    flat[group % 2, :, pl.ds(at, BLK)] = (
                        mid[rows, line * STEP : line * STEP + 8, :].reshape(1, BLK).astype(bf16)
                    )
            return carry

        lax.fori_loop(0, NBC, step, 0)
        flat_copy(group).start()

    keep.wait()
    fetch_right.wait()
    powers = []
    for slot in range(SLOTS):
        arrive(0, slot)
        for copy in block_copies[slot]:
            copy.wait_recv()
        grad = blocks[slot].reshape(BLK, BLK)
        precond[slot] = contract_last(grad, right_box[slot]).astype(bf16)
        direct(0, slot)
    pass_root(1, 2)
    for slot in range(SLOTS):
        grad = blocks[slot].reshape(BLK, BLK)
        powers.append(jnp.sum(jnp.square(grad.astype(f32))) / (BLK * BLK))
    pltpu.make_async_copy(inbox_0, inbox_0, back_recv.at[0]).wait()
    place_group(0)
    ring_group(0)
    place_group(1)
    for slot in range(SLOTS):
        direct(1, slot)
    ring_group(1)
    for slot in range(SLOTS):
        share(slot)
    forward(0)
    pltpu.make_async_copy(inbox_1, inbox_1, back_recv.at[1]).wait()
    place_group(2)
    ring_group(2)
    place_group(3)
    ring_group(3)
    for copy in shares:
        copy.wait_recv()
    for slot in range(SLOTS):
        graft(slot)
    forward(1)
    fetch_left_fac.wait()
    fetch_right_fac.wait()
    statistics(0)
    forward(2)
    statistics(1)
    pltpu.make_async_copy(factor_box, factor_box, factor_recv).wait()
    flatten(0)
    flatten(1)
    forward(3)
    statistics(2)
    flatten(2)
    flatten(3)
    flat_copy(2).wait()
    flat_copy(3).wait()
    for group in range(GROUPS):
        for copy in every[group]:
            copy.wait_send()
    for copy in shares + copies:
        copy.wait_send()
    for slot in range(SLOTS):
        for half in range(HALVES):
            for copy in root_copies[half][slot]:
                copy.wait_send()
            finish_all(functools.partial(back, slot, half))
        finish_all(functools.partial(tell, slot))
        for origin in range(3):
            finish_all(functools.partial(piece, origin, slot))
        for copy in block_copies[slot]:
            copy.wait_send()
        for copy in leave(slot):
            copy.wait()


def contract_last(a, b):
    return lax.dot_general(a, b, (((1,), (1,)), ((), ())), preferred_element_type=f32)


def on_device(grads, slot_table, left_factor, right_factor, left_root, right_root):
    smem = pl.BlockSpec(memory_space=pltpu.SMEM)
    hbm = pl.BlockSpec(memory_space=pl.ANY)
    dma = pltpu.SemaphoreType.DMA
    vmem = pltpu.VMEM

    new_left, new_right, update = pl.pallas_call(
        shampoo,
        in_specs=[smem] + [hbm] * 5,
        out_specs=[hbm] * 3,
        out_shape=[
            jax.ShapeDtypeStruct((SLOTS, 256, BLK), f32),
            jax.ShapeDtypeStruct((SLOTS, 256, BLK), f32),
            jax.ShapeDtypeStruct((1, 128 * COLS), bf16),
        ],
        scratch_shapes=[
            vmem((2, 1, QROWS * COLS), bf16),
            vmem((2, 16 * STEP, 128), f32),
            vmem((N_X, NBC, QROWS, BLK), bf16),
            vmem((CUT, QROWS, BLK), bf16),
            vmem((NBC - CUT, QROWS, BLK), bf16),
            vmem((CUT, QROWS, BLK), bf16),
            vmem((NBC - CUT, QROWS, BLK), bf16),
        ]
        + [vmem((NBC, QROWS, BLK), bf16)] * 5
        + [
            vmem((3, SLOTS, SUBS, QROWS, BLK), bf16),
            vmem((SLOTS, SUBS, N_X, QROWS, BLK), bf16),
            vmem((SLOTS, N_X, 2, HALVES, HROWS, BLK), bf16),
            vmem((SLOTS, 256, BLK), bf16),
            vmem((SLOTS, BLK, 256), bf16),
            vmem((SLOTS, 8, 128), f32),
            vmem((SLOTS, 3, 8, 128), f32),
            vmem((SLOTS, 8, 128), f32),
            vmem((CELLS, 8, 128), f32),
            vmem((HALVES, SLOTS, SUBS, HROWS, 256), bf16),
            vmem((CELLS, HROWS, 256), bf16),
            vmem((CELLS, HROWS, 256), bf16),
            vmem((N_X, GROUPS, NBC, QROWS, 256), bf16),
            vmem((SLOTS, 256, BLK), f32),
            vmem((SLOTS, 256, BLK), f32),
            pltpu.SMEM((NBC,), jnp.int32),
            dma((2,)),
            dma,
            dma,
            dma((SLOTS, 2)),
            dma((10,)),
            dma((10,)),
            dma((SLOTS, HALVES, 6)),
            dma((SLOTS, HALVES, 6)),
            dma((2,)),
            dma((3, SLOTS, SUBS)),
            dma((3, SLOTS)),
            dma((SLOTS, 2)),
            dma((SLOTS, 2)),
            dma((SLOTS, 3)),
            dma((SLOTS, 3)),
            dma((SLOTS, SUBS)),
            dma,
            dma((HALVES, SLOTS, SUBS)),
            dma((HALVES,)),
            dma((GROUPS, 6)),
            dma((GROUPS, 6)),
        ],
        compiler_params=pltpu.CompilerParams(
            collective_id=0, has_side_effects=True, vmem_limit_bytes=VMEM_BYTES
        ),
        name="shampoo",
    )(slot_table.T, grads, left_root.reshape(SLOTS, 2, HALVES, HROWS, BLK), right_root[0], left_factor[0], right_factor[0])

    shapes = [
        jax.ShapeDtypeStruct((1, 128 * COLS), bf16),
        jax.ShapeDtypeStruct((SLOTS * 256, BLK), f32),
        jax.ShapeDtypeStruct((SLOTS * 256, BLK), f32),
    ]
    flat, new_left, new_right = pl.pallas_call(
        deliver,
        in_specs=[hbm] * 3,
        out_specs=[hbm] * 3,
        out_shape=shapes,
        scratch_shapes=[vmem(shape.shape, shape.dtype) for shape in shapes] + [dma((3, PARTS))] * 2,
        compiler_params=pltpu.CompilerParams(vmem_limit_bytes=VMEM_BYTES),
        name="deliver",
    )(update, new_left.reshape(SLOTS * 256, BLK), new_right.reshape(SLOTS * 256, BLK))
    rows = (1, SLOTS, 256, BLK)
    return new_left.reshape(rows), new_right.reshape(rows), flat


def solution(mesh):
    rows = P("shard", None, "replica", None)
    flat = P("replica", "shard")
    return jax.shard_map(
        on_device,
        mesh=mesh,
        in_specs=(flat, P(), rows, rows, rows, rows),
        out_specs=(rows, rows, flat),
        check_vma=False,
    )
```

```python
import functools

import jax
import jax.numpy as jnp
from jax import lax
from jax.experimental import pallas as pl
from jax.experimental.pallas import tpu as pltpu
from jax.sharding import PartitionSpec as P

ROWS = 4096
COLS = 15360
BLK = 1024
EPSILON = 1e-06

N_X = 4
N_S = 32
SLOTS = 3
NBR = 4
NBC = 15
SUBS = 8
CELLS = 24
QROWS = 32
CUT = 8
GROUPS = 4
MESH = pl.DeviceIdType.MESH
f32 = jnp.float32
bf16 = jnp.bfloat16
VMEM_BYTES = 58 * 1024 * 1024


STEP = 9
HALVES = 2
HROWS = 64
PARTS = 8


def deliver(*refs):
    sources, targets, boxes = refs[:3], refs[3:6], refs[6:9]
    read_sem, write_sem = refs[9:]
    reads, writes = [], []
    for index in range(3):
        for part in range(PARTS):
            if index == 0:
                count = 128 * COLS // PARTS
                at = (slice(None), pl.ds(part * count, count))
            else:
                count = SLOTS * 256 // PARTS
                at = (pl.ds(part * count, count),)
            box = boxes[index].at[at]
            reads.append(pltpu.make_async_copy(sources[index].at[at], box, read_sem.at[index, part]))
            writes.append(pltpu.make_async_copy(box, targets[index].at[at], write_sem.at[index, part]))
    for read in reads:
        read.start()
    for read, write in zip(reads, writes):
        read.wait()
        write.start()
    for write in writes:
        write.wait()


def hail(me_x, me_s):
    barrier = pltpu.get_barrier_semaphore()

    def one(step, carry):
        pl.semaphore_signal(
            barrier, inc=1, device_id=(me_x, lax.rem(me_s + step, N_S)), device_id_type=MESH
        )
        return carry

    lax.fori_loop(1, N_S, one, 0)
    for far in range(1, N_X):
        pl.semaphore_signal(
            barrier, inc=1, device_id=(lax.rem(me_x + far, N_X), me_s), device_id_type=MESH
        )


def admitted():
    pl.semaphore_wait(pltpu.get_barrier_semaphore(), N_S - 1 + N_X - 1)


def shampoo(
    table, grads, left, right, left_fac, right_fac, new_left, new_right, update,
    flat, mid, tiles, fwd_a, fwd_b, part_a, part_b, from_p, from_m,
    sum_own, sum_down, sum_up, outbox, blocks, roots, right_box, precond,
    sums, sum_box, factors, factor_box, raw, inbox_0, inbox_1, gathered, left_box, right_fac_box, places,
    flat_sem, right_sem, keep_sem, out_sem, send, recv, root_send, root_recv,
    fac_sem, piece_send, piece_recv, block_send, block_recv, sum_send, sum_recv, factor_send, factor_recv,
    back_send, back_recv, ring_send, ring_recv,
):
    me_x, me_s = lax.axis_index("replica"), lax.axis_index("shard")
    row, sub = me_s // SUBS, lax.rem(me_s, SUBS)
    up, down, over = lax.rem(me_x + 1, N_X), lax.rem(me_x + 3, N_X), lax.rem(me_x + 2, N_X)
    low, high = pl.ds(0, CUT), pl.ds(CUT, NBC - CUT)
    inbox = (inbox_0, inbox_1)
    OVER, DOWN, UP, OWN = range(4)

    def cross(src, dst, send_sem, recv_sem, x):
        return pltpu.make_async_remote_copy(
            src_ref=src, dst_ref=dst, send_sem=send_sem, recv_sem=recv_sem,
            device_id=(x, me_s), device_id_type=MESH,
        )

    def remote(src, dst, place, x):
        return cross(src, dst, send.at[place], recv.at[place], x)

    copies = [
        remote(tiles.at[OVER, low], fwd_a, 0, down),
        remote(tiles.at[OVER, high], fwd_b, 1, up),
        remote(tiles.at[DOWN, high], from_p.at[high], 2, down),
        remote(tiles.at[UP, low], from_m.at[low], 3, up),
        remote(part_a, from_p.at[low], 4, down),
        remote(part_b, from_m.at[high], 5, up),
        remote(sum_own.at[low], sum_down.at[low], 6, up),
        remote(sum_own.at[high], sum_up.at[high], 7, down),
        remote(sum_own.at[high], sum_down.at[high], 8, up),
        remote(sum_own.at[low], sum_up.at[low], 9, down),
    ]
    def root(slot, half):
        mine, there = left.at[slot], roots.at[slot, me_x]
        below, above = roots.at[slot, down, 0, half], roots.at[slot, up, 1, half]

        def one(place, src, dst, x):
            return cross(
                src, dst, root_send.at[slot, half, place], root_recv.at[slot, half, place], x
            )

        return [
            one(0, mine.at[0, half], there.at[0, half], up),
            one(1, mine.at[1, half], there.at[1, half], down),
            one(2, mine.at[1, half], there.at[1, half], up),
            one(3, mine.at[0, half], there.at[0, half], down),
            one(4, below, below, up),
            one(5, above, above, down),
        ]

    root_copies = [[root(slot, half) for slot in range(SLOTS)] for half in range(HALVES)]

    def start_root(half, slot):
        for copy in root_copies[half][slot][:4]:
            copy.start()

    def pass_root(half, slot):
        for place in range(2):
            root_copies[half][slot][place].wait_recv()
            root_copies[half][slot][place + 4].start()

    keep = pltpu.make_async_copy(left, roots.at[:, me_x], keep_sem)
    fetch_right = pltpu.make_async_copy(right, right_box, right_sem)
    fetch_left_fac = pltpu.make_async_copy(left_fac, left_box, fac_sem.at[0])
    fetch_right_fac = pltpu.make_async_copy(right_fac, right_fac_box, fac_sem.at[1])
    size = QROWS * COLS
    quarters = (over, down, up, me_x)
    loads = [
        pltpu.make_async_copy(
            grads.at[:, pl.ds(pl.multiple_of(quarters[part] * size, size), size)],
            flat.at[part % 2], flat_sem.at[part % 2],
        )
        for part in range(N_X)
    ]

    def unpack(part, first, last):
        def step(col, carry):
            for half in range(2):
                for line in range(16):
                    at = pl.multiple_of((half * 16 + line) * COLS + col * BLK, BLK)
                    mid[half, line * STEP : line * STEP + 8, :] = (
                        flat[part % 2, :, pl.ds(at, BLK)].astype(f32).reshape(8, 128)
                    )
            for half in range(2):
                for lane in range(8):
                    tiles[part, col, half * 16 : half * 16 + 16, lane * 128 : lane * 128 + 128] = (
                        mid[half, pl.ds(lane, 16, STEP), :].astype(bf16)
                    )
            return carry

        lax.fori_loop(first, last, step, 0)

    def sender(src, dst, send_sem, recv_sem, target):
        away = lambda: pltpu.make_async_remote_copy(
            src_ref=src, dst_ref=dst, send_sem=send_sem, recv_sem=recv_sem,
            device_id=(me_x, target), device_id_type=MESH,
        )
        home = lambda: pltpu.make_async_copy(src, dst, recv_sem)
        return target, away, home

    sums_of = (sum_own, sum_down, sum_up)
    from_of = (me_x, down, up)

    def piece(origin, place, count):
        holder = lax.rem(count + me_s // NBR, SUBS) * NBR + lax.rem(row + NBR - place, NBR)
        src, dst = outbox.at[origin, place, count], blocks.at[place, sub, from_of[origin]]
        return sender(
            src, dst, piece_send.at[origin, place, count], piece_recv.at[origin, place], holder
        )

    def spread(origin):
        for place in range(SLOTS):

            def step(count, carry):
                holder, away, home = piece(origin, place, count)
                block = table[place, holder]
                outbox[origin, place, count] = sums_of[origin][lax.rem(jnp.maximum(block, 0), NBC)]

                @pl.when(holder != me_s)
                def _():
                    away().start()

                @pl.when(holder == me_s)
                def _():
                    home().start()

                return carry

            lax.fori_loop(0, SUBS, step, 0)

    def gather_block(slot):
        def one(place, subs, x_from, x):
            ref = blocks.at[slot, subs, x_from]
            return cross(ref, ref, block_send.at[slot, place], block_recv.at[slot, place], x)

        return [one(0, pl.ds(0, 4), down, up), one(1, pl.ds(4, 4), up, down)]

    block_copies = [gather_block(slot) for slot in range(SLOTS)]

    def arrive(origin, slot):
        pieces = blocks.at[slot, :, from_of[origin]]
        pltpu.make_async_copy(pieces, pieces, piece_recv.at[origin, slot]).wait()

    def locate(col, carry):
        wanted = row * NBC + col
        index = 0
        for cell in range(CELLS):
            place = cell % SLOTS
            holder = cell // SLOTS * NBR + lax.rem(row + NBR - place, NBR)
            index = jnp.where(table[place, holder] == wanted, cell, index)
        places[col] = index
        return carry

    def add_a(col, carry):
        part_a[col] = (fwd_a[col].astype(f32) + tiles[DOWN, col].astype(f32)).astype(bf16)
        return carry

    def add_b(col, carry):
        part_b[col] = (fwd_b[col].astype(f32) + tiles[UP, CUT + col].astype(f32)).astype(bf16)
        return carry

    def add_all(col, carry):
        sum_own[col] = (
            tiles[OWN, col].astype(f32) + (from_p[col].astype(f32) + from_m[col].astype(f32))
        ).astype(bf16)
        return carry

    loads[0].start()
    loads[1].start()
    fetch_right.start()
    fetch_left_fac.start()
    fetch_right_fac.start()
    hail(me_x, me_s)
    loads[0].wait()
    unpack(OVER, 0, CUT)
    admitted()
    keep.start()
    copies[0].start()
    unpack(OVER, CUT, NBC)
    copies[1].start()
    loads[2].start()
    loads[1].wait()
    unpack(DOWN, 0, NBC)
    copies[2].start()
    loads[3].start()
    loads[2].wait()
    unpack(UP, 0, NBC)
    copies[3].start()
    copies[0].wait_recv()
    lax.fori_loop(0, CUT, add_a, 0)
    copies[4].start()
    copies[1].wait_recv()
    lax.fori_loop(0, NBC - CUT, add_b, 0)
    copies[5].start()
    loads[3].wait()
    unpack(OWN, 0, NBC)
    copies[3].wait_recv()
    copies[4].wait_recv()
    lax.fori_loop(0, CUT, add_all, 0)
    copies[6].start()
    copies[9].start()
    copies[2].wait_recv()
    copies[5].wait_recv()
    lax.fori_loop(CUT, NBC, add_all, 0)
    copies[7].start()
    copies[8].start()
    spread(0)
    lax.fori_loop(0, NBC, locate, 0)
    copies[6].wait_recv()
    copies[8].wait_recv()
    start_root(0, 0)
    spread(1)
    copies[7].wait_recv()
    copies[9].wait_recv()
    start_root(0, 1)
    spread(2)
    start_root(0, 2)
    for slot in range(SLOTS):
        pass_root(0, slot)
    for slot in range(SLOTS):
        if slot < SLOTS - 1:
            start_root(1, slot)
        arrive(1, slot)
        block_copies[slot][0].start()
        arrive(2, slot)
        block_copies[slot][1].start()
    pass_root(1, 0)
    pass_root(1, 1)

    def target_of(place, count):
        target_sub = lax.rem(3 * count + 3 * sub + 2 * row, SUBS)
        return target_sub, lax.rem(me_s + place, NBR) * SUBS + target_sub

    def back(place, half, count):
        target_sub, target = target_of(place, count)
        return sender(
            raw.at[half, place, target_sub], inbox[half].at[me_s // NBR * SLOTS + place],
            back_send.at[half, place, count], back_recv.at[half], target,
        )

    def tell(place, count):
        target_sub, target = target_of(place, count)
        return sender(
            factors.at[place], factor_box.at[me_s // NBR * SLOTS + place],
            factor_send.at[place, count], factor_recv, target,
        )

    def start_all(describe):
        def step(count, carry):
            target, away, home = describe(count)

            @pl.when(target != me_s)
            def _():
                away().start()

            @pl.when(target == me_s)
            def _():
                home().start()

            return carry

        lax.fori_loop(0, SUBS, step, 0)

    def finish_all(describe):
        def step(count, carry):
            target, away, home = describe(count)

            @pl.when(target != me_s)
            def _():
                away().wait_send()

            return carry

        lax.fori_loop(0, SUBS, step, 0)

    squares = [[] for slot in range(SLOTS)]

    def direct(half, slot):
        for copy in root_copies[half][slot][2:]:
            copy.wait_recv()
        result = jnp.dot(
            roots[slot, :, :, half].reshape(BLK // HALVES, BLK), precond[slot],
            preferred_element_type=f32,
        )
        raw[half, slot] = result.astype(bf16).reshape(SUBS, HROWS, 256)
        start_all(functools.partial(back, slot, half))
        squares[slot].append(jnp.sum(jnp.square(result)))

    shares = []

    def share(slot):
        sums[slot] = jnp.full((8, 128), squares[slot][0] + squares[slot][1], f32)
        for index, x in enumerate((up, down, over)):
            copy = cross(
                sums.at[slot], sum_box.at[slot, index],
                sum_send.at[slot, index], sum_recv.at[slot, index], x,
            )
            copy.start()
            shares.append(copy)

    def graft(slot):
        total = sums[slot] + (sum_box[slot, 0] + sum_box[slot, 1] + sum_box[slot, 2])
        factors[slot] = jnp.sqrt(powers[slot]) / jnp.sqrt(total / (BLK * BLK) + EPSILON)
        start_all(functools.partial(tell, slot))

    def ring(src, dst, group, place, x):
        return cross(src, dst, ring_send.at[group, place], ring_recv.at[group, place], x)

    def links(group):
        mine = gathered.at[me_x, group]
        below, above = gathered.at[down, group, low], gathered.at[up, group, high]
        return [
            ring(mine.at[low], mine.at[low], group, 0, up),
            ring(mine.at[high], mine.at[high], group, 1, down),
            ring(mine.at[high], mine.at[high], group, 2, up),
            ring(mine.at[low], mine.at[low], group, 3, down),
            ring(below, below, group, 4, up),
            ring(above, above, group, 5, down),
        ]

    every = [links(group) for group in range(GROUPS)]

    def statistics(slot):
        whole = blocks[slot].reshape(BLK, BLK)
        scale = jnp.where(table[slot, me_s] >= 0, 1.0 / BLK, 0.0).astype(f32)
        rows = blocks[slot, pl.ds(me_x * 2, 2)].reshape(256, BLK)
        left_box[slot] = left_box[slot] + contract_last(rows, whole) * scale
        start = pl.multiple_of(me_x * 256, 256)
        cols = blocks[slot, :, :, :, pl.ds(start, 256)].reshape(BLK, 256)
        right_fac_box[slot] = (
            right_fac_box[slot] + jnp.dot(cols.T, whole, preferred_element_type=f32) * scale
        )
        for copy in leave(slot):
            copy.start()

    def leave(slot):
        return [
            pltpu.make_async_copy(left_box.at[slot], new_left.at[slot], out_sem.at[slot, 0]),
            pltpu.make_async_copy(right_fac_box.at[slot], new_right.at[slot], out_sem.at[slot, 1]),
        ]

    def forward(group):
        every[group][0].wait_recv()
        every[group][4].start()
        every[group][1].wait_recv()
        every[group][5].start()

    def place_group(group):
        half, first = group // 2, group % 2 * QROWS

        def step(col, carry):
            gathered[me_x, group, col] = inbox[half][places[col], pl.ds(first, QROWS)]
            return carry

        lax.fori_loop(0, NBC, step, 0)

    def ring_group(group):
        for copy in every[group][:4]:
            copy.start()

    def flat_copy(group):
        at = pl.ds(group * size, size)
        return pltpu.make_async_copy(flat.at[group % 2], update.at[:, at], flat_sem.at[group % 2])

    def flatten(group):
        for copy in every[group][2:]:
            copy.wait_recv()
        if group >= 2:
            flat_copy(group - 2).wait()

        def step(col, carry):
            factor = factor_box[places[col]][0:1, :]
            for rows in range(2):
                for part in range(N_X):
                    for lane in range(2):
                        value = gathered[
                            part, group, col, rows * 16 : rows * 16 + 16, lane * 128 : lane * 128 + 128
                        ].astype(f32)
                        mid[rows, pl.ds(part * 2 + lane, 16, STEP), :] = value * factor
            for rows in range(2):
                for line in range(16):
                    at = pl.multiple_of((rows * 16 + line) * COLS + col * BLK, BLK)
                    flat[group % 2, :, pl.ds(at, BLK)] = (
                        mid[rows, line * STEP : line * STEP + 8, :].reshape(1, BLK).astype(bf16)
                    )
            return carry

        lax.fori_loop(0, NBC, step, 0)
        flat_copy(group).start()

    keep.wait()
    fetch_right.wait()
    fetch_left_fac.wait()
    fetch_right_fac.wait()
    powers = []
    for slot in range(SLOTS):
        arrive(0, slot)
        for copy in block_copies[slot]:
            copy.wait_recv()
        if slot == SLOTS - 1:
            start_root(1, slot)
        grad = blocks[slot].reshape(BLK, BLK)
        precond[slot] = contract_last(grad, right_box[slot]).astype(bf16)
        direct(0, slot)
        if slot == 0:
            statistics(0)
    for slot in range(SLOTS):
        grad = blocks[slot].reshape(BLK, BLK)
        powers.append(jnp.sum(jnp.square(grad.astype(f32))) / (BLK * BLK))
    pltpu.make_async_copy(inbox_0, inbox_0, back_recv.at[0]).wait()
    place_group(0)
    ring_group(0)
    place_group(1)
    pass_root(1, 2)
    direct(1, 0)
    direct(1, 1)
    statistics(1)
    forward(0)
    direct(1, 2)
    ring_group(1)
    for slot in range(SLOTS):
        share(slot)
    pltpu.make_async_copy(inbox_1, inbox_1, back_recv.at[1]).wait()
    place_group(2)
    ring_group(2)
    place_group(3)
    ring_group(3)
    for copy in shares:
        copy.wait_recv()
    for slot in range(SLOTS):
        graft(slot)
    forward(1)
    statistics(2)
    forward(2)
    pltpu.make_async_copy(factor_box, factor_box, factor_recv).wait()
    flatten(0)
    forward(3)
    flatten(1)
    flatten(2)
    flatten(3)
    flat_copy(2).wait()
    flat_copy(3).wait()
    for group in range(GROUPS):
        for copy in every[group]:
            copy.wait_send()
    for copy in shares + copies:
        copy.wait_send()
    for slot in range(SLOTS):
        for half in range(HALVES):
            for copy in root_copies[half][slot]:
                copy.wait_send()
            finish_all(functools.partial(back, slot, half))
        finish_all(functools.partial(tell, slot))
        for origin in range(3):
            finish_all(functools.partial(piece, origin, slot))
        for copy in block_copies[slot]:
            copy.wait_send()
        for copy in leave(slot):
            copy.wait()


def contract_last(a, b):
    return lax.dot_general(a, b, (((1,), (1,)), ((), ())), preferred_element_type=f32)


def on_device(grads, slot_table, left_factor, right_factor, left_root, right_root):
    smem = pl.BlockSpec(memory_space=pltpu.SMEM)
    hbm = pl.BlockSpec(memory_space=pl.ANY)
    dma = pltpu.SemaphoreType.DMA
    vmem = pltpu.VMEM

    new_left, new_right, update = pl.pallas_call(
        shampoo,
        in_specs=[smem] + [hbm] * 5,
        out_specs=[hbm] * 3,
        out_shape=[
            jax.ShapeDtypeStruct((SLOTS, 256, BLK), f32),
            jax.ShapeDtypeStruct((SLOTS, 256, BLK), f32),
            jax.ShapeDtypeStruct((1, 128 * COLS), bf16),
        ],
        scratch_shapes=[
            vmem((2, 1, QROWS * COLS), bf16),
            vmem((2, 16 * STEP, 128), f32),
            vmem((N_X, NBC, QROWS, BLK), bf16),
            vmem((CUT, QROWS, BLK), bf16),
            vmem((NBC - CUT, QROWS, BLK), bf16),
            vmem((CUT, QROWS, BLK), bf16),
            vmem((NBC - CUT, QROWS, BLK), bf16),
        ]
        + [vmem((NBC, QROWS, BLK), bf16)] * 5
        + [
            vmem((3, SLOTS, SUBS, QROWS, BLK), bf16),
            vmem((SLOTS, SUBS, N_X, QROWS, BLK), bf16),
            vmem((SLOTS, N_X, 2, HALVES, HROWS, BLK), bf16),
            vmem((SLOTS, 256, BLK), bf16),
            vmem((SLOTS, BLK, 256), bf16),
            vmem((SLOTS, 8, 128), f32),
            vmem((SLOTS, 3, 8, 128), f32),
            vmem((SLOTS, 8, 128), f32),
            vmem((CELLS, 8, 128), f32),
            vmem((HALVES, SLOTS, SUBS, HROWS, 256), bf16),
            vmem((CELLS, HROWS, 256), bf16),
            vmem((CELLS, HROWS, 256), bf16),
            vmem((N_X, GROUPS, NBC, QROWS, 256), bf16),
            vmem((SLOTS, 256, BLK), f32),
            vmem((SLOTS, 256, BLK), f32),
            pltpu.SMEM((NBC,), jnp.int32),
            dma((2,)),
            dma,
            dma,
            dma((SLOTS, 2)),
            dma((10,)),
            dma((10,)),
            dma((SLOTS, HALVES, 6)),
            dma((SLOTS, HALVES, 6)),
            dma((2,)),
            dma((3, SLOTS, SUBS)),
            dma((3, SLOTS)),
            dma((SLOTS, 2)),
            dma((SLOTS, 2)),
            dma((SLOTS, 3)),
            dma((SLOTS, 3)),
            dma((SLOTS, SUBS)),
            dma,
            dma((HALVES, SLOTS, SUBS)),
            dma((HALVES,)),
            dma((GROUPS, 6)),
            dma((GROUPS, 6)),
        ],
        compiler_params=pltpu.CompilerParams(
            collective_id=0, has_side_effects=True, vmem_limit_bytes=VMEM_BYTES
        ),
        name="shampoo",
    )(slot_table.T, grads, left_root.reshape(SLOTS, 2, HALVES, HROWS, BLK), right_root[0], left_factor[0], right_factor[0])

    shapes = [
        jax.ShapeDtypeStruct((1, 128 * COLS), bf16),
        jax.ShapeDtypeStruct((SLOTS * 256, BLK), f32),
        jax.ShapeDtypeStruct((SLOTS * 256, BLK), f32),
    ]
    flat, new_left, new_right = pl.pallas_call(
        deliver,
        in_specs=[hbm] * 3,
        out_specs=[hbm] * 3,
        out_shape=shapes,
        scratch_shapes=[vmem(shape.shape, shape.dtype) for shape in shapes] + [dma((3, PARTS))] * 2,
        compiler_params=pltpu.CompilerParams(vmem_limit_bytes=VMEM_BYTES),
        name="deliver",
    )(update, new_left.reshape(SLOTS * 256, BLK), new_right.reshape(SLOTS * 256, BLK))
    rows = (1, SLOTS, 256, BLK)
    return new_left.reshape(rows), new_right.reshape(rows), flat


def solution(mesh):
    rows = P("shard", None, "replica", None)
    flat = P("replica", "shard")
    return jax.shard_map(
        on_device,
        mesh=mesh,
        in_specs=(flat, P(), rows, rows, rows, rows),
        out_specs=(rows, rows, flat),
        check_vma=False,
    )
```

```python
import functools

import jax
import jax.numpy as jnp
from jax import lax
from jax.experimental import pallas as pl
from jax.experimental.pallas import tpu as pltpu
from jax.sharding import PartitionSpec as P

ROWS = 4096
COLS = 15360
BLK = 1024
EPSILON = 1e-06

N_X = 4
N_S = 32
SLOTS = 3
NBR = 4
NBC = 15
SUBS = 8
CELLS = 24
QROWS = 32
CUT = 8
GROUPS = 4
SPLIT = 5
MESH = pl.DeviceIdType.MESH
f32 = jnp.float32
bf16 = jnp.bfloat16
VMEM_BYTES = 58 * 1024 * 1024


STEP = 9
HALVES = 2
HROWS = 64
PARTS = 8


def deliver(*refs):
    sources, targets, boxes = refs[:3], refs[3:6], refs[6:9]
    read_sem, write_sem = refs[9:]
    reads, writes = [], []
    for index in range(3):
        for part in range(PARTS):
            if index == 0:
                count = 128 * COLS // PARTS
                at = (slice(None), pl.ds(part * count, count))
            else:
                count = SLOTS * 256 // PARTS
                at = (pl.ds(part * count, count),)
            box = boxes[index].at[at]
            reads.append(pltpu.make_async_copy(sources[index].at[at], box, read_sem.at[index, part]))
            writes.append(pltpu.make_async_copy(box, targets[index].at[at], write_sem.at[index, part]))
    for read in reads:
        read.start()
    for read, write in zip(reads, writes):
        read.wait()
        write.start()
    for write in writes:
        write.wait()


def hail(me_x, me_s):
    barrier = pltpu.get_barrier_semaphore()

    def one(step, carry):
        pl.semaphore_signal(
            barrier, inc=1, device_id=(me_x, lax.rem(me_s + step, N_S)), device_id_type=MESH
        )
        return carry

    lax.fori_loop(1, N_S, one, 0)
    for far in range(1, N_X):
        pl.semaphore_signal(
            barrier, inc=1, device_id=(lax.rem(me_x + far, N_X), me_s), device_id_type=MESH
        )


def admitted():
    pl.semaphore_wait(pltpu.get_barrier_semaphore(), N_S - 1 + N_X - 1)


def shampoo(
    table, grads, left, right, left_fac, right_fac, new_left, new_right, update,
    flat, mid, tiles, fwd_a, fwd_b, part_a, part_b, from_p, from_m,
    sum_own, sum_down, outbox, blocks, roots, right_box, precond,
    sums, sum_box, factors, factor_box, raw, inbox_0, inbox_1, gathered, left_box, right_fac_box, places,
    flat_sem, right_sem, keep_sem, out_sem, send, recv, root_send, root_recv,
    fac_sem, piece_send, piece_recv, block_send, block_recv, sum_send, sum_recv, factor_send, factor_recv,
    back_send, back_recv, ring_send, ring_recv,
):
    me_x, me_s = lax.axis_index("replica"), lax.axis_index("shard")
    row, sub = me_s // SUBS, lax.rem(me_s, SUBS)
    up, down, over = lax.rem(me_x + 1, N_X), lax.rem(me_x + 3, N_X), lax.rem(me_x + 2, N_X)
    low, high = pl.ds(0, CUT), pl.ds(CUT, NBC - CUT)
    inbox = (inbox_0, inbox_1)
    OVER, DOWN, UP, OWN = range(4)

    def cross(src, dst, send_sem, recv_sem, x):
        return pltpu.make_async_remote_copy(
            src_ref=src, dst_ref=dst, send_sem=send_sem, recv_sem=recv_sem,
            device_id=(x, me_s), device_id_type=MESH,
        )

    def remote(src, dst, place, x):
        return cross(src, dst, send.at[place], recv.at[place], x)

    copies = [
        remote(tiles.at[OVER, low], fwd_a, 0, down),
        remote(tiles.at[OVER, high], fwd_b, 1, up),
        remote(tiles.at[DOWN, high], from_p.at[high], 2, down),
        remote(tiles.at[UP, low], from_m.at[low], 3, up),
        remote(part_a, from_p.at[low], 4, down),
        remote(part_b, from_m.at[high], 5, up),
        remote(sum_own.at[low], sum_down.at[low], 6, up),
        remote(sum_own.at[high], sum_down.at[high], 7, up),
    ]
    def root(slot, half):
        mine, there = left.at[slot], roots.at[slot, me_x]
        below, above = roots.at[slot, down, 0, half], roots.at[slot, up, 1, half]

        def one(place, src, dst, x):
            return cross(
                src, dst, root_send.at[slot, half, place], root_recv.at[slot, half, place], x
            )

        return [
            one(0, mine.at[0, half], there.at[0, half], up),
            one(1, mine.at[1, half], there.at[1, half], down),
            one(2, mine.at[1, half], there.at[1, half], up),
            one(3, mine.at[0, half], there.at[0, half], down),
            one(4, below, below, up),
            one(5, above, above, down),
        ]

    root_copies = [[root(slot, half) for slot in range(SLOTS)] for half in range(HALVES)]

    def start_root(half, slot):
        for copy in root_copies[half][slot][:4]:
            copy.start()

    def pass_root(half, slot):
        for place in range(2):
            root_copies[half][slot][place].wait_recv()
            root_copies[half][slot][place + 4].start()

    keep = pltpu.make_async_copy(left, roots.at[:, me_x], keep_sem)
    fetch_right = pltpu.make_async_copy(right, right_box, right_sem)
    fetch_left_fac = pltpu.make_async_copy(left_fac, left_box, fac_sem.at[0])
    fetch_right_fac = pltpu.make_async_copy(right_fac, right_fac_box, fac_sem.at[1])
    size = QROWS * COLS
    quarters = (over, down, up, me_x)
    loads = [
        pltpu.make_async_copy(
            grads.at[:, pl.ds(pl.multiple_of(quarters[part] * size, size), size)],
            flat.at[part % 2], flat_sem.at[part % 2],
        )
        for part in range(N_X)
    ]

    def unpack(part, first, last):
        def step(col, carry):
            for half in range(2):
                for line in range(16):
                    at = pl.multiple_of((half * 16 + line) * COLS + col * BLK, BLK)
                    mid[half, line * STEP : line * STEP + 8, :] = (
                        flat[part % 2, :, pl.ds(at, BLK)].astype(f32).reshape(8, 128)
                    )
            for half in range(2):
                for lane in range(8):
                    tiles[part, col, half * 16 : half * 16 + 16, lane * 128 : lane * 128 + 128] = (
                        mid[half, pl.ds(lane, 16, STEP), :].astype(bf16)
                    )
            return carry

        lax.fori_loop(first, last, step, 0)

    def sender(src, dst, send_sem, recv_sem, target):
        away = lambda: pltpu.make_async_remote_copy(
            src_ref=src, dst_ref=dst, send_sem=send_sem, recv_sem=recv_sem,
            device_id=(me_x, target), device_id_type=MESH,
        )
        home = lambda: pltpu.make_async_copy(src, dst, recv_sem)
        return target, away, home

    sums_of = (sum_own, sum_down)
    from_of = (me_x, down)

    def piece(origin, place, count):
        holder = lax.rem(count + me_s // NBR, SUBS) * NBR + lax.rem(row + NBR - place, NBR)
        src, dst = outbox.at[origin, place, count], blocks.at[place, sub, from_of[origin]]
        return sender(
            src, dst, piece_send.at[origin, place, count], piece_recv.at[origin, place], holder
        )

    def spread(origin):
        for place in range(SLOTS):

            def step(count, carry):
                holder, away, home = piece(origin, place, count)
                block = table[place, holder]
                outbox[origin, place, count] = sums_of[origin][lax.rem(jnp.maximum(block, 0), NBC)]

                @pl.when(holder != me_s)
                def _():
                    away().start()

                @pl.when(holder == me_s)
                def _():
                    home().start()

                return carry

            lax.fori_loop(0, SUBS, step, 0)

    def gather_block(slot):
        def one(place, subs, x_from, x):
            ref = blocks.at[slot, subs, x_from]
            return cross(ref, ref, block_send.at[slot, place], block_recv.at[slot, place], x)

        return [
            one(0, pl.ds(0, SUBS), me_x, down),
            one(1, pl.ds(0, SPLIT), down, up),
            one(2, pl.ds(SPLIT, SUBS - SPLIT), up, down),
        ]

    block_copies = [gather_block(slot) for slot in range(SLOTS)]

    def arrive(origin, slot):
        pieces = blocks.at[slot, :, from_of[origin]]
        pltpu.make_async_copy(pieces, pieces, piece_recv.at[origin, slot]).wait()

    def locate(col, carry):
        wanted = row * NBC + col
        index = 0
        for cell in range(CELLS):
            place = cell % SLOTS
            holder = cell // SLOTS * NBR + lax.rem(row + NBR - place, NBR)
            index = jnp.where(table[place, holder] == wanted, cell, index)
        places[col] = index
        return carry

    def add_a(col, carry):
        part_a[col] = (fwd_a[col].astype(f32) + tiles[DOWN, col].astype(f32)).astype(bf16)
        return carry

    def add_b(col, carry):
        part_b[col] = (fwd_b[col].astype(f32) + tiles[UP, CUT + col].astype(f32)).astype(bf16)
        return carry

    def add_all(col, carry):
        sum_own[col] = (
            tiles[OWN, col].astype(f32) + (from_p[col].astype(f32) + from_m[col].astype(f32))
        ).astype(bf16)
        return carry

    loads[0].start()
    loads[1].start()
    fetch_right.start()
    fetch_left_fac.start()
    fetch_right_fac.start()
    hail(me_x, me_s)
    loads[0].wait()
    unpack(OVER, 0, CUT)
    admitted()
    keep.start()
    copies[0].start()
    unpack(OVER, CUT, NBC)
    copies[1].start()
    loads[2].start()
    loads[1].wait()
    unpack(DOWN, 0, NBC)
    copies[2].start()
    loads[3].start()
    loads[2].wait()
    unpack(UP, 0, NBC)
    copies[3].start()
    copies[0].wait_recv()
    lax.fori_loop(0, CUT, add_a, 0)
    copies[4].start()
    copies[1].wait_recv()
    lax.fori_loop(0, NBC - CUT, add_b, 0)
    copies[5].start()
    loads[3].wait()
    unpack(OWN, 0, NBC)
    copies[3].wait_recv()
    copies[4].wait_recv()
    lax.fori_loop(0, CUT, add_all, 0)
    copies[6].start()
    copies[2].wait_recv()
    copies[5].wait_recv()
    lax.fori_loop(CUT, NBC, add_all, 0)
    copies[7].start()
    spread(0)
    start_root(0, 0)
    lax.fori_loop(0, NBC, locate, 0)
    copies[6].wait_recv()
    copies[7].wait_recv()
    spread(1)
    for slot in range(SLOTS):
        arrive(0, slot)
        block_copies[slot][0].start()
    start_root(0, 1)
    start_root(0, 2)
    pass_root(0, 0)
    for slot in range(SLOTS):
        block_copies[slot][0].wait_recv()
        block_copies[slot][2].start()
    pass_root(0, 1)
    pass_root(0, 2)
    for slot in range(SLOTS):
        if slot < SLOTS - 1:
            start_root(1, slot)
        arrive(1, slot)
        block_copies[slot][1].start()
    pass_root(1, 0)
    pass_root(1, 1)

    def target_of(place, count):
        target_sub = lax.rem(3 * count + 3 * sub + 2 * row, SUBS)
        return target_sub, lax.rem(me_s + place, NBR) * SUBS + target_sub

    def back(place, half, count):
        target_sub, target = target_of(place, count)
        return sender(
            raw.at[half, place, target_sub], inbox[half].at[me_s // NBR * SLOTS + place],
            back_send.at[half, place, count], back_recv.at[half], target,
        )

    def tell(place, count):
        target_sub, target = target_of(place, count)
        return sender(
            factors.at[place], factor_box.at[me_s // NBR * SLOTS + place],
            factor_send.at[place, count], factor_recv, target,
        )

    def start_all(describe):
        def step(count, carry):
            target, away, home = describe(count)

            @pl.when(target != me_s)
            def _():
                away().start()

            @pl.when(target == me_s)
            def _():
                home().start()

            return carry

        lax.fori_loop(0, SUBS, step, 0)

    def finish_all(describe):
        def step(count, carry):
            target, away, home = describe(count)

            @pl.when(target != me_s)
            def _():
                away().wait_send()

            return carry

        lax.fori_loop(0, SUBS, step, 0)

    squares = [[] for slot in range(SLOTS)]

    def direct(half, slot):
        for copy in root_copies[half][slot][2:]:
            copy.wait_recv()
        result = jnp.dot(
            roots[slot, :, :, half].reshape(BLK // HALVES, BLK), precond[slot],
            preferred_element_type=f32,
        )
        raw[half, slot] = result.astype(bf16).reshape(SUBS, HROWS, 256)
        start_all(functools.partial(back, slot, half))
        squares[slot].append(jnp.sum(jnp.square(result)))

    shares = []

    def share(slot):
        sums[slot] = jnp.full((8, 128), squares[slot][0] + squares[slot][1], f32)
        for index, x in enumerate((up, down, over)):
            copy = cross(
                sums.at[slot], sum_box.at[slot, index],
                sum_send.at[slot, index], sum_recv.at[slot, index], x,
            )
            copy.start()
            shares.append(copy)

    def graft(slot):
        total = sums[slot] + (sum_box[slot, 0] + sum_box[slot, 1] + sum_box[slot, 2])
        factors[slot] = jnp.sqrt(powers[slot]) / jnp.sqrt(total / (BLK * BLK) + EPSILON)
        start_all(functools.partial(tell, slot))

    def ring(src, dst, group, place, x):
        return cross(src, dst, ring_send.at[group, place], ring_recv.at[group, place], x)

    def links(group):
        mine = gathered.at[me_x, group]
        below, above = gathered.at[down, group, low], gathered.at[up, group, high]
        return [
            ring(mine.at[low], mine.at[low], group, 0, up),
            ring(mine.at[high], mine.at[high], group, 1, down),
            ring(mine.at[high], mine.at[high], group, 2, up),
            ring(mine.at[low], mine.at[low], group, 3, down),
            ring(below, below, group, 4, up),
            ring(above, above, group, 5, down),
        ]

    every = [links(group) for group in range(GROUPS)]

    def statistics(slot):
        whole = blocks[slot].reshape(BLK, BLK)
        scale = jnp.where(table[slot, me_s] >= 0, 1.0 / BLK, 0.0).astype(f32)
        rows = blocks[slot, pl.ds(me_x * 2, 2)].reshape(256, BLK)
        left_box[slot] = left_box[slot] + contract_last(rows, whole) * scale
        start = pl.multiple_of(me_x * 256, 256)
        cols = blocks[slot, :, :, :, pl.ds(start, 256)].reshape(BLK, 256)
        right_fac_box[slot] = (
            right_fac_box[slot] + jnp.dot(cols.T, whole, preferred_element_type=f32) * scale
        )
        for copy in leave(slot):
            copy.start()

    def leave(slot):
        return [
            pltpu.make_async_copy(left_box.at[slot], new_left.at[slot], out_sem.at[slot, 0]),
            pltpu.make_async_copy(right_fac_box.at[slot], new_right.at[slot], out_sem.at[slot, 1]),
        ]

    def forward(group):
        every[group][0].wait_recv()
        every[group][4].start()
        every[group][1].wait_recv()
        every[group][5].start()

    def place_group(group):
        half, first = group // 2, group % 2 * QROWS

        def step(col, carry):
            gathered[me_x, group, col] = inbox[half][places[col], pl.ds(first, QROWS)]
            return carry

        lax.fori_loop(0, NBC, step, 0)

    def ring_group(group):
        for copy in every[group][:4]:
            copy.start()

    def flat_copy(group):
        at = pl.ds(group * size, size)
        return pltpu.make_async_copy(flat.at[group % 2], update.at[:, at], flat_sem.at[group % 2])

    def flatten(group):
        for copy in every[group][2:]:
            copy.wait_recv()
        if group >= 2:
            flat_copy(group - 2).wait()

        def step(col, carry):
            factor = factor_box[places[col]][0:1, :]
            for rows in range(2):
                for part in range(N_X):
                    for lane in range(2):
                        value = gathered[
                            part, group, col, rows * 16 : rows * 16 + 16, lane * 128 : lane * 128 + 128
                        ].astype(f32)
                        mid[rows, pl.ds(part * 2 + lane, 16, STEP), :] = value * factor
            for rows in range(2):
                for line in range(16):
                    at = pl.multiple_of((rows * 16 + line) * COLS + col * BLK, BLK)
                    flat[group % 2, :, pl.ds(at, BLK)] = (
                        mid[rows, line * STEP : line * STEP + 8, :].reshape(1, BLK).astype(bf16)
                    )
            return carry

        lax.fori_loop(0, NBC, step, 0)
        flat_copy(group).start()

    keep.wait()
    fetch_right.wait()
    fetch_left_fac.wait()
    fetch_right_fac.wait()
    powers = []
    for slot in range(SLOTS):
        for copy in block_copies[slot][1:]:
            copy.wait_recv()
        if slot == SLOTS - 1:
            start_root(1, slot)
        grad = blocks[slot].reshape(BLK, BLK)
        precond[slot] = contract_last(grad, right_box[slot]).astype(bf16)
        direct(0, slot)
        if slot == 0:
            statistics(0)
    for slot in range(SLOTS):
        grad = blocks[slot].reshape(BLK, BLK)
        powers.append(jnp.sum(jnp.square(grad.astype(f32))) / (BLK * BLK))
    pltpu.make_async_copy(inbox_0, inbox_0, back_recv.at[0]).wait()
    place_group(0)
    ring_group(0)
    place_group(1)
    pass_root(1, 2)
    direct(1, 0)
    direct(1, 1)
    statistics(1)
    forward(0)
    direct(1, 2)
    ring_group(1)
    for slot in range(SLOTS):
        share(slot)
    pltpu.make_async_copy(inbox_1, inbox_1, back_recv.at[1]).wait()
    place_group(2)
    ring_group(2)
    place_group(3)
    ring_group(3)
    for copy in shares:
        copy.wait_recv()
    for slot in range(SLOTS):
        graft(slot)
    forward(1)
    statistics(2)
    forward(2)
    pltpu.make_async_copy(factor_box, factor_box, factor_recv).wait()
    flatten(0)
    forward(3)
    flatten(1)
    flatten(2)
    flatten(3)
    flat_copy(2).wait()
    flat_copy(3).wait()
    for group in range(GROUPS):
        for copy in every[group]:
            copy.wait_send()
    for copy in shares + copies:
        copy.wait_send()
    for slot in range(SLOTS):
        for half in range(HALVES):
            for copy in root_copies[half][slot]:
                copy.wait_send()
            finish_all(functools.partial(back, slot, half))
        finish_all(functools.partial(tell, slot))
        for origin in range(2):
            finish_all(functools.partial(piece, origin, slot))
        for copy in block_copies[slot]:
            copy.wait_send()
        for copy in leave(slot):
            copy.wait()


def contract_last(a, b):
    return lax.dot_general(a, b, (((1,), (1,)), ((), ())), preferred_element_type=f32)


def on_device(grads, slot_table, left_factor, right_factor, left_root, right_root):
    smem = pl.BlockSpec(memory_space=pltpu.SMEM)
    hbm = pl.BlockSpec(memory_space=pl.ANY)
    dma = pltpu.SemaphoreType.DMA
    vmem = pltpu.VMEM

    new_left, new_right, update = pl.pallas_call(
        shampoo,
        in_specs=[smem] + [hbm] * 5,
        out_specs=[hbm] * 3,
        out_shape=[
            jax.ShapeDtypeStruct((SLOTS, 256, BLK), f32),
            jax.ShapeDtypeStruct((SLOTS, 256, BLK), f32),
            jax.ShapeDtypeStruct((1, 128 * COLS), bf16),
        ],
        scratch_shapes=[
            vmem((2, 1, QROWS * COLS), bf16),
            vmem((2, 16 * STEP, 128), f32),
            vmem((N_X, NBC, QROWS, BLK), bf16),
            vmem((CUT, QROWS, BLK), bf16),
            vmem((NBC - CUT, QROWS, BLK), bf16),
            vmem((CUT, QROWS, BLK), bf16),
            vmem((NBC - CUT, QROWS, BLK), bf16),
        ]
        + [vmem((NBC, QROWS, BLK), bf16)] * 4
        + [
            vmem((2, SLOTS, SUBS, QROWS, BLK), bf16),
            vmem((SLOTS, SUBS, N_X, QROWS, BLK), bf16),
            vmem((SLOTS, N_X, 2, HALVES, HROWS, BLK), bf16),
            vmem((SLOTS, 256, BLK), bf16),
            vmem((SLOTS, BLK, 256), bf16),
            vmem((SLOTS, 8, 128), f32),
            vmem((SLOTS, 3, 8, 128), f32),
            vmem((SLOTS, 8, 128), f32),
            vmem((CELLS, 8, 128), f32),
            vmem((HALVES, SLOTS, SUBS, HROWS, 256), bf16),
            vmem((CELLS, HROWS, 256), bf16),
            vmem((CELLS, HROWS, 256), bf16),
            vmem((N_X, GROUPS, NBC, QROWS, 256), bf16),
            vmem((SLOTS, 256, BLK), f32),
            vmem((SLOTS, 256, BLK), f32),
            pltpu.SMEM((NBC,), jnp.int32),
            dma((2,)),
            dma,
            dma,
            dma((SLOTS, 2)),
            dma((8,)),
            dma((8,)),
            dma((SLOTS, HALVES, 6)),
            dma((SLOTS, HALVES, 6)),
            dma((2,)),
            dma((2, SLOTS, SUBS)),
            dma((2, SLOTS)),
            dma((SLOTS, 3)),
            dma((SLOTS, 3)),
            dma((SLOTS, 3)),
            dma((SLOTS, 3)),
            dma((SLOTS, SUBS)),
            dma,
            dma((HALVES, SLOTS, SUBS)),
            dma((HALVES,)),
            dma((GROUPS, 6)),
            dma((GROUPS, 6)),
        ],
        compiler_params=pltpu.CompilerParams(
            collective_id=0, has_side_effects=True, vmem_limit_bytes=VMEM_BYTES
        ),
        name="shampoo",
    )(slot_table.T, grads, left_root.reshape(SLOTS, 2, HALVES, HROWS, BLK), right_root[0], left_factor[0], right_factor[0])

    shapes = [
        jax.ShapeDtypeStruct((1, 128 * COLS), bf16),
        jax.ShapeDtypeStruct((SLOTS * 256, BLK), f32),
        jax.ShapeDtypeStruct((SLOTS * 256, BLK), f32),
    ]
    flat, new_left, new_right = pl.pallas_call(
        deliver,
        in_specs=[hbm] * 3,
        out_specs=[hbm] * 3,
        out_shape=shapes,
        scratch_shapes=[vmem(shape.shape, shape.dtype) for shape in shapes] + [dma((3, PARTS))] * 2,
        compiler_params=pltpu.CompilerParams(vmem_limit_bytes=VMEM_BYTES),
        name="deliver",
    )(update, new_left.reshape(SLOTS * 256, BLK), new_right.reshape(SLOTS * 256, BLK))
    rows = (1, SLOTS, 256, BLK)
    return new_left.reshape(rows), new_right.reshape(rows), flat


def solution(mesh):
    rows = P("shard", None, "replica", None)
    flat = P("replica", "shard")
    return jax.shard_map(
        on_device,
        mesh=mesh,
        in_specs=(flat, P(), rows, rows, rows, rows),
        out_specs=(rows, rows, flat),
        check_vma=False,
    )
```

```python
import functools

import jax
import jax.numpy as jnp
from jax import lax
from jax.experimental import pallas as pl
from jax.experimental.pallas import tpu as pltpu
from jax.sharding import PartitionSpec as P

ROWS = 4096
COLS = 15360
BLK = 1024
EPSILON = 1e-06

N_X = 4
N_S = 32
SLOTS = 3
NBR = 4
NBC = 15
SUBS = 8
CELLS = 24
QROWS = 32
CUT = 8
GROUPS = 4
MESH = pl.DeviceIdType.MESH
f32 = jnp.float32
bf16 = jnp.bfloat16
VMEM_BYTES = 58 * 1024 * 1024


STEP = 9
HALVES = 2
HROWS = 64
PARTS = 8


def deliver(*refs):
    sources, targets, boxes = refs[:3], refs[3:6], refs[6:9]
    read_sem, write_sem = refs[9:]
    reads, writes = [], []
    for index in range(3):
        for part in range(PARTS):
            if index == 0:
                count = 128 * COLS // PARTS
                at = (slice(None), pl.ds(part * count, count))
            else:
                count = SLOTS * 256 // PARTS
                at = (pl.ds(part * count, count),)
            box = boxes[index].at[at]
            reads.append(pltpu.make_async_copy(sources[index].at[at], box, read_sem.at[index, part]))
            writes.append(pltpu.make_async_copy(box, targets[index].at[at], write_sem.at[index, part]))
    for read in reads:
        read.start()
    for read, write in zip(reads, writes):
        read.wait()
        write.start()
    for write in writes:
        write.wait()


def hail(me_x, me_s):
    barrier = pltpu.get_barrier_semaphore()

    def one(step, carry):
        pl.semaphore_signal(
            barrier, inc=1, device_id=(me_x, lax.rem(me_s + step, N_S)), device_id_type=MESH
        )
        return carry

    lax.fori_loop(1, N_S, one, 0)
    for far in range(1, N_X):
        pl.semaphore_signal(
            barrier, inc=1, device_id=(lax.rem(me_x + far, N_X), me_s), device_id_type=MESH
        )


def admitted():
    pl.semaphore_wait(pltpu.get_barrier_semaphore(), N_S - 1 + N_X - 1)


def shampoo(
    table, grads, left, right, left_fac, right_fac, new_left, new_right, update,
    flat, mid, tiles, fwd_a, fwd_b, part_a, part_b, from_p, from_m,
    sum_own, sum_down, sum_up, outbox, blocks, roots, right_box, precond,
    sums, sum_box, factors, factor_box, raw, inbox_0, inbox_1, gathered, left_box, right_fac_box, places,
    flat_sem, right_sem, keep_sem, out_sem, send, recv, root_send, root_recv,
    fac_sem, piece_send, piece_recv, block_send, block_recv, sum_send, sum_recv, factor_send, factor_recv,
    back_send, back_recv, ring_send, ring_recv,
):
    me_x, me_s = lax.axis_index("replica"), lax.axis_index("shard")
    row, sub = me_s // SUBS, lax.rem(me_s, SUBS)
    up, down, over = lax.rem(me_x + 1, N_X), lax.rem(me_x + 3, N_X), lax.rem(me_x + 2, N_X)
    low, high = pl.ds(0, CUT), pl.ds(CUT, NBC - CUT)
    inbox = (inbox_0, inbox_1)
    OVER, DOWN, UP, OWN = range(4)

    def cross(src, dst, send_sem, recv_sem, x):
        return pltpu.make_async_remote_copy(
            src_ref=src, dst_ref=dst, send_sem=send_sem, recv_sem=recv_sem,
            device_id=(x, me_s), device_id_type=MESH,
        )

    def remote(src, dst, place, x):
        return cross(src, dst, send.at[place], recv.at[place], x)

    copies = [
        remote(tiles.at[OVER, low], fwd_a, 0, down),
        remote(tiles.at[OVER, high], fwd_b, 1, up),
        remote(tiles.at[DOWN, high], from_p.at[high], 2, down),
        remote(tiles.at[UP, low], from_m.at[low], 3, up),
        remote(part_a, from_p.at[low], 4, down),
        remote(part_b, from_m.at[high], 5, up),
        remote(sum_own.at[low], sum_down.at[low], 6, up),
        remote(sum_own.at[high], sum_up.at[high], 7, down),
        remote(sum_own.at[high], sum_down.at[high], 8, up),
        remote(sum_own.at[low], sum_up.at[low], 9, down),
    ]
    def root(slot, half):
        mine, there = left.at[slot], roots.at[slot, me_x]
        below, above = roots.at[slot, down, 0, half], roots.at[slot, up, 1, half]

        def one(place, src, dst, x):
            return cross(
                src, dst, root_send.at[slot, half, place], root_recv.at[slot, half, place], x
            )

        return [
            one(0, mine.at[0, half], there.at[0, half], up),
            one(1, mine.at[1, half], there.at[1, half], down),
            one(2, mine.at[1, half], there.at[1, half], up),
            one(3, mine.at[0, half], there.at[0, half], down),
            one(4, below, below, up),
            one(5, above, above, down),
        ]

    root_copies = [[root(slot, half) for slot in range(SLOTS)] for half in range(HALVES)]

    def start_root(half, slot):
        for copy in root_copies[half][slot][:4]:
            copy.start()

    def pass_root(half, slot):
        for place in range(2):
            root_copies[half][slot][place].wait_recv()
            root_copies[half][slot][place + 4].start()

    keep = pltpu.make_async_copy(left, roots.at[:, me_x], keep_sem)
    fetch_right = pltpu.make_async_copy(right, right_box, right_sem)
    fetch_left_fac = pltpu.make_async_copy(left_fac, left_box, fac_sem.at[0])
    fetch_right_fac = pltpu.make_async_copy(right_fac, right_fac_box, fac_sem.at[1])
    size = QROWS * COLS
    quarters = (over, down, up, me_x)
    loads = [
        pltpu.make_async_copy(
            grads.at[:, pl.ds(pl.multiple_of(quarters[part] * size, size), size)],
            flat.at[part % 2], flat_sem.at[part % 2],
        )
        for part in range(N_X)
    ]

    def unpack(part, first, last):
        def step(col, carry):
            for half in range(2):
                for line in range(16):
                    at = pl.multiple_of((half * 16 + line) * COLS + col * BLK, BLK)
                    mid[half, line * STEP : line * STEP + 8, :] = (
                        flat[part % 2, :, pl.ds(at, BLK)].astype(f32).reshape(8, 128)
                    )
            for half in range(2):
                for lane in range(8):
                    tiles[part, col, half * 16 : half * 16 + 16, lane * 128 : lane * 128 + 128] = (
                        mid[half, pl.ds(lane, 16, STEP), :].astype(bf16)
                    )
            return carry

        lax.fori_loop(first, last, step, 0)

    def sender(src, dst, send_sem, recv_sem, target):
        away = lambda: pltpu.make_async_remote_copy(
            src_ref=src, dst_ref=dst, send_sem=send_sem, recv_sem=recv_sem,
            device_id=(me_x, target), device_id_type=MESH,
        )
        home = lambda: pltpu.make_async_copy(src, dst, recv_sem)
        return target, away, home

    sums_of = (sum_own, sum_down, sum_up)
    from_of = (me_x, down, up)

    def piece(origin, place, count):
        holder = lax.rem(count + me_s // NBR, SUBS) * NBR + lax.rem(row + NBR - place, NBR)
        src, dst = outbox.at[origin, place, count], blocks.at[place, sub, from_of[origin]]
        return sender(
            src, dst, piece_send.at[origin, place, count], piece_recv.at[origin, place], holder
        )

    def spread(origin):
        for place in range(SLOTS):

            def step(count, carry):
                holder, away, home = piece(origin, place, count)
                block = table[place, holder]
                outbox[origin, place, count] = sums_of[origin][lax.rem(jnp.maximum(block, 0), NBC)]

                @pl.when(holder != me_s)
                def _():
                    away().start()

                @pl.when(holder == me_s)
                def _():
                    home().start()

                return carry

            lax.fori_loop(0, SUBS, step, 0)

    def gather_block(slot):
        def one(place, subs, x_from, x):
            ref = blocks.at[slot, subs, x_from]
            return cross(ref, ref, block_send.at[slot, place], block_recv.at[slot, place], x)

        return [one(0, pl.ds(0, 4), down, up), one(1, pl.ds(4, 4), up, down)]

    block_copies = [gather_block(slot) for slot in range(SLOTS)]

    def arrive(origin, slot):
        pieces = blocks.at[slot, :, from_of[origin]]
        pltpu.make_async_copy(pieces, pieces, piece_recv.at[origin, slot]).wait()

    def locate(col, carry):
        wanted = row * NBC + col
        index = 0
        for cell in range(CELLS):
            place = cell % SLOTS
            holder = cell // SLOTS * NBR + lax.rem(row + NBR - place, NBR)
            index = jnp.where(table[place, holder] == wanted, cell, index)
        places[col] = index
        return carry

    def add_a(col, carry):
        part_a[col] = (fwd_a[col].astype(f32) + tiles[DOWN, col].astype(f32)).astype(bf16)
        return carry

    def add_b(col, carry):
        part_b[col] = (fwd_b[col].astype(f32) + tiles[UP, CUT + col].astype(f32)).astype(bf16)
        return carry

    def add_all(col, carry):
        sum_own[col] = (
            tiles[OWN, col].astype(f32) + (from_p[col].astype(f32) + from_m[col].astype(f32))
        ).astype(bf16)
        return carry

    loads[0].start()
    loads[1].start()
    fetch_right.start()
    fetch_left_fac.start()
    fetch_right_fac.start()
    hail(me_x, me_s)
    loads[0].wait()
    unpack(OVER, 0, CUT)
    admitted()
    keep.start()
    copies[0].start()
    unpack(OVER, CUT, NBC)
    copies[1].start()
    loads[2].start()
    loads[1].wait()
    unpack(DOWN, 0, NBC)
    copies[2].start()
    loads[3].start()
    loads[2].wait()
    unpack(UP, 0, NBC)
    copies[3].start()
    copies[0].wait_recv()
    lax.fori_loop(0, CUT, add_a, 0)
    copies[4].start()
    copies[1].wait_recv()
    lax.fori_loop(0, NBC - CUT, add_b, 0)
    copies[5].start()
    loads[3].wait()
    unpack(OWN, 0, NBC)
    copies[3].wait_recv()
    copies[4].wait_recv()
    start_root(0, 0)
    lax.fori_loop(0, CUT, add_all, 0)
    copies[6].start()
    copies[9].start()
    copies[2].wait_recv()
    copies[5].wait_recv()
    lax.fori_loop(CUT, NBC, add_all, 0)
    copies[7].start()
    copies[8].start()
    spread(0)
    start_root(0, 1)
    lax.fori_loop(0, NBC, locate, 0)
    copies[6].wait_recv()
    copies[8].wait_recv()
    spread(1)
    start_root(0, 2)
    copies[7].wait_recv()
    copies[9].wait_recv()
    spread(2)
    for slot in range(SLOTS):
        pass_root(0, slot)
    for slot in range(SLOTS):
        if slot < SLOTS - 1:
            start_root(1, slot)
        arrive(1, slot)
        block_copies[slot][0].start()
        arrive(2, slot)
        block_copies[slot][1].start()
    pass_root(1, 0)
    pass_root(1, 1)

    def target_of(place, count):
        target_sub = lax.rem(3 * count + 3 * sub + 2 * row, SUBS)
        return target_sub, lax.rem(me_s + place, NBR) * SUBS + target_sub

    def back(place, half, count):
        target_sub, target = target_of(place, count)
        return sender(
            raw.at[half, place, target_sub], inbox[half].at[me_s // NBR * SLOTS + place],
            back_send.at[half, place, count], back_recv.at[half], target,
        )

    def tell(place, count):
        target_sub, target = target_of(place, count)
        return sender(
            factors.at[place], factor_box.at[me_s // NBR * SLOTS + place],
            factor_send.at[place, count], factor_recv, target,
        )

    def start_all(describe):
        def step(count, carry):
            target, away, home = describe(count)

            @pl.when(target != me_s)
            def _():
                away().start()

            @pl.when(target == me_s)
            def _():
                home().start()

            return carry

        lax.fori_loop(0, SUBS, step, 0)

    def finish_all(describe):
        def step(count, carry):
            target, away, home = describe(count)

            @pl.when(target != me_s)
            def _():
                away().wait_send()

            return carry

        lax.fori_loop(0, SUBS, step, 0)

    squares = [[] for slot in range(SLOTS)]

    def direct(half, slot):
        for copy in root_copies[half][slot][2:]:
            copy.wait_recv()
        result = jnp.dot(
            roots[slot, :, :, half].reshape(BLK // HALVES, BLK), precond[slot],
            preferred_element_type=f32,
        )
        raw[half, slot] = result.astype(bf16).reshape(SUBS, HROWS, 256)
        start_all(functools.partial(back, slot, half))
        squares[slot].append(jnp.sum(jnp.square(result)))

    shares = []

    def share(slot):
        sums[slot] = jnp.full((8, 128), squares[slot][0] + squares[slot][1], f32)
        for index, x in enumerate((up, down, over)):
            copy = cross(
                sums.at[slot], sum_box.at[slot, index],
                sum_send.at[slot, index], sum_recv.at[slot, index], x,
            )
            copy.start()
            shares.append(copy)

    def graft(slot):
        total = sums[slot] + (sum_box[slot, 0] + sum_box[slot, 1] + sum_box[slot, 2])
        factors[slot] = jnp.sqrt(powers[slot]) / jnp.sqrt(total / (BLK * BLK) + EPSILON)
        start_all(functools.partial(tell, slot))

    def ring(src, dst, group, place, x):
        return cross(src, dst, ring_send.at[group, place], ring_recv.at[group, place], x)

    def links(group):
        mine = gathered.at[me_x, group]
        below, above = gathered.at[down, group, low], gathered.at[up, group, high]
        return [
            ring(mine.at[low], mine.at[low], group, 0, up),
            ring(mine.at[high], mine.at[high], group, 1, down),
            ring(mine.at[high], mine.at[high], group, 2, up),
            ring(mine.at[low], mine.at[low], group, 3, down),
            ring(below, below, group, 4, up),
            ring(above, above, group, 5, down),
        ]

    every = [links(group) for group in range(GROUPS)]

    def statistics(slot):
        whole = blocks[slot].reshape(BLK, BLK)
        scale = jnp.where(table[slot, me_s] >= 0, 1.0 / BLK, 0.0).astype(f32)
        rows = blocks[slot, pl.ds(me_x * 2, 2)].reshape(256, BLK)
        left_box[slot] = left_box[slot] + contract_last(rows, whole) * scale
        start = pl.multiple_of(me_x * 256, 256)
        cols = blocks[slot, :, :, :, pl.ds(start, 256)].reshape(BLK, 256)
        right_fac_box[slot] = (
            right_fac_box[slot] + jnp.dot(cols.T, whole, preferred_element_type=f32) * scale
        )
        for copy in leave(slot):
            copy.start()

    def leave(slot):
        return [
            pltpu.make_async_copy(left_box.at[slot], new_left.at[slot], out_sem.at[slot, 0]),
            pltpu.make_async_copy(right_fac_box.at[slot], new_right.at[slot], out_sem.at[slot, 1]),
        ]

    def forward(group):
        every[group][0].wait_recv()
        every[group][4].start()
        every[group][1].wait_recv()
        every[group][5].start()

    def place_group(group):
        half, first = group // 2, group % 2 * QROWS

        def step(col, carry):
            gathered[me_x, group, col] = inbox[half][places[col], pl.ds(first, QROWS)]
            return carry

        lax.fori_loop(0, NBC, step, 0)

    def ring_group(group):
        for copy in every[group][:4]:
            copy.start()

    def flat_copy(group):
        at = pl.ds(group * size, size)
        return pltpu.make_async_copy(flat.at[group % 2], update.at[:, at], flat_sem.at[group % 2])

    def flatten(group):
        for copy in every[group][2:]:
            copy.wait_recv()
        if group >= 2:
            flat_copy(group - 2).wait()

        def step(col, carry):
            factor = factor_box[places[col]][0:1, :]
            for rows in range(2):
                for part in range(N_X):
                    for lane in range(2):
                        value = gathered[
                            part, group, col, rows * 16 : rows * 16 + 16, lane * 128 : lane * 128 + 128
                        ].astype(f32)
                        mid[rows, pl.ds(part * 2 + lane, 16, STEP), :] = value * factor
            for rows in range(2):
                for line in range(16):
                    at = pl.multiple_of((rows * 16 + line) * COLS + col * BLK, BLK)
                    flat[group % 2, :, pl.ds(at, BLK)] = (
                        mid[rows, line * STEP : line * STEP + 8, :].reshape(1, BLK).astype(bf16)
                    )
            return carry

        lax.fori_loop(0, NBC, step, 0)
        flat_copy(group).start()

    keep.wait()
    fetch_right.wait()
    fetch_left_fac.wait()
    fetch_right_fac.wait()
    powers = []
    for slot in range(SLOTS):
        arrive(0, slot)
        for copy in block_copies[slot]:
            copy.wait_recv()
        if slot == SLOTS - 1:
            start_root(1, slot)
        grad = blocks[slot].reshape(BLK, BLK)
        precond[slot] = contract_last(grad, right_box[slot]).astype(bf16)
        direct(0, slot)
        if slot == 0:
            statistics(0)
    for slot in range(SLOTS):
        grad = blocks[slot].reshape(BLK, BLK)
        powers.append(jnp.sum(jnp.square(grad.astype(f32))) / (BLK * BLK))
    pltpu.make_async_copy(inbox_0, inbox_0, back_recv.at[0]).wait()
    place_group(0)
    ring_group(0)
    place_group(1)
    pass_root(1, 2)
    ring_group(1)
    direct(1, 0)
    direct(1, 1)
    forward(0)
    direct(1, 2)
    for slot in range(SLOTS):
        share(slot)
    pltpu.make_async_copy(inbox_1, inbox_1, back_recv.at[1]).wait()
    place_group(2)
    ring_group(2)
    place_group(3)
    ring_group(3)
    for copy in shares:
        copy.wait_recv()
    for slot in range(SLOTS):
        graft(slot)
    forward(1)
    statistics(1)
    forward(2)
    statistics(2)
    pltpu.make_async_copy(factor_box, factor_box, factor_recv).wait()
    flatten(0)
    forward(3)
    flatten(1)
    flatten(2)
    flatten(3)
    flat_copy(2).wait()
    flat_copy(3).wait()
    for group in range(GROUPS):
        for copy in every[group]:
            copy.wait_send()
    for copy in shares + copies:
        copy.wait_send()
    for slot in range(SLOTS):
        for half in range(HALVES):
            for copy in root_copies[half][slot]:
                copy.wait_send()
            finish_all(functools.partial(back, slot, half))
        finish_all(functools.partial(tell, slot))
        for origin in range(3):
            finish_all(functools.partial(piece, origin, slot))
        for copy in block_copies[slot]:
            copy.wait_send()
        for copy in leave(slot):
            copy.wait()


def contract_last(a, b):
    return lax.dot_general(a, b, (((1,), (1,)), ((), ())), preferred_element_type=f32)


def on_device(grads, slot_table, left_factor, right_factor, left_root, right_root):
    smem = pl.BlockSpec(memory_space=pltpu.SMEM)
    hbm = pl.BlockSpec(memory_space=pl.ANY)
    dma = pltpu.SemaphoreType.DMA
    vmem = pltpu.VMEM

    new_left, new_right, update = pl.pallas_call(
        shampoo,
        in_specs=[smem] + [hbm] * 5,
        out_specs=[hbm] * 3,
        out_shape=[
            jax.ShapeDtypeStruct((SLOTS, 256, BLK), f32),
            jax.ShapeDtypeStruct((SLOTS, 256, BLK), f32),
            jax.ShapeDtypeStruct((1, 128 * COLS), bf16),
        ],
        scratch_shapes=[
            vmem((2, 1, QROWS * COLS), bf16),
            vmem((2, 16 * STEP, 128), f32),
            vmem((N_X, NBC, QROWS, BLK), bf16),
            vmem((CUT, QROWS, BLK), bf16),
            vmem((NBC - CUT, QROWS, BLK), bf16),
            vmem((CUT, QROWS, BLK), bf16),
            vmem((NBC - CUT, QROWS, BLK), bf16),
        ]
        + [vmem((NBC, QROWS, BLK), bf16)] * 5
        + [
            vmem((3, SLOTS, SUBS, QROWS, BLK), bf16),
            vmem((SLOTS, SUBS, N_X, QROWS, BLK), bf16),
            vmem((SLOTS, N_X, 2, HALVES, HROWS, BLK), bf16),
            vmem((SLOTS, 256, BLK), bf16),
            vmem((SLOTS, BLK, 256), bf16),
            vmem((SLOTS, 8, 128), f32),
            vmem((SLOTS, 3, 8, 128), f32),
            vmem((SLOTS, 8, 128), f32),
            vmem((CELLS, 8, 128), f32),
            vmem((HALVES, SLOTS, SUBS, HROWS, 256), bf16),
            vmem((CELLS, HROWS, 256), bf16),
            vmem((CELLS, HROWS, 256), bf16),
            vmem((N_X, GROUPS, NBC, QROWS, 256), bf16),
            vmem((SLOTS, 256, BLK), f32),
            vmem((SLOTS, 256, BLK), f32),
            pltpu.SMEM((NBC,), jnp.int32),
            dma((2,)),
            dma,
            dma,
            dma((SLOTS, 2)),
            dma((10,)),
            dma((10,)),
            dma((SLOTS, HALVES, 6)),
            dma((SLOTS, HALVES, 6)),
            dma((2,)),
            dma((3, SLOTS, SUBS)),
            dma((3, SLOTS)),
            dma((SLOTS, 2)),
            dma((SLOTS, 2)),
            dma((SLOTS, 3)),
            dma((SLOTS, 3)),
            dma((SLOTS, SUBS)),
            dma,
            dma((HALVES, SLOTS, SUBS)),
            dma((HALVES,)),
            dma((GROUPS, 6)),
            dma((GROUPS, 6)),
        ],
        compiler_params=pltpu.CompilerParams(
            collective_id=0, has_side_effects=True, vmem_limit_bytes=VMEM_BYTES
        ),
        name="shampoo",
    )(slot_table.T, grads, left_root.reshape(SLOTS, 2, HALVES, HROWS, BLK), right_root[0], left_factor[0], right_factor[0])

    shapes = [
        jax.ShapeDtypeStruct((1, 128 * COLS), bf16),
        jax.ShapeDtypeStruct((SLOTS * 256, BLK), f32),
        jax.ShapeDtypeStruct((SLOTS * 256, BLK), f32),
    ]
    flat, new_left, new_right = pl.pallas_call(
        deliver,
        in_specs=[hbm] * 3,
        out_specs=[hbm] * 3,
        out_shape=shapes,
        scratch_shapes=[vmem(shape.shape, shape.dtype) for shape in shapes] + [dma((3, PARTS))] * 2,
        compiler_params=pltpu.CompilerParams(vmem_limit_bytes=VMEM_BYTES),
        name="deliver",
    )(update, new_left.reshape(SLOTS * 256, BLK), new_right.reshape(SLOTS * 256, BLK))
    rows = (1, SLOTS, 256, BLK)
    return new_left.reshape(rows), new_right.reshape(rows), flat


def solution(mesh):
    rows = P("shard", None, "replica", None)
    flat = P("replica", "shard")
    return jax.shard_map(
        on_device,
        mesh=mesh,
        in_specs=(flat, P(), rows, rows, rows, rows),
        out_specs=(rows, rows, flat),
        check_vma=False,
    )
```

```python
import functools

import jax
import jax.numpy as jnp
from jax import lax
from jax.experimental import pallas as pl
from jax.experimental.pallas import tpu as pltpu
from jax.sharding import PartitionSpec as P

ROWS = 4096
COLS = 15360
BLK = 1024
EPSILON = 1e-06

N_X = 4
N_S = 32
SLOTS = 3
NBR = 4
NBC = 15
SUBS = 8
CELLS = 24
QROWS = 32
CUT = 8
GROUPS = 4
MESH = pl.DeviceIdType.MESH
f32 = jnp.float32
bf16 = jnp.bfloat16
VMEM_BYTES = 58 * 1024 * 1024


STEP = 9
HALVES = 2
HROWS = 64
PARTS = 8


def deliver(*refs):
    sources, targets, boxes = refs[:3], refs[3:6], refs[6:9]
    read_sem, write_sem = refs[9:]
    reads, writes = [], []
    for index in range(3):
        for part in range(PARTS):
            if index == 0:
                count = 128 * COLS // PARTS
                at = (slice(None), pl.ds(part * count, count))
            else:
                count = SLOTS * 256 // PARTS
                at = (pl.ds(part * count, count),)
            box = boxes[index].at[at]
            reads.append(pltpu.make_async_copy(sources[index].at[at], box, read_sem.at[index, part]))
            writes.append(pltpu.make_async_copy(box, targets[index].at[at], write_sem.at[index, part]))
    for read in reads:
        read.start()
    for read, write in zip(reads, writes):
        read.wait()
        write.start()
    for write in writes:
        write.wait()


def hail(me_x, me_s):
    barrier = pltpu.get_barrier_semaphore()

    def one(step, carry):
        pl.semaphore_signal(
            barrier, inc=1, device_id=(me_x, lax.rem(me_s + step, N_S)), device_id_type=MESH
        )
        return carry

    lax.fori_loop(1, N_S, one, 0)
    for far in range(1, N_X):
        pl.semaphore_signal(
            barrier, inc=1, device_id=(lax.rem(me_x + far, N_X), me_s), device_id_type=MESH
        )


def admitted():
    pl.semaphore_wait(pltpu.get_barrier_semaphore(), N_S - 1 + N_X - 1)


def shampoo(
    table, grads, left, right, left_fac, right_fac, new_left, new_right, update,
    flat, mid, tiles, fwd_a, fwd_b, part_a, part_b, from_p, from_m,
    sum_own, sum_down, sum_up, outbox, blocks, roots, right_box, precond,
    sums, sum_box, factors, factor_box, raw, inbox_0, inbox_1, gathered, left_box, right_fac_box, places,
    flat_sem, right_sem, keep_sem, out_sem, send, recv, root_send, root_recv,
    fac_sem, piece_send, piece_recv, block_send, block_recv, sum_send, sum_recv, factor_send, factor_recv,
    back_send, back_recv, ring_send, ring_recv,
):
    me_x, me_s = lax.axis_index("replica"), lax.axis_index("shard")
    row, sub = me_s // SUBS, lax.rem(me_s, SUBS)
    up, down, over = lax.rem(me_x + 1, N_X), lax.rem(me_x + 3, N_X), lax.rem(me_x + 2, N_X)
    low, high = pl.ds(0, CUT), pl.ds(CUT, NBC - CUT)
    inbox = (inbox_0, inbox_1)
    OVER, DOWN, UP, OWN = range(4)

    def cross(src, dst, send_sem, recv_sem, x):
        return pltpu.make_async_remote_copy(
            src_ref=src, dst_ref=dst, send_sem=send_sem, recv_sem=recv_sem,
            device_id=(x, me_s), device_id_type=MESH,
        )

    def remote(src, dst, place, x):
        return cross(src, dst, send.at[place], recv.at[place], x)

    copies = [
        remote(tiles.at[OVER, low], fwd_a, 0, down),
        remote(tiles.at[OVER, high], fwd_b, 1, up),
        remote(tiles.at[DOWN, high], from_p.at[high], 2, down),
        remote(tiles.at[UP, low], from_m.at[low], 3, up),
        remote(part_a, from_p.at[low], 4, down),
        remote(part_b, from_m.at[high], 5, up),
        remote(sum_own.at[low], sum_down.at[low], 6, up),
        remote(sum_own.at[high], sum_up.at[high], 7, down),
        remote(sum_own.at[high], sum_down.at[high], 8, up),
        remote(sum_own.at[low], sum_up.at[low], 9, down),
    ]
    def root(slot, half):
        mine, there = left.at[slot], roots.at[slot, me_x]
        below, above = roots.at[slot, down, 0, half], roots.at[slot, up, 1, half]

        def one(place, src, dst, x):
            return cross(
                src, dst, root_send.at[slot, half, place], root_recv.at[slot, half, place], x
            )

        return [
            one(0, mine.at[0, half], there.at[0, half], up),
            one(1, mine.at[1, half], there.at[1, half], down),
            one(2, mine.at[1, half], there.at[1, half], up),
            one(3, mine.at[0, half], there.at[0, half], down),
            one(4, below, below, up),
            one(5, above, above, down),
        ]

    root_copies = [[root(slot, half) for slot in range(SLOTS)] for half in range(HALVES)]

    def start_root(half, slot):
        for copy in root_copies[half][slot][:4]:
            copy.start()

    def pass_root(half, slot):
        for place in range(2):
            root_copies[half][slot][place].wait_recv()
            root_copies[half][slot][place + 4].start()

    keep = pltpu.make_async_copy(left, roots.at[:, me_x], keep_sem)
    fetch_right = pltpu.make_async_copy(right, right_box, right_sem)
    fetch_left_fac = pltpu.make_async_copy(left_fac, left_box, fac_sem.at[0])
    fetch_right_fac = pltpu.make_async_copy(right_fac, right_fac_box, fac_sem.at[1])
    size = QROWS * COLS
    quarters = (over, down, up, me_x)
    loads = [
        pltpu.make_async_copy(
            grads.at[:, pl.ds(pl.multiple_of(quarters[part] * size, size), size)],
            flat.at[part % 2], flat_sem.at[part % 2],
        )
        for part in range(N_X)
    ]

    def unpack(part, first, last):
        def step(col, carry):
            for half in range(2):
                for line in range(16):
                    at = pl.multiple_of((half * 16 + line) * COLS + col * BLK, BLK)
                    mid[half, line * STEP : line * STEP + 8, :] = (
                        flat[part % 2, :, pl.ds(at, BLK)].astype(f32).reshape(8, 128)
                    )
            for half in range(2):
                for lane in range(8):
                    tiles[part, col, half * 16 : half * 16 + 16, lane * 128 : lane * 128 + 128] = (
                        mid[half, pl.ds(lane, 16, STEP), :].astype(bf16)
                    )
            return carry

        lax.fori_loop(first, last, step, 0)

    def sender(src, dst, send_sem, recv_sem, target):
        away = lambda: pltpu.make_async_remote_copy(
            src_ref=src, dst_ref=dst, send_sem=send_sem, recv_sem=recv_sem,
            device_id=(me_x, target), device_id_type=MESH,
        )
        home = lambda: pltpu.make_async_copy(src, dst, recv_sem)
        return target, away, home

    sums_of = (sum_own, sum_down, sum_up)
    from_of = (me_x, down, up)

    def piece(origin, place, count):
        holder = lax.rem(count + me_s // NBR, SUBS) * NBR + lax.rem(row + NBR - place, NBR)
        src, dst = outbox.at[origin, place, count], blocks.at[place, sub, from_of[origin]]
        return sender(
            src, dst, piece_send.at[origin, place, count], piece_recv.at[origin, place], holder
        )

    def spread(origin):
        for place in range(SLOTS):

            def step(count, carry):
                holder, away, home = piece(origin, place, count)
                block = table[place, holder]
                outbox[origin, place, count] = sums_of[origin][lax.rem(jnp.maximum(block, 0), NBC)]

                @pl.when(holder != me_s)
                def _():
                    away().start()

                @pl.when(holder == me_s)
                def _():
                    home().start()

                return carry

            lax.fori_loop(0, SUBS, step, 0)

    def gather_block(slot):
        def one(place, subs, x_from, x):
            ref = blocks.at[slot, subs, x_from]
            return cross(ref, ref, block_send.at[slot, place], block_recv.at[slot, place], x)

        return [one(0, pl.ds(0, 4), down, up), one(1, pl.ds(4, 4), up, down)]

    block_copies = [gather_block(slot) for slot in range(SLOTS)]

    def arrive(origin, slot):
        pieces = blocks.at[slot, :, from_of[origin]]
        pltpu.make_async_copy(pieces, pieces, piece_recv.at[origin, slot]).wait()

    def locate(col, carry):
        wanted = row * NBC + col
        index = 0
        for cell in range(CELLS):
            place = cell % SLOTS
            holder = cell // SLOTS * NBR + lax.rem(row + NBR - place, NBR)
            index = jnp.where(table[place, holder] == wanted, cell, index)
        places[col] = index
        return carry

    def add_a(col, carry):
        part_a[col] = (fwd_a[col].astype(f32) + tiles[DOWN, col].astype(f32)).astype(bf16)
        return carry

    def add_b(col, carry):
        part_b[col] = (fwd_b[col].astype(f32) + tiles[UP, CUT + col].astype(f32)).astype(bf16)
        return carry

    def add_all(col, carry):
        sum_own[col] = (
            tiles[OWN, col].astype(f32) + (from_p[col].astype(f32) + from_m[col].astype(f32))
        ).astype(bf16)
        return carry

    loads[0].start()
    loads[1].start()
    fetch_right.start()
    fetch_left_fac.start()
    fetch_right_fac.start()
    hail(me_x, me_s)
    loads[0].wait()
    unpack(OVER, 0, CUT)
    admitted()
    keep.start()
    copies[0].start()
    unpack(OVER, CUT, NBC)
    copies[1].start()
    loads[2].start()
    loads[1].wait()
    unpack(DOWN, 0, NBC)
    copies[2].start()
    loads[3].start()
    loads[2].wait()
    unpack(UP, 0, NBC)
    copies[3].start()
    copies[0].wait_recv()
    lax.fori_loop(0, CUT, add_a, 0)
    copies[4].start()
    copies[1].wait_recv()
    lax.fori_loop(0, NBC - CUT, add_b, 0)
    copies[5].start()
    loads[3].wait()
    unpack(OWN, 0, NBC)
    copies[3].wait_recv()
    copies[4].wait_recv()
    lax.fori_loop(0, CUT, add_all, 0)
    copies[6].start()
    copies[9].start()
    copies[2].wait_recv()
    copies[5].wait_recv()
    lax.fori_loop(CUT, NBC, add_all, 0)
    copies[7].start()
    copies[8].start()
    spread(0)
    lax.fori_loop(0, NBC, locate, 0)
    copies[6].wait_recv()
    copies[8].wait_recv()
    start_root(0, 0)
    spread(1)
    copies[7].wait_recv()
    copies[9].wait_recv()
    start_root(0, 1)
    spread(2)
    start_root(0, 2)
    for slot in range(SLOTS):
        pass_root(0, slot)
    for slot in range(SLOTS):
        if slot < SLOTS - 1:
            start_root(1, slot)
        arrive(1, slot)
        block_copies[slot][0].start()
        arrive(2, slot)
        block_copies[slot][1].start()
    pass_root(1, 0)
    pass_root(1, 1)

    def target_of(place, count):
        target_sub = lax.rem(3 * count + 3 * sub + 2 * row, SUBS)
        return target_sub, lax.rem(me_s + place, NBR) * SUBS + target_sub

    def back(place, half, count):
        target_sub, target = target_of(place, count)
        return sender(
            raw.at[half, place, target_sub], inbox[half].at[me_s // NBR * SLOTS + place],
            back_send.at[half, place, count], back_recv.at[half], target,
        )

    def tell(place, count):
        target_sub, target = target_of(place, count)
        return sender(
            factors.at[place], factor_box.at[me_s // NBR * SLOTS + place],
            factor_send.at[place, count], factor_recv, target,
        )

    def start_all(describe):
        def step(count, carry):
            target, away, home = describe(count)

            @pl.when(target != me_s)
            def _():
                away().start()

            @pl.when(target == me_s)
            def _():
                home().start()

            return carry

        lax.fori_loop(0, SUBS, step, 0)

    def finish_all(describe):
        def step(count, carry):
            target, away, home = describe(count)

            @pl.when(target != me_s)
            def _():
                away().wait_send()

            return carry

        lax.fori_loop(0, SUBS, step, 0)

    squares = [[] for slot in range(SLOTS)]

    def direct(half, slot):
        for copy in root_copies[half][slot][2:]:
            copy.wait_recv()
        result = jnp.dot(
            roots[slot, :, :, half].reshape(BLK // HALVES, BLK), precond[slot],
            preferred_element_type=f32,
        )
        raw[half, slot] = result.astype(bf16).reshape(SUBS, HROWS, 256)
        start_all(functools.partial(back, slot, half))
        squares[slot].append(jnp.sum(jnp.square(result)))

    shares = []

    def share(slot):
        sums[slot] = jnp.full((8, 128), squares[slot][0] + squares[slot][1], f32)
        for index, x in enumerate((up, down, over)):
            copy = cross(
                sums.at[slot], sum_box.at[slot, index],
                sum_send.at[slot, index], sum_recv.at[slot, index], x,
            )
            copy.start()
            shares.append(copy)

    def graft(slot):
        total = sums[slot] + (sum_box[slot, 0] + sum_box[slot, 1] + sum_box[slot, 2])
        factors[slot] = jnp.sqrt(powers[slot]) / jnp.sqrt(total / (BLK * BLK) + EPSILON)
        start_all(functools.partial(tell, slot))

    def ring(src, dst, group, place, x):
        return cross(src, dst, ring_send.at[group, place], ring_recv.at[group, place], x)

    def links(group):
        mine = gathered.at[me_x, group]
        below, above = gathered.at[down, group, low], gathered.at[up, group, high]
        return [
            ring(mine.at[low], mine.at[low], group, 0, up),
            ring(mine.at[high], mine.at[high], group, 1, down),
            ring(mine.at[high], mine.at[high], group, 2, up),
            ring(mine.at[low], mine.at[low], group, 3, down),
            ring(below, below, group, 4, up),
            ring(above, above, group, 5, down),
        ]

    every = [links(group) for group in range(GROUPS)]

    def statistics(slot):
        whole = blocks[slot].reshape(BLK, BLK)
        scale = jnp.where(table[slot, me_s] >= 0, 1.0 / BLK, 0.0).astype(f32)
        rows = blocks[slot, pl.ds(me_x * 2, 2)].reshape(256, BLK)
        left_box[slot] = left_box[slot] + contract_last(rows, whole) * scale
        start = pl.multiple_of(me_x * 256, 256)
        cols = blocks[slot, :, :, :, pl.ds(start, 256)].reshape(BLK, 256)
        right_fac_box[slot] = (
            right_fac_box[slot] + jnp.dot(cols.T, whole, preferred_element_type=f32) * scale
        )
        for copy in leave(slot):
            copy.start()

    def leave(slot):
        return [
            pltpu.make_async_copy(left_box.at[slot], new_left.at[slot], out_sem.at[slot, 0]),
            pltpu.make_async_copy(right_fac_box.at[slot], new_right.at[slot], out_sem.at[slot, 1]),
        ]

    def forward(group):
        every[group][0].wait_recv()
        every[group][4].start()
        every[group][1].wait_recv()
        every[group][5].start()

    def place_group(group):
        half, first = group // 2, group % 2 * QROWS

        def step(col, carry):
            gathered[me_x, group, col] = inbox[half][places[col], pl.ds(first, QROWS)]
            return carry

        lax.fori_loop(0, NBC, step, 0)

    def ring_group(group):
        for copy in every[group][:4]:
            copy.start()

    def flat_copy(group):
        at = pl.ds(group * size, size)
        return pltpu.make_async_copy(flat.at[group % 2], update.at[:, at], flat_sem.at[group % 2])

    def flatten(group):
        for copy in every[group][2:]:
            copy.wait_recv()
        if group >= 2:
            flat_copy(group - 2).wait()

        def step(col, carry):
            factor = factor_box[places[col]][0:1, :]
            for rows in range(2):
                for part in range(N_X):
                    for lane in range(2):
                        value = gathered[
                            part, group, col, rows * 16 : rows * 16 + 16, lane * 128 : lane * 128 + 128
                        ].astype(f32)
                        mid[rows, pl.ds(part * 2 + lane, 16, STEP), :] = value * factor
            for rows in range(2):
                for line in range(16):
                    at = pl.multiple_of((rows * 16 + line) * COLS + col * BLK, BLK)
                    flat[group % 2, :, pl.ds(at, BLK)] = (
                        mid[rows, line * STEP : line * STEP + 8, :].reshape(1, BLK).astype(bf16)
                    )
            return carry

        lax.fori_loop(0, NBC, step, 0)
        flat_copy(group).start()

    keep.wait()
    fetch_right.wait()
    fetch_left_fac.wait()
    fetch_right_fac.wait()
    powers = []
    for slot in range(SLOTS):
        arrive(0, slot)
        for copy in block_copies[slot]:
            copy.wait_recv()
        if slot == SLOTS - 1:
            start_root(1, slot)
        grad = blocks[slot].reshape(BLK, BLK)
        precond[slot] = contract_last(grad, right_box[slot]).astype(bf16)
        direct(0, slot)
        if slot != 1:
            statistics(slot)
    for slot in range(SLOTS):
        grad = blocks[slot].reshape(BLK, BLK)
        powers.append(jnp.sum(jnp.square(grad.astype(f32))) / (BLK * BLK))
    pltpu.make_async_copy(inbox_0, inbox_0, back_recv.at[0]).wait()
    place_group(0)
    ring_group(0)
    place_group(1)
    pass_root(1, 2)
    ring_group(1)
    direct(1, 0)
    direct(1, 1)
    forward(0)
    direct(1, 2)
    for slot in range(SLOTS):
        share(slot)
    statistics(1)
    pltpu.make_async_copy(inbox_1, inbox_1, back_recv.at[1]).wait()
    place_group(2)
    ring_group(2)
    place_group(3)
    ring_group(3)
    for copy in shares:
        copy.wait_recv()
    for slot in range(SLOTS):
        graft(slot)
    forward(1)
    pltpu.make_async_copy(factor_box, factor_box, factor_recv).wait()
    flatten(0)
    forward(2)
    flatten(1)
    forward(3)
    flatten(2)
    flatten(3)
    flat_copy(2).wait()
    flat_copy(3).wait()
    for group in range(GROUPS):
        for copy in every[group]:
            copy.wait_send()
    for copy in shares + copies:
        copy.wait_send()
    for slot in range(SLOTS):
        for half in range(HALVES):
            for copy in root_copies[half][slot]:
                copy.wait_send()
            finish_all(functools.partial(back, slot, half))
        finish_all(functools.partial(tell, slot))
        for origin in range(3):
            finish_all(functools.partial(piece, origin, slot))
        for copy in block_copies[slot]:
            copy.wait_send()
        for copy in leave(slot):
            copy.wait()


def contract_last(a, b):
    return lax.dot_general(a, b, (((1,), (1,)), ((), ())), preferred_element_type=f32)


def on_device(grads, slot_table, left_factor, right_factor, left_root, right_root):
    smem = pl.BlockSpec(memory_space=pltpu.SMEM)
    hbm = pl.BlockSpec(memory_space=pl.ANY)
    dma = pltpu.SemaphoreType.DMA
    vmem = pltpu.VMEM

    new_left, new_right, update = pl.pallas_call(
        shampoo,
        in_specs=[smem] + [hbm] * 5,
        out_specs=[hbm] * 3,
        out_shape=[
            jax.ShapeDtypeStruct((SLOTS, 256, BLK), f32),
            jax.ShapeDtypeStruct((SLOTS, 256, BLK), f32),
            jax.ShapeDtypeStruct((1, 128 * COLS), bf16),
        ],
        scratch_shapes=[
            vmem((2, 1, QROWS * COLS), bf16),
            vmem((2, 16 * STEP, 128), f32),
            vmem((N_X, NBC, QROWS, BLK), bf16),
            vmem((CUT, QROWS, BLK), bf16),
            vmem((NBC - CUT, QROWS, BLK), bf16),
            vmem((CUT, QROWS, BLK), bf16),
            vmem((NBC - CUT, QROWS, BLK), bf16),
        ]
        + [vmem((NBC, QROWS, BLK), bf16)] * 5
        + [
            vmem((3, SLOTS, SUBS, QROWS, BLK), bf16),
            vmem((SLOTS, SUBS, N_X, QROWS, BLK), bf16),
            vmem((SLOTS, N_X, 2, HALVES, HROWS, BLK), bf16),
            vmem((SLOTS, 256, BLK), bf16),
            vmem((SLOTS, BLK, 256), bf16),
            vmem((SLOTS, 8, 128), f32),
            vmem((SLOTS, 3, 8, 128), f32),
            vmem((SLOTS, 8, 128), f32),
            vmem((CELLS, 8, 128), f32),
            vmem((HALVES, SLOTS, SUBS, HROWS, 256), bf16),
            vmem((CELLS, HROWS, 256), bf16),
            vmem((CELLS, HROWS, 256), bf16),
            vmem((N_X, GROUPS, NBC, QROWS, 256), bf16),
            vmem((SLOTS, 256, BLK), f32),
            vmem((SLOTS, 256, BLK), f32),
            pltpu.SMEM((NBC,), jnp.int32),
            dma((2,)),
            dma,
            dma,
            dma((SLOTS, 2)),
            dma((10,)),
            dma((10,)),
            dma((SLOTS, HALVES, 6)),
            dma((SLOTS, HALVES, 6)),
            dma((2,)),
            dma((3, SLOTS, SUBS)),
            dma((3, SLOTS)),
            dma((SLOTS, 2)),
            dma((SLOTS, 2)),
            dma((SLOTS, 3)),
            dma((SLOTS, 3)),
            dma((SLOTS, SUBS)),
            dma,
            dma((HALVES, SLOTS, SUBS)),
            dma((HALVES,)),
            dma((GROUPS, 6)),
            dma((GROUPS, 6)),
        ],
        compiler_params=pltpu.CompilerParams(
            collective_id=0, has_side_effects=True, vmem_limit_bytes=VMEM_BYTES
        ),
        name="shampoo",
    )(slot_table.T, grads, left_root.reshape(SLOTS, 2, HALVES, HROWS, BLK), right_root[0], left_factor[0], right_factor[0])

    shapes = [
        jax.ShapeDtypeStruct((1, 128 * COLS), bf16),
        jax.ShapeDtypeStruct((SLOTS * 256, BLK), f32),
        jax.ShapeDtypeStruct((SLOTS * 256, BLK), f32),
    ]
    flat, new_left, new_right = pl.pallas_call(
        deliver,
        in_specs=[hbm] * 3,
        out_specs=[hbm] * 3,
        out_shape=shapes,
        scratch_shapes=[vmem(shape.shape, shape.dtype) for shape in shapes] + [dma((3, PARTS))] * 2,
        compiler_params=pltpu.CompilerParams(vmem_limit_bytes=VMEM_BYTES),
        name="deliver",
    )(update, new_left.reshape(SLOTS * 256, BLK), new_right.reshape(SLOTS * 256, BLK))
    rows = (1, SLOTS, 256, BLK)
    return new_left.reshape(rows), new_right.reshape(rows), flat


def solution(mesh):
    rows = P("shard", None, "replica", None)
    flat = P("replica", "shard")
    return jax.shard_map(
        on_device,
        mesh=mesh,
        in_specs=(flat, P(), rows, rows, rows, rows),
        out_specs=(rows, rows, flat),
        check_vma=False,
    )
```

```python
import functools

import jax
import jax.numpy as jnp
from jax import lax
from jax.experimental import pallas as pl
from jax.experimental.pallas import tpu as pltpu
from jax.sharding import PartitionSpec as P

ROWS = 4096
COLS = 15360
BLK = 1024
EPSILON = 1e-06

N_X = 4
N_S = 32
SLOTS = 3
NBR = 4
NBC = 15
SUBS = 8
CELLS = 24
QROWS = 32
CUT = 8
GROUPS = 4
MESH = pl.DeviceIdType.MESH
f32 = jnp.float32
bf16 = jnp.bfloat16
VMEM_BYTES = 58 * 1024 * 1024


STEP = 9
HALVES = 2
HROWS = 64
PARTS = 8


def deliver(*refs):
    sources, targets, boxes = refs[:3], refs[3:6], refs[6:9]
    read_sem, write_sem = refs[9:]
    reads, writes = [], []
    for index in range(3):
        for part in range(PARTS):
            if index == 0:
                count = 128 * COLS // PARTS
                at = (slice(None), pl.ds(part * count, count))
            else:
                count = SLOTS * 256 // PARTS
                at = (pl.ds(part * count, count),)
            box = boxes[index].at[at]
            reads.append(pltpu.make_async_copy(sources[index].at[at], box, read_sem.at[index, part]))
            writes.append(pltpu.make_async_copy(box, targets[index].at[at], write_sem.at[index, part]))
    for read in reads:
        read.start()
    for read, write in zip(reads, writes):
        read.wait()
        write.start()
    for write in writes:
        write.wait()


def hail(me_x, me_s):
    barrier = pltpu.get_barrier_semaphore()

    def one(step, carry):
        pl.semaphore_signal(
            barrier, inc=1, device_id=(me_x, lax.rem(me_s + step, N_S)), device_id_type=MESH
        )
        return carry

    lax.fori_loop(1, N_S, one, 0)
    for far in range(1, N_X):
        pl.semaphore_signal(
            barrier, inc=1, device_id=(lax.rem(me_x + far, N_X), me_s), device_id_type=MESH
        )


def admitted():
    pl.semaphore_wait(pltpu.get_barrier_semaphore(), N_S - 1 + N_X - 1)


def shampoo(
    table, grads, left, right, left_fac, right_fac, new_left, new_right, update,
    flat, mid, tiles, fwd_a, fwd_b, part_a, part_b, from_p, from_m,
    sum_own, sum_down, sum_up, outbox, blocks, roots, right_box, precond,
    sums, sum_box, factors, factor_box, raw, inbox_0, inbox_1, gathered, left_box, right_fac_box, places,
    flat_sem, right_sem, keep_sem, out_sem, send, recv, root_send, root_recv,
    fac_sem, piece_send, piece_recv, block_send, block_recv, sum_send, sum_recv, factor_send, factor_recv,
    back_send, back_recv, ring_send, ring_recv,
):
    me_x, me_s = lax.axis_index("replica"), lax.axis_index("shard")
    row, sub = me_s // SUBS, lax.rem(me_s, SUBS)
    up, down, over = lax.rem(me_x + 1, N_X), lax.rem(me_x + 3, N_X), lax.rem(me_x + 2, N_X)
    low, high = pl.ds(0, CUT), pl.ds(CUT, NBC - CUT)
    top, bottom = pl.ds(0, 16), pl.ds(16, 16)
    inbox = (inbox_0, inbox_1)
    OVER, DOWN, UP, OWN = range(4)

    def cross(src, dst, send_sem, recv_sem, x):
        return pltpu.make_async_remote_copy(
            src_ref=src, dst_ref=dst, send_sem=send_sem, recv_sem=recv_sem,
            device_id=(x, me_s), device_id_type=MESH,
        )

    def remote(src, dst, place, x):
        return cross(src, dst, send.at[place], recv.at[place], x)

    copies = [
        remote(tiles.at[OVER, low], fwd_a, 0, down),
        remote(tiles.at[OVER, high], fwd_b, 1, up),
        remote(tiles.at[DOWN, high], from_p.at[high], 2, down),
        remote(tiles.at[UP, low], from_m.at[low], 3, up),
        remote(part_a, from_p.at[low], 4, down),
        remote(part_b, from_m.at[high], 5, up),
        remote(sum_own.at[low, top], sum_down.at[low], 6, up),
        remote(sum_own.at[high, top], sum_up.at[high], 7, down),
        remote(sum_own.at[high, top], sum_down.at[high], 8, up),
        remote(sum_own.at[low, top], sum_up.at[low], 9, down),
    ]
    def root(slot, half):
        mine, there = left.at[slot], roots.at[slot, me_x]
        below, above = roots.at[slot, down, 0, half], roots.at[slot, up, 1, half]

        def one(place, src, dst, x):
            return cross(
                src, dst, root_send.at[slot, half, place], root_recv.at[slot, half, place], x
            )

        return [
            one(0, mine.at[0, half], there.at[0, half], up),
            one(1, mine.at[1, half], there.at[1, half], down),
            one(2, mine.at[1, half], there.at[1, half], up),
            one(3, mine.at[0, half], there.at[0, half], down),
            one(4, below, below, up),
            one(5, above, above, down),
        ]

    root_copies = [[root(slot, half) for slot in range(SLOTS)] for half in range(HALVES)]

    def start_root(half, slot):
        for copy in root_copies[half][slot][:4]:
            copy.start()

    def pass_root(half, slot):
        for place in range(2):
            root_copies[half][slot][place].wait_recv()
            root_copies[half][slot][place + 4].start()

    keep = pltpu.make_async_copy(left, roots.at[:, me_x], keep_sem)
    fetch_right = pltpu.make_async_copy(right, right_box, right_sem)
    fetch_left_fac = pltpu.make_async_copy(left_fac, left_box, fac_sem.at[0])
    fetch_right_fac = pltpu.make_async_copy(right_fac, right_fac_box, fac_sem.at[1])
    size = QROWS * COLS
    quarters = (over, down, up, me_x)
    loads = [
        pltpu.make_async_copy(
            grads.at[:, pl.ds(pl.multiple_of(quarters[part] * size, size), size)],
            flat.at[part % 2], flat_sem.at[part % 2],
        )
        for part in range(N_X)
    ]

    def unpack(part, first, last):
        def step(col, carry):
            for half in range(2):
                for line in range(16):
                    at = pl.multiple_of((half * 16 + line) * COLS + col * BLK, BLK)
                    mid[half, line * STEP : line * STEP + 8, :] = (
                        flat[part % 2, :, pl.ds(at, BLK)].astype(f32).reshape(8, 128)
                    )
            for half in range(2):
                for lane in range(8):
                    tiles[part, col, half * 16 : half * 16 + 16, lane * 128 : lane * 128 + 128] = (
                        mid[half, pl.ds(lane, 16, STEP), :].astype(bf16)
                    )
            return carry

        lax.fori_loop(first, last, step, 0)

    def sender(src, dst, send_sem, recv_sem, target):
        away = lambda: pltpu.make_async_remote_copy(
            src_ref=src, dst_ref=dst, send_sem=send_sem, recv_sem=recv_sem,
            device_id=(me_x, target), device_id_type=MESH,
        )
        home = lambda: pltpu.make_async_copy(src, dst, recv_sem)
        return target, away, home

    sums_of = (sum_own, sum_down, sum_up)
    from_of = (me_x, down, up)

    def piece(origin, place, count):
        holder = lax.rem(count + me_s // NBR, SUBS) * NBR + lax.rem(row + NBR - place, NBR)
        rows = pl.ds(0, QROWS) if origin == 0 else top
        src = outbox.at[origin, place, count, rows]
        dst = blocks.at[place, sub, from_of[origin], rows]
        return sender(
            src, dst, piece_send.at[origin, place, count], piece_recv.at[origin, place], holder
        )

    def spread(origin):
        for place in range(SLOTS):

            def step(count, carry):
                holder, away, home = piece(origin, place, count)
                block = table[place, holder]
                outbox[origin, place, count, : QROWS if origin == 0 else 16] = sums_of[origin][lax.rem(jnp.maximum(block, 0), NBC)]

                @pl.when(holder != me_s)
                def _():
                    away().start()

                @pl.when(holder == me_s)
                def _():
                    home().start()

                return carry

            lax.fori_loop(0, SUBS, step, 0)

    def gather_block(slot):
        def one(place, subs, x_from, rows, x):
            ref = blocks.at[slot, subs, x_from, rows]
            return cross(ref, ref, block_send.at[slot, place], block_recv.at[slot, place], x)

        every_sub, first, second = pl.ds(0, 8), pl.ds(0, 4), pl.ds(4, 4)
        return [
            one(0, every_sub, me_x, bottom, up),
            one(1, every_sub, me_x, bottom, down),
            one(2, first, down, top, up),
            one(3, second, up, top, down),
            one(4, first, down, bottom, up),
            one(5, second, up, bottom, down),
        ]

    block_copies = [gather_block(slot) for slot in range(SLOTS)]

    def arrive(origin, slot):
        pieces = blocks.at[slot, :, from_of[origin], pl.ds(0, QROWS) if origin == 0 else top]
        pltpu.make_async_copy(pieces, pieces, piece_recv.at[origin, slot]).wait()

    def locate(col, carry):
        wanted = row * NBC + col
        index = 0
        for cell in range(CELLS):
            place = cell % SLOTS
            holder = cell // SLOTS * NBR + lax.rem(row + NBR - place, NBR)
            index = jnp.where(table[place, holder] == wanted, cell, index)
        places[col] = index
        return carry

    def add_a(col, carry):
        part_a[col] = (fwd_a[col].astype(f32) + tiles[DOWN, col].astype(f32)).astype(bf16)
        return carry

    def add_b(col, carry):
        part_b[col] = (fwd_b[col].astype(f32) + tiles[UP, CUT + col].astype(f32)).astype(bf16)
        return carry

    def add_all(col, carry):
        sum_own[col] = (
            tiles[OWN, col].astype(f32) + (from_p[col].astype(f32) + from_m[col].astype(f32))
        ).astype(bf16)
        return carry

    loads[0].start()
    loads[1].start()
    fetch_right.start()
    fetch_left_fac.start()
    fetch_right_fac.start()
    hail(me_x, me_s)
    loads[0].wait()
    unpack(OVER, 0, CUT)
    admitted()
    keep.start()
    copies[0].start()
    unpack(OVER, CUT, NBC)
    copies[1].start()
    loads[2].start()
    loads[1].wait()
    unpack(DOWN, 0, NBC)
    copies[2].start()
    loads[3].start()
    loads[2].wait()
    unpack(UP, 0, NBC)
    copies[3].start()
    copies[0].wait_recv()
    lax.fori_loop(0, CUT, add_a, 0)
    copies[4].start()
    copies[1].wait_recv()
    lax.fori_loop(0, NBC - CUT, add_b, 0)
    copies[5].start()
    loads[3].wait()
    unpack(OWN, 0, NBC)
    copies[3].wait_recv()
    copies[4].wait_recv()
    lax.fori_loop(0, CUT, add_all, 0)
    copies[6].start()
    copies[9].start()
    copies[2].wait_recv()
    copies[5].wait_recv()
    lax.fori_loop(CUT, NBC, add_all, 0)
    copies[7].start()
    copies[8].start()
    spread(0)
    lax.fori_loop(0, NBC, locate, 0)
    copies[6].wait_recv()
    copies[8].wait_recv()
    start_root(0, 0)
    spread(1)
    copies[7].wait_recv()
    copies[9].wait_recv()
    start_root(0, 1)
    spread(2)
    for slot in range(SLOTS):
        arrive(0, slot)
        block_copies[slot][0].start()
        block_copies[slot][1].start()
    start_root(0, 2)
    pass_root(0, 0)
    pass_root(0, 1)
    for slot in range(SLOTS):
        for place in range(2):
            block_copies[slot][place].wait_recv()
            block_copies[slot][place + 4].start()
    pass_root(0, 2)
    for slot in range(SLOTS):
        if slot < SLOTS - 1:
            start_root(1, slot)
        arrive(1, slot)
        block_copies[slot][2].start()
        arrive(2, slot)
        block_copies[slot][3].start()
    pass_root(1, 0)
    pass_root(1, 1)

    def target_of(place, count):
        target_sub = lax.rem(3 * count + 3 * sub + 2 * row, SUBS)
        return target_sub, lax.rem(me_s + place, NBR) * SUBS + target_sub

    def back(place, half, count):
        target_sub, target = target_of(place, count)
        return sender(
            raw.at[half, place, target_sub], inbox[half].at[me_s // NBR * SLOTS + place],
            back_send.at[half, place, count], back_recv.at[half], target,
        )

    def tell(place, count):
        target_sub, target = target_of(place, count)
        return sender(
            factors.at[place], factor_box.at[me_s // NBR * SLOTS + place],
            factor_send.at[place, count], factor_recv, target,
        )

    def start_all(describe):
        def step(count, carry):
            target, away, home = describe(count)

            @pl.when(target != me_s)
            def _():
                away().start()

            @pl.when(target == me_s)
            def _():
                home().start()

            return carry

        lax.fori_loop(0, SUBS, step, 0)

    def finish_all(describe):
        def step(count, carry):
            target, away, home = describe(count)

            @pl.when(target != me_s)
            def _():
                away().wait_send()

            return carry

        lax.fori_loop(0, SUBS, step, 0)

    squares = [[] for slot in range(SLOTS)]

    def direct(half, slot):
        for copy in root_copies[half][slot][2:]:
            copy.wait_recv()
        result = jnp.dot(
            roots[slot, :, :, half].reshape(BLK // HALVES, BLK), precond[slot],
            preferred_element_type=f32,
        )
        raw[half, slot] = result.astype(bf16).reshape(SUBS, HROWS, 256)
        start_all(functools.partial(back, slot, half))
        squares[slot].append(jnp.sum(jnp.square(result)))

    shares = []

    def share(slot):
        sums[slot] = jnp.full((8, 128), squares[slot][0] + squares[slot][1], f32)
        for index, x in enumerate((up, down, over)):
            copy = cross(
                sums.at[slot], sum_box.at[slot, index],
                sum_send.at[slot, index], sum_recv.at[slot, index], x,
            )
            copy.start()
            shares.append(copy)

    def graft(slot):
        total = sums[slot] + (sum_box[slot, 0] + sum_box[slot, 1] + sum_box[slot, 2])
        factors[slot] = jnp.sqrt(powers[slot]) / jnp.sqrt(total / (BLK * BLK) + EPSILON)
        start_all(functools.partial(tell, slot))

    def ring(src, dst, group, place, x):
        return cross(src, dst, ring_send.at[group, place], ring_recv.at[group, place], x)

    def links(group):
        mine = gathered.at[me_x, group]
        below, above = gathered.at[down, group, low], gathered.at[up, group, high]
        return [
            ring(mine.at[low], mine.at[low], group, 0, up),
            ring(mine.at[high], mine.at[high], group, 1, down),
            ring(mine.at[high], mine.at[high], group, 2, up),
            ring(mine.at[low], mine.at[low], group, 3, down),
            ring(below, below, group, 4, up),
            ring(above, above, group, 5, down),
        ]

    every = [links(group) for group in range(GROUPS)]

    def statistics(slot):
        whole = blocks[slot].reshape(BLK, BLK)
        scale = jnp.where(table[slot, me_s] >= 0, 1.0 / BLK, 0.0).astype(f32)
        rows = blocks[slot, pl.ds(me_x * 2, 2)].reshape(256, BLK)
        left_box[slot] = left_box[slot] + contract_last(rows, whole) * scale
        start = pl.multiple_of(me_x * 256, 256)
        cols = blocks[slot, :, :, :, pl.ds(start, 256)].reshape(BLK, 256)
        right_fac_box[slot] = (
            right_fac_box[slot] + jnp.dot(cols.T, whole, preferred_element_type=f32) * scale
        )
        for copy in leave(slot):
            copy.start()

    def leave(slot):
        return [
            pltpu.make_async_copy(left_box.at[slot], new_left.at[slot], out_sem.at[slot, 0]),
            pltpu.make_async_copy(right_fac_box.at[slot], new_right.at[slot], out_sem.at[slot, 1]),
        ]

    def forward(group):
        every[group][0].wait_recv()
        every[group][4].start()
        every[group][1].wait_recv()
        every[group][5].start()

    def place_group(group):
        half, first = group // 2, group % 2 * QROWS

        def step(col, carry):
            gathered[me_x, group, col] = inbox[half][places[col], pl.ds(first, QROWS)]
            return carry

        lax.fori_loop(0, NBC, step, 0)

    def ring_group(group):
        for copy in every[group][:4]:
            copy.start()

    def flat_copy(group):
        at = pl.ds(group * size, size)
        return pltpu.make_async_copy(flat.at[group % 2], update.at[:, at], flat_sem.at[group % 2])

    def flatten(group):
        for copy in every[group][2:]:
            copy.wait_recv()
        if group >= 2:
            flat_copy(group - 2).wait()

        def step(col, carry):
            factor = factor_box[places[col]][0:1, :]
            for rows in range(2):
                for part in range(N_X):
                    for lane in range(2):
                        value = gathered[
                            part, group, col, rows * 16 : rows * 16 + 16, lane * 128 : lane * 128 + 128
                        ].astype(f32)
                        mid[rows, pl.ds(part * 2 + lane, 16, STEP), :] = value * factor
            for rows in range(2):
                for line in range(16):
                    at = pl.multiple_of((rows * 16 + line) * COLS + col * BLK, BLK)
                    flat[group % 2, :, pl.ds(at, BLK)] = (
                        mid[rows, line * STEP : line * STEP + 8, :].reshape(1, BLK).astype(bf16)
                    )
            return carry

        lax.fori_loop(0, NBC, step, 0)
        flat_copy(group).start()

    keep.wait()
    fetch_right.wait()
    fetch_left_fac.wait()
    fetch_right_fac.wait()
    powers = []
    for slot in range(SLOTS):
        for copy in block_copies[slot][2:]:
            copy.wait_recv()
        if slot == SLOTS - 1:
            start_root(1, slot)
        grad = blocks[slot].reshape(BLK, BLK)
        precond[slot] = contract_last(grad, right_box[slot]).astype(bf16)
        direct(0, slot)
        if slot == 0:
            statistics(0)
    for slot in range(SLOTS):
        grad = blocks[slot].reshape(BLK, BLK)
        powers.append(jnp.sum(jnp.square(grad.astype(f32))) / (BLK * BLK))
    pltpu.make_async_copy(inbox_0, inbox_0, back_recv.at[0]).wait()
    place_group(0)
    ring_group(0)
    place_group(1)
    pass_root(1, 2)
    direct(1, 0)
    direct(1, 1)
    statistics(1)
    forward(0)
    direct(1, 2)
    ring_group(1)
    for slot in range(SLOTS):
        share(slot)
    pltpu.make_async_copy(inbox_1, inbox_1, back_recv.at[1]).wait()
    place_group(2)
    ring_group(2)
    place_group(3)
    ring_group(3)
    for copy in shares:
        copy.wait_recv()
    for slot in range(SLOTS):
        graft(slot)
    forward(1)
    statistics(2)
    forward(2)
    pltpu.make_async_copy(factor_box, factor_box, factor_recv).wait()
    flatten(0)
    forward(3)
    flatten(1)
    flatten(2)
    flatten(3)
    flat_copy(2).wait()
    flat_copy(3).wait()
    for group in range(GROUPS):
        for copy in every[group]:
            copy.wait_send()
    for copy in shares + copies:
        copy.wait_send()
    for slot in range(SLOTS):
        for half in range(HALVES):
            for copy in root_copies[half][slot]:
                copy.wait_send()
            finish_all(functools.partial(back, slot, half))
        finish_all(functools.partial(tell, slot))
        for origin in range(3):
            finish_all(functools.partial(piece, origin, slot))
        for copy in block_copies[slot]:
            copy.wait_send()
        for copy in leave(slot):
            copy.wait()


def contract_last(a, b):
    return lax.dot_general(a, b, (((1,), (1,)), ((), ())), preferred_element_type=f32)


def on_device(grads, slot_table, left_factor, right_factor, left_root, right_root):
    smem = pl.BlockSpec(memory_space=pltpu.SMEM)
    hbm = pl.BlockSpec(memory_space=pl.ANY)
    dma = pltpu.SemaphoreType.DMA
    vmem = pltpu.VMEM

    new_left, new_right, update = pl.pallas_call(
        shampoo,
        in_specs=[smem] + [hbm] * 5,
        out_specs=[hbm] * 3,
        out_shape=[
            jax.ShapeDtypeStruct((SLOTS, 256, BLK), f32),
            jax.ShapeDtypeStruct((SLOTS, 256, BLK), f32),
            jax.ShapeDtypeStruct((1, 128 * COLS), bf16),
        ],
        scratch_shapes=[
            vmem((2, 1, QROWS * COLS), bf16),
            vmem((2, 16 * STEP, 128), f32),
            vmem((N_X, NBC, QROWS, BLK), bf16),
            vmem((CUT, QROWS, BLK), bf16),
            vmem((NBC - CUT, QROWS, BLK), bf16),
            vmem((CUT, QROWS, BLK), bf16),
            vmem((NBC - CUT, QROWS, BLK), bf16),
        ]
        + [vmem((NBC, QROWS, BLK), bf16)] * 3
        + [vmem((NBC, 16, BLK), bf16)] * 2
        + [
            vmem((3, SLOTS, SUBS, QROWS, BLK), bf16),
            vmem((SLOTS, SUBS, N_X, QROWS, BLK), bf16),
            vmem((SLOTS, N_X, 2, HALVES, HROWS, BLK), bf16),
            vmem((SLOTS, 256, BLK), bf16),
            vmem((SLOTS, BLK, 256), bf16),
            vmem((SLOTS, 8, 128), f32),
            vmem((SLOTS, 3, 8, 128), f32),
            vmem((SLOTS, 8, 128), f32),
            vmem((CELLS, 8, 128), f32),
            vmem((HALVES, SLOTS, SUBS, HROWS, 256), bf16),
            vmem((CELLS, HROWS, 256), bf16),
            vmem((CELLS, HROWS, 256), bf16),
            vmem((N_X, GROUPS, NBC, QROWS, 256), bf16),
            vmem((SLOTS, 256, BLK), f32),
            vmem((SLOTS, 256, BLK), f32),
            pltpu.SMEM((NBC,), jnp.int32),
            dma((2,)),
            dma,
            dma,
            dma((SLOTS, 2)),
            dma((10,)),
            dma((10,)),
            dma((SLOTS, HALVES, 6)),
            dma((SLOTS, HALVES, 6)),
            dma((2,)),
            dma((3, SLOTS, SUBS)),
            dma((3, SLOTS)),
            dma((SLOTS, 6)),
            dma((SLOTS, 6)),
            dma((SLOTS, 3)),
            dma((SLOTS, 3)),
            dma((SLOTS, SUBS)),
            dma,
            dma((HALVES, SLOTS, SUBS)),
            dma((HALVES,)),
            dma((GROUPS, 6)),
            dma((GROUPS, 6)),
        ],
        compiler_params=pltpu.CompilerParams(
            collective_id=0, has_side_effects=True, vmem_limit_bytes=VMEM_BYTES
        ),
        name="shampoo",
    )(slot_table.T, grads, left_root.reshape(SLOTS, 2, HALVES, HROWS, BLK), right_root[0], left_factor[0], right_factor[0])

    shapes = [
        jax.ShapeDtypeStruct((1, 128 * COLS), bf16),
        jax.ShapeDtypeStruct((SLOTS * 256, BLK), f32),
        jax.ShapeDtypeStruct((SLOTS * 256, BLK), f32),
    ]
    flat, new_left, new_right = pl.pallas_call(
        deliver,
        in_specs=[hbm] * 3,
        out_specs=[hbm] * 3,
        out_shape=shapes,
        scratch_shapes=[vmem(shape.shape, shape.dtype) for shape in shapes] + [dma((3, PARTS))] * 2,
        compiler_params=pltpu.CompilerParams(vmem_limit_bytes=VMEM_BYTES),
        name="deliver",
    )(update, new_left.reshape(SLOTS * 256, BLK), new_right.reshape(SLOTS * 256, BLK))
    rows = (1, SLOTS, 256, BLK)
    return new_left.reshape(rows), new_right.reshape(rows), flat


def solution(mesh):
    rows = P("shard", None, "replica", None)
    flat = P("replica", "shard")
    return jax.shard_map(
        on_device,
        mesh=mesh,
        in_specs=(flat, P(), rows, rows, rows, rows),
        out_specs=(rows, rows, flat),
        check_vma=False,
    )
```

```python
import functools

import jax
import jax.numpy as jnp
from jax import lax
from jax.experimental import pallas as pl
from jax.experimental.pallas import tpu as pltpu
from jax.sharding import PartitionSpec as P

ROWS = 4096
COLS = 15360
BLK = 1024
EPSILON = 1e-06

N_X = 4
N_S = 32
SLOTS = 3
NBR = 4
NBC = 15
SUBS = 8
CELLS = 24
QROWS = 32
CUT = 8
GROUPS = 4
MESH = pl.DeviceIdType.MESH
f32 = jnp.float32
bf16 = jnp.bfloat16
VMEM_BYTES = 58 * 1024 * 1024


STEP = 9
HALVES = 2
HROWS = 64
PARTS = 8


def deliver(*refs):
    sources, targets, boxes = refs[:3], refs[3:6], refs[6:9]
    read_sem, write_sem = refs[9:]
    reads, writes = [], []
    for index in range(3):
        for part in range(PARTS):
            if index == 0:
                count = 128 * COLS // PARTS
                at = (slice(None), pl.ds(part * count, count))
            else:
                count = SLOTS * 256 // PARTS
                at = (pl.ds(part * count, count),)
            box = boxes[index].at[at]
            reads.append(pltpu.make_async_copy(sources[index].at[at], box, read_sem.at[index, part]))
            writes.append(pltpu.make_async_copy(box, targets[index].at[at], write_sem.at[index, part]))
    for read in reads:
        read.start()
    for read, write in zip(reads, writes):
        read.wait()
        write.start()
    for write in writes:
        write.wait()


def hail(me_x, me_s):
    barrier = pltpu.get_barrier_semaphore()

    def one(step, carry):
        pl.semaphore_signal(
            barrier, inc=1, device_id=(me_x, lax.rem(me_s + step, N_S)), device_id_type=MESH
        )
        return carry

    lax.fori_loop(1, N_S, one, 0)
    for far in range(1, N_X):
        pl.semaphore_signal(
            barrier, inc=1, device_id=(lax.rem(me_x + far, N_X), me_s), device_id_type=MESH
        )


def admitted():
    pl.semaphore_wait(pltpu.get_barrier_semaphore(), N_S - 1 + N_X - 1)


def shampoo(
    table, grads, left, right, left_fac, right_fac, new_left, new_right, update,
    flat, mid, tiles, fwd_a, fwd_b, part_a, part_b, from_p, from_m,
    sum_own, sum_down, sum_up, outbox, blocks, roots, right_box, precond,
    sums, sum_box, factors, factor_box, raw, inbox_0, inbox_1, gathered, left_box, right_fac_box, places,
    flat_sem, right_sem, keep_sem, out_sem, send, recv, root_send, root_recv,
    fac_sem, piece_send, piece_recv, block_send, block_recv, sum_send, sum_recv, factor_send, factor_recv,
    back_send, back_recv, ring_send, ring_recv,
):
    me_x, me_s = lax.axis_index("replica"), lax.axis_index("shard")
    row, sub = me_s // SUBS, lax.rem(me_s, SUBS)
    up, down, over = lax.rem(me_x + 1, N_X), lax.rem(me_x + 3, N_X), lax.rem(me_x + 2, N_X)
    low, high = pl.ds(0, CUT), pl.ds(CUT, NBC - CUT)
    inbox = (inbox_0, inbox_1)
    OVER, DOWN, UP, OWN = range(4)

    def cross(src, dst, send_sem, recv_sem, x):
        return pltpu.make_async_remote_copy(
            src_ref=src, dst_ref=dst, send_sem=send_sem, recv_sem=recv_sem,
            device_id=(x, me_s), device_id_type=MESH,
        )

    def remote(src, dst, place, x):
        return cross(src, dst, send.at[place], recv.at[place], x)

    copies = [
        remote(tiles.at[OVER, low], fwd_a, 0, down),
        remote(tiles.at[OVER, high], fwd_b, 1, up),
        remote(tiles.at[DOWN, high], from_p.at[high], 2, down),
        remote(tiles.at[UP, low], from_m.at[low], 3, up),
        remote(part_a, from_p.at[low], 4, down),
        remote(part_b, from_m.at[high], 5, up),
        remote(sum_own.at[low], sum_down.at[low], 6, up),
        remote(sum_own.at[high], sum_up.at[high], 7, down),
        remote(sum_own.at[high], sum_down.at[high], 8, up),
        remote(sum_own.at[low], sum_up.at[low], 9, down),
    ]
    def root(slot, half):
        mine, there = left.at[slot], roots.at[slot, me_x]
        below, above = roots.at[slot, down, 0, half], roots.at[slot, up, 1, half]

        def one(place, src, dst, x):
            return cross(
                src, dst, root_send.at[slot, half, place], root_recv.at[slot, half, place], x
            )

        return [
            one(0, mine.at[0, half], there.at[0, half], up),
            one(1, mine.at[1, half], there.at[1, half], down),
            one(2, mine.at[1, half], there.at[1, half], up),
            one(3, mine.at[0, half], there.at[0, half], down),
            one(4, below, below, up),
            one(5, above, above, down),
        ]

    root_copies = [[root(slot, half) for slot in range(SLOTS)] for half in range(HALVES)]

    def start_root(half, slot):
        for copy in root_copies[half][slot][:4]:
            copy.start()

    def pass_root(half, slot):
        for place in range(2):
            root_copies[half][slot][place].wait_recv()
            root_copies[half][slot][place + 4].start()

    keep = pltpu.make_async_copy(left, roots.at[:, me_x], keep_sem)
    fetch_right = pltpu.make_async_copy(right, right_box, right_sem)
    fetch_left_fac = pltpu.make_async_copy(left_fac, left_box, fac_sem.at[0])
    fetch_right_fac = pltpu.make_async_copy(right_fac, right_fac_box, fac_sem.at[1])
    size = QROWS * COLS
    quarters = (over, down, up, me_x)
    loads = [
        pltpu.make_async_copy(
            grads.at[:, pl.ds(pl.multiple_of(quarters[part] * size, size), size)],
            flat.at[part % 2], flat_sem.at[part % 2],
        )
        for part in range(N_X)
    ]

    def unpack(part, first, last):
        def step(col, carry):
            for half in range(2):
                for line in range(16):
                    at = pl.multiple_of((half * 16 + line) * COLS + col * BLK, BLK)
                    mid[half, line * STEP : line * STEP + 8, :] = (
                        flat[part % 2, :, pl.ds(at, BLK)].astype(f32).reshape(8, 128)
                    )
            for half in range(2):
                for lane in range(8):
                    tiles[part, col, half * 16 : half * 16 + 16, lane * 128 : lane * 128 + 128] = (
                        mid[half, pl.ds(lane, 16, STEP), :].astype(bf16)
                    )
            return carry

        lax.fori_loop(first, last, step, 0)

    def sender(src, dst, send_sem, recv_sem, target):
        away = lambda: pltpu.make_async_remote_copy(
            src_ref=src, dst_ref=dst, send_sem=send_sem, recv_sem=recv_sem,
            device_id=(me_x, target), device_id_type=MESH,
        )
        home = lambda: pltpu.make_async_copy(src, dst, recv_sem)
        return target, away, home

    sums_of = (sum_own, sum_down, sum_up)
    from_of = (me_x, down, up)

    def piece(origin, place, count):
        holder = lax.rem(count + me_s // NBR, SUBS) * NBR + lax.rem(row + NBR - place, NBR)
        src, dst = outbox.at[origin, place, count], blocks.at[place, sub, from_of[origin]]
        return sender(
            src, dst, piece_send.at[origin, place, count], piece_recv.at[origin, place], holder
        )

    def spread(origin):
        for place in range(SLOTS):

            def step(count, carry):
                holder, away, home = piece(origin, place, count)
                block = table[place, holder]
                outbox[origin, place, count] = sums_of[origin][lax.rem(jnp.maximum(block, 0), NBC)]

                @pl.when(holder != me_s)
                def _():
                    away().start()

                @pl.when(holder == me_s)
                def _():
                    home().start()

                return carry

            lax.fori_loop(0, SUBS, step, 0)

    def gather_block(slot):
        def one(place, subs, x_from, x):
            ref = blocks.at[slot, subs, x_from]
            return cross(ref, ref, block_send.at[slot, place], block_recv.at[slot, place], x)

        return [one(0, pl.ds(0, 4), down, up), one(1, pl.ds(4, 4), up, down)]

    block_copies = [gather_block(slot) for slot in range(SLOTS)]

    def arrive(origin, slot):
        pieces = blocks.at[slot, :, from_of[origin]]
        pltpu.make_async_copy(pieces, pieces, piece_recv.at[origin, slot]).wait()

    def locate(col, carry):
        wanted = row * NBC + col
        index = 0
        for cell in range(CELLS):
            place = cell % SLOTS
            holder = cell // SLOTS * NBR + lax.rem(row + NBR - place, NBR)
            index = jnp.where(table[place, holder] == wanted, cell, index)
        places[col] = index
        return carry

    def add_a(col, carry):
        part_a[col] = (fwd_a[col].astype(f32) + tiles[DOWN, col].astype(f32)).astype(bf16)
        return carry

    def add_b(col, carry):
        part_b[col] = (fwd_b[col].astype(f32) + tiles[UP, CUT + col].astype(f32)).astype(bf16)
        return carry

    def add_all(col, carry):
        sum_own[col] = (
            tiles[OWN, col].astype(f32) + (from_p[col].astype(f32) + from_m[col].astype(f32))
        ).astype(bf16)
        return carry

    loads[0].start()
    loads[1].start()
    fetch_right.start()
    fetch_left_fac.start()
    fetch_right_fac.start()
    hail(me_x, me_s)
    loads[0].wait()
    unpack(OVER, 0, CUT)
    admitted()
    keep.start()
    copies[0].start()
    unpack(OVER, CUT, NBC)
    copies[1].start()
    loads[2].start()
    loads[1].wait()
    unpack(DOWN, 0, NBC)
    copies[2].start()
    loads[3].start()
    loads[2].wait()
    unpack(UP, 0, NBC)
    copies[3].start()
    copies[0].wait_recv()
    lax.fori_loop(0, CUT, add_a, 0)
    copies[4].start()
    copies[1].wait_recv()
    lax.fori_loop(0, NBC - CUT, add_b, 0)
    copies[5].start()
    loads[3].wait()
    unpack(OWN, 0, NBC)
    copies[3].wait_recv()
    copies[4].wait_recv()
    lax.fori_loop(0, CUT, add_all, 0)
    copies[6].start()
    copies[9].start()
    copies[2].wait_recv()
    copies[5].wait_recv()
    lax.fori_loop(CUT, NBC, add_all, 0)
    copies[7].start()
    copies[8].start()
    spread(0)
    lax.fori_loop(0, NBC, locate, 0)
    copies[6].wait_recv()
    start_root(0, 0)
    copies[8].wait_recv()
    spread(1)
    copies[7].wait_recv()
    copies[9].wait_recv()
    start_root(0, 1)
    spread(2)
    start_root(0, 2)
    for slot in range(SLOTS):
        pass_root(0, slot)
    for slot in range(SLOTS):
        if slot < SLOTS - 1:
            start_root(1, slot)
        arrive(1, slot)
        block_copies[slot][0].start()
        arrive(2, slot)
        block_copies[slot][1].start()
    pass_root(1, 0)
    pass_root(1, 1)

    def target_of(place, count):
        target_sub = lax.rem(3 * count + 3 * sub + 2 * row, SUBS)
        return target_sub, lax.rem(me_s + place, NBR) * SUBS + target_sub

    def back(place, half, count):
        target_sub, target = target_of(place, count)
        return sender(
            raw.at[half, place, target_sub], inbox[half].at[me_s // NBR * SLOTS + place],
            back_send.at[half, place, count], back_recv.at[half], target,
        )

    def tell(place, count):
        target_sub, target = target_of(place, count)
        return sender(
            factors.at[place], factor_box.at[me_s // NBR * SLOTS + place],
            factor_send.at[place, count], factor_recv, target,
        )

    def start_all(describe):
        def step(count, carry):
            target, away, home = describe(count)

            @pl.when(target != me_s)
            def _():
                away().start()

            @pl.when(target == me_s)
            def _():
                home().start()

            return carry

        lax.fori_loop(0, SUBS, step, 0)

    def finish_all(describe):
        def step(count, carry):
            target, away, home = describe(count)

            @pl.when(target != me_s)
            def _():
                away().wait_send()

            return carry

        lax.fori_loop(0, SUBS, step, 0)

    squares = [[] for slot in range(SLOTS)]

    def direct(half, slot):
        for copy in root_copies[half][slot][2:]:
            copy.wait_recv()
        result = jnp.dot(
            roots[slot, :, :, half].reshape(BLK // HALVES, BLK), precond[slot],
            preferred_element_type=f32,
        )
        raw[half, slot] = result.astype(bf16).reshape(SUBS, HROWS, 256)
        start_all(functools.partial(back, slot, half))
        squares[slot].append(jnp.sum(jnp.square(result)))

    shares = []

    def share(slot):
        sums[slot] = jnp.full((8, 128), squares[slot][0] + squares[slot][1], f32)
        for index, x in enumerate((up, down, over)):
            copy = cross(
                sums.at[slot], sum_box.at[slot, index],
                sum_send.at[slot, index], sum_recv.at[slot, index], x,
            )
            copy.start()
            shares.append(copy)

    def graft(slot):
        total = sums[slot] + (sum_box[slot, 0] + sum_box[slot, 1] + sum_box[slot, 2])
        factors[slot] = jnp.sqrt(powers[slot]) / jnp.sqrt(total / (BLK * BLK) + EPSILON)
        start_all(functools.partial(tell, slot))

    def ring(src, dst, group, place, x):
        return cross(src, dst, ring_send.at[group, place], ring_recv.at[group, place], x)

    def links(group):
        mine = gathered.at[me_x, group]
        below, above = gathered.at[down, group, low], gathered.at[up, group, high]
        return [
            ring(mine.at[low], mine.at[low], group, 0, up),
            ring(mine.at[high], mine.at[high], group, 1, down),
            ring(mine.at[high], mine.at[high], group, 2, up),
            ring(mine.at[low], mine.at[low], group, 3, down),
            ring(below, below, group, 4, up),
            ring(above, above, group, 5, down),
        ]

    every = [links(group) for group in range(GROUPS)]

    def statistics(slot):
        whole = blocks[slot].reshape(BLK, BLK)
        scale = jnp.where(table[slot, me_s] >= 0, 1.0 / BLK, 0.0).astype(f32)
        rows = blocks[slot, pl.ds(me_x * 2, 2)].reshape(256, BLK)
        left_box[slot] = left_box[slot] + contract_last(rows, whole) * scale
        start = pl.multiple_of(me_x * 256, 256)
        cols = blocks[slot, :, :, :, pl.ds(start, 256)].reshape(BLK, 256)
        right_fac_box[slot] = (
            right_fac_box[slot] + jnp.dot(cols.T, whole, preferred_element_type=f32) * scale
        )
        for copy in leave(slot):
            copy.start()

    def leave(slot):
        return [
            pltpu.make_async_copy(left_box.at[slot], new_left.at[slot], out_sem.at[slot, 0]),
            pltpu.make_async_copy(right_fac_box.at[slot], new_right.at[slot], out_sem.at[slot, 1]),
        ]

    def forward(group):
        every[group][0].wait_recv()
        every[group][4].start()
        every[group][1].wait_recv()
        every[group][5].start()

    def place_group(group):
        half, first = group // 2, group % 2 * QROWS

        def step(col, carry):
            gathered[me_x, group, col] = inbox[half][places[col], pl.ds(first, QROWS)]
            return carry

        lax.fori_loop(0, NBC, step, 0)

    def ring_group(group):
        for copy in every[group][:4]:
            copy.start()

    def flat_copy(group):
        at = pl.ds(group * size, size)
        return pltpu.make_async_copy(flat.at[group % 2], update.at[:, at], flat_sem.at[group % 2])

    def flatten(group):
        for copy in every[group][2:]:
            copy.wait_recv()
        if group >= 2:
            flat_copy(group - 2).wait()

        def step(col, carry):
            factor = factor_box[places[col]][0:1, :]
            for rows in range(2):
                for part in range(N_X):
                    for lane in range(2):
                        value = gathered[
                            part, group, col, rows * 16 : rows * 16 + 16, lane * 128 : lane * 128 + 128
                        ].astype(f32)
                        mid[rows, pl.ds(part * 2 + lane, 16, STEP), :] = value * factor
            for rows in range(2):
                for line in range(16):
                    at = pl.multiple_of((rows * 16 + line) * COLS + col * BLK, BLK)
                    flat[group % 2, :, pl.ds(at, BLK)] = (
                        mid[rows, line * STEP : line * STEP + 8, :].reshape(1, BLK).astype(bf16)
                    )
            return carry

        lax.fori_loop(0, NBC, step, 0)
        flat_copy(group).start()

    keep.wait()
    fetch_right.wait()
    fetch_left_fac.wait()
    fetch_right_fac.wait()
    powers = []
    for slot in range(SLOTS):
        arrive(0, slot)
        for copy in block_copies[slot]:
            copy.wait_recv()
        if slot == SLOTS - 1:
            start_root(1, slot)
        grad = blocks[slot].reshape(BLK, BLK)
        precond[slot] = contract_last(grad, right_box[slot]).astype(bf16)
        direct(0, slot)
        if slot == 0:
            statistics(0)
    for slot in range(SLOTS):
        grad = blocks[slot].reshape(BLK, BLK)
        powers.append(jnp.sum(jnp.square(grad.astype(f32))) / (BLK * BLK))
    pltpu.make_async_copy(inbox_0, inbox_0, back_recv.at[0]).wait()
    place_group(0)
    ring_group(0)
    place_group(1)
    pass_root(1, 2)
    direct(1, 0)
    direct(1, 1)
    statistics(1)
    forward(0)
    direct(1, 2)
    ring_group(1)
    for slot in range(SLOTS):
        share(slot)
    pltpu.make_async_copy(inbox_1, inbox_1, back_recv.at[1]).wait()
    place_group(2)
    ring_group(2)
    place_group(3)
    ring_group(3)
    for copy in shares:
        copy.wait_recv()
    for slot in range(SLOTS):
        graft(slot)
    forward(1)
    statistics(2)
    forward(2)
    pltpu.make_async_copy(factor_box, factor_box, factor_recv).wait()
    flatten(0)
    forward(3)
    flatten(1)
    flatten(2)
    flatten(3)
    flat_copy(2).wait()
    flat_copy(3).wait()
    for group in range(GROUPS):
        for copy in every[group]:
            copy.wait_send()
    for copy in shares + copies:
        copy.wait_send()
    for slot in range(SLOTS):
        for half in range(HALVES):
            for copy in root_copies[half][slot]:
                copy.wait_send()
            finish_all(functools.partial(back, slot, half))
        finish_all(functools.partial(tell, slot))
        for origin in range(3):
            finish_all(functools.partial(piece, origin, slot))
        for copy in block_copies[slot]:
            copy.wait_send()
        for copy in leave(slot):
            copy.wait()


def contract_last(a, b):
    return lax.dot_general(a, b, (((1,), (1,)), ((), ())), preferred_element_type=f32)


def on_device(grads, slot_table, left_factor, right_factor, left_root, right_root):
    smem = pl.BlockSpec(memory_space=pltpu.SMEM)
    hbm = pl.BlockSpec(memory_space=pl.ANY)
    dma = pltpu.SemaphoreType.DMA
    vmem = pltpu.VMEM

    new_left, new_right, update = pl.pallas_call(
        shampoo,
        in_specs=[smem] + [hbm] * 5,
        out_specs=[hbm] * 3,
        out_shape=[
            jax.ShapeDtypeStruct((SLOTS, 256, BLK), f32),
            jax.ShapeDtypeStruct((SLOTS, 256, BLK), f32),
            jax.ShapeDtypeStruct((1, 128 * COLS), bf16),
        ],
        scratch_shapes=[
            vmem((2, 1, QROWS * COLS), bf16),
            vmem((2, 16 * STEP, 128), f32),
            vmem((N_X, NBC, QROWS, BLK), bf16),
            vmem((CUT, QROWS, BLK), bf16),
            vmem((NBC - CUT, QROWS, BLK), bf16),
            vmem((CUT, QROWS, BLK), bf16),
            vmem((NBC - CUT, QROWS, BLK), bf16),
        ]
        + [vmem((NBC, QROWS, BLK), bf16)] * 5
        + [
            vmem((3, SLOTS, SUBS, QROWS, BLK), bf16),
            vmem((SLOTS, SUBS, N_X, QROWS, BLK), bf16),
            vmem((SLOTS, N_X, 2, HALVES, HROWS, BLK), bf16),
            vmem((SLOTS, 256, BLK), bf16),
            vmem((SLOTS, BLK, 256), bf16),
            vmem((SLOTS, 8, 128), f32),
            vmem((SLOTS, 3, 8, 128), f32),
            vmem((SLOTS, 8, 128), f32),
            vmem((CELLS, 8, 128), f32),
            vmem((HALVES, SLOTS, SUBS, HROWS, 256), bf16),
            vmem((CELLS, HROWS, 256), bf16),
            vmem((CELLS, HROWS, 256), bf16),
            vmem((N_X, GROUPS, NBC, QROWS, 256), bf16),
            vmem((SLOTS, 256, BLK), f32),
            vmem((SLOTS, 256, BLK), f32),
            pltpu.SMEM((NBC,), jnp.int32),
            dma((2,)),
            dma,
            dma,
            dma((SLOTS, 2)),
            dma((10,)),
            dma((10,)),
            dma((SLOTS, HALVES, 6)),
            dma((SLOTS, HALVES, 6)),
            dma((2,)),
            dma((3, SLOTS, SUBS)),
            dma((3, SLOTS)),
            dma((SLOTS, 2)),
            dma((SLOTS, 2)),
            dma((SLOTS, 3)),
            dma((SLOTS, 3)),
            dma((SLOTS, SUBS)),
            dma,
            dma((HALVES, SLOTS, SUBS)),
            dma((HALVES,)),
            dma((GROUPS, 6)),
            dma((GROUPS, 6)),
        ],
        compiler_params=pltpu.CompilerParams(
            collective_id=0, has_side_effects=True, vmem_limit_bytes=VMEM_BYTES
        ),
        name="shampoo",
    )(slot_table.T, grads, left_root.reshape(SLOTS, 2, HALVES, HROWS, BLK), right_root[0], left_factor[0], right_factor[0])

    shapes = [
        jax.ShapeDtypeStruct((1, 128 * COLS), bf16),
        jax.ShapeDtypeStruct((SLOTS * 256, BLK), f32),
        jax.ShapeDtypeStruct((SLOTS * 256, BLK), f32),
    ]
    flat, new_left, new_right = pl.pallas_call(
        deliver,
        in_specs=[hbm] * 3,
        out_specs=[hbm] * 3,
        out_shape=shapes,
        scratch_shapes=[vmem(shape.shape, shape.dtype) for shape in shapes] + [dma((3, PARTS))] * 2,
        compiler_params=pltpu.CompilerParams(vmem_limit_bytes=VMEM_BYTES),
        name="deliver",
    )(update, new_left.reshape(SLOTS * 256, BLK), new_right.reshape(SLOTS * 256, BLK))
    rows = (1, SLOTS, 256, BLK)
    return new_left.reshape(rows), new_right.reshape(rows), flat


def solution(mesh):
    rows = P("shard", None, "replica", None)
    flat = P("replica", "shard")
    return jax.shard_map(
        on_device,
        mesh=mesh,
        in_specs=(flat, P(), rows, rows, rows, rows),
        out_specs=(rows, rows, flat),
        check_vma=False,
    )
```
